256 devices in a mesh: tm: 8 (over x_hi, y), space: 32 (over x_lo, z, core).
Axes of the slice: x: 4 (x_hi: 2, x_lo: 2; x = x_hi * 2 + x_lo), y: 4, z: 8, core: 2. Of those that a mesh axis runs over, the one named last changes fastest.
Arguments:
- node_values: float32 [8, 3, 8, 512, 2048], P('tm', None, None, 'space'), may hold values from -1 to 1
Outputs:
- next_iterate: float32 [8, 3, 8, 512, 2048], P('tm', None, None, 'space')
The draws below stay inside these ranges and needn't reach their ends.
All inputs are finite; a program needn't handle non-finite values.
Results may differ from the reference program's by a relative error of at most 0.0001.
Values sent between devices are 32-bit elements; how exact they have to be, the bound alone decides.
A program may use at most 64 MiB of HBM per device.

```python
import jax
import jax.numpy as jnp

Z = 8
NY = 2048
NX = 512
SLICES = 8


def block_scale(own_key, extent, shards, smallest, top_value):
    gain = 1.0
    for axis_at, shards_of in shards:
        draws = jax.random.uniform(jax.random.fold_in(jax.random.fold_in(own_key, 6), axis_at), (shards_of,), jnp.float32, smallest / len(shards), top_value / len(shards))
        gain = gain * jnp.repeat(jnp.exp(draws), extent[axis_at] // shards_of).reshape((-1,) + (1,) * (len(extent) - 1 - axis_at))
    return gain


def setup_inputs(seed: int = 0) -> dict:
    key_of = jax.random.split(jax.random.key(seed), 2)
    return {
        "node_values": jnp.clip(jax.random.uniform(key_of[0], (SLICES, 3, Z, NX, NY), jnp.float32, -1.0, 1.0) * block_scale(key_of[0], (SLICES, 3, Z, NX, NY), ((0, 8), (3, 32)), -0.4, 0.0), -1.0, 1.0),
    }


DIFFUSION = 1.0
GROWTH = 2.0
STEP = 0.25
WEIGHTS = ((5.0 / 24.0, 1.0 / 3.0, -1.0 / 24.0), (-1.0 / 24.0, 1.0 / 3.0, 5.0 / 24.0))


def forcing(region, factor):
    beside = jnp.roll(region, -1, 1) + jnp.roll(region, 1, 1)
    beside = beside + jnp.roll(region, 1, 0) + jnp.roll(region, -1, 0)
    beside = beside + jnp.roll(region, 1, 2) + jnp.roll(region, -1, 2)
    return DIFFUSION * factor * (beside - 6.0 * region) + GROWTH * (region - region * region * region)


def quadrature(terms, which_row):
    weights_row = WEIGHTS[which_row]
    return weights_row[0] * terms[0] + weights_row[1] * terms[1] + weights_row[2] * terms[2]


def restricted(region):
    depth_cells, across, length = region.shape
    blocks = region.reshape((depth_cells // 2, 2, across // 2, 2, length // 2, 2))
    return blocks.mean(axis=(1, 3, 5))


def refine_axis(region, which_axis):
    lower_half = 0.75 * region + 0.25 * jnp.roll(region, 1, which_axis)
    upper_half = 0.75 * region + 0.25 * jnp.roll(region, -1, which_axis)
    joined = jnp.stack([lower_half, upper_half], which_axis + 1)
    new_shape = list(region.shape)
    new_shape[which_axis] = 2 * new_shape[which_axis]
    return joined.reshape(new_shape)


def refine(region):
    return refine_axis(refine_axis(refine_axis(region, 1), 0), 2)


def reference(node_values):
    results = []
    coarse_finish = None
    previous_end = None
    for slice_index in range(SLICES):
        start_nodes = node_values[slice_index]
        node_rates = [forcing(start_nodes[position], 1.0) for position in range(3)]
        sweep_one = start_nodes[0] + STEP * quadrature(node_rates, 0)
        later_one = forcing(sweep_one, 1.0)
        sweep_two = sweep_one + 0.5 * STEP * (later_one - node_rates[1]) + STEP * quadrature(node_rates, 1)
        later_two = forcing(sweep_two, 1.0)
        coarse_nodes = [restricted(start_nodes[0]), restricted(sweep_one), restricted(sweep_two)]
        coarse_later = [restricted(node_rates[0]), restricted(later_one), restricted(later_two)]
        coarse_rates = [forcing(coarse_nodes[0], 0.25), forcing(coarse_nodes[1], 0.25)]
        beginning = coarse_nodes[0] if slice_index == 0 else coarse_finish
        middle = beginning + 0.5 * STEP * (forcing(beginning, 0.25) - coarse_rates[0]) + STEP * quadrature(coarse_later, 0)
        coarse_finish = middle + 0.5 * STEP * (forcing(middle, 0.25) - coarse_rates[1]) + STEP * quadrature(coarse_later, 1)
        corrected_one = sweep_one + refine(middle - coarse_nodes[1])
        corrected_two = sweep_two + refine(coarse_finish - coarse_nodes[2])
        head_value = start_nodes[0] if slice_index == 0 else previous_end
        results.append(jnp.stack([head_value, corrected_one, corrected_two]))
        previous_end = corrected_two
    return jnp.stack(results)
```

```python
import functools

import jax
import jax.numpy as jnp
from jax import lax
from jax.experimental import pallas as pl
from jax.experimental.pallas import tpu as pltpu
from jax.sharding import PartitionSpec as P

STEP = 0.25
WEIGHTS = ((5.0 / 24.0, 1.0 / 3.0, -1.0 / 24.0), (-1.0 / 24.0, 1.0 / 3.0, 5.0 / 24.0))
MESH = pl.DeviceIdType.MESH
F32 = jnp.float32


def fine_rate(above, center, below):
    lanes = center.shape[-1]
    beside = above + below + pltpu.roll(center, 1, 0) + pltpu.roll(center, 7, 0)
    beside = beside + pltpu.roll(center, 1, 1) + pltpu.roll(center, lanes - 1, 1)
    return beside - center * (4.0 + 2.0 * (center * center))


def iotas():
    sub = lax.broadcasted_iota(jnp.int32, (8, 128), 0)
    lane = lax.broadcasted_iota(jnp.int32, (8, 128), 1)
    return sub, lane


def take(value, index, axis):
    return jnp.take_along_axis(value, index, axis=axis, mode="promise_in_bounds")


def split_tiles(value):
    return [value[:, 128 * t : 128 * (t + 1)] for t in range(value.shape[1] // 128)]


def lane_neighbours(tiles, lane):
    count = len(tiles)
    right_rolled = [pltpu.roll(t, 1, 1) for t in tiles]
    left_rolled = [pltpu.roll(t, 127, 1) for t in tiles]
    before = [pltpu.roll(right_rolled[-1], 4, 0)] + right_rolled[:-1]
    after = left_rolled[1:] + [pltpu.roll(left_rolled[0], 4, 0)]
    left = [jnp.where(lane == 0, before[i], right_rolled[i]) for i in range(count)]
    right = [jnp.where(lane == 127, after[i], left_rolled[i]) for i in range(count)]
    return left, right


def coarse_rate(above, center, below):
    sub, lane = iotas()
    up_index = (sub // 4) * 4 + (sub + 1) % 4
    down_index = (sub // 4) * 4 + (sub + 3) % 4
    a, c, b = split_tiles(above), split_tiles(center), split_tiles(below)
    left, right = lane_neighbours(c, lane)
    out = []
    for i in range(len(c)):
        beside = a[i] + b[i] + take(c[i], up_index, 0) + take(c[i], down_index, 0) + left[i] + right[i]
        out.append(0.25 * beside + c[i] * (0.5 - 2.0 * (c[i] * c[i])))
    return jnp.concatenate(out, axis=1)


def restrict_row(pair_sum, staging):
    sub, lane = iotas()
    tiles = split_tiles(pair_sum)
    half = len(tiles) // 2
    for t in range(half):
        staging[pl.ds(16 * t, 8), :] = tiles[t]
        staging[pl.ds(16 * t + 8, 8), :] = tiles[t + half]
    packed = [
        staging[pl.ds(16 * t, 8, stride=2), :] + staging[pl.ds(16 * t + 1, 8, stride=2), :]
        for t in range(half)
    ]
    index = jnp.where(lane < 64, 2 * lane, 2 * lane - 127)
    out = []
    for t in range(half // 2):
        p, q = packed[2 * t], packed[2 * t + 1]
        mixed = jnp.where(lane % 2 == 0, p + pltpu.roll(p, 127, 1), q + pltpu.roll(q, 1, 1))
        out.append(0.125 * take(mixed, index, 1))
    return jnp.concatenate(out, axis=1)


def main_kernel(
    u_hbm, vv_hbm, d_hbm,
    ub, v1, tt, f0, v2, g1, c0, c1, c2, c2p, a0, a1, w0, w1, w2, dd, staging,
    load_sem, u_send, u_recv, h_send, h_recv, w_send, w_recv, v_send, v_recv, p_send, p_recv, out_sem,
):
    tm, sp = lax.axis_index("tm"), lax.axis_index("space")
    n_tm, n_sp = lax.axis_size("tm"), lax.axis_size("space")
    left, right = lax.rem(sp + n_sp - 1, n_sp), lax.rem(sp + 1, n_sp)
    not_first, not_last = tm > 0, tm < n_tm - 1
    half_step = 0.5 * STEP

    def load(m, r):
        return pltpu.make_async_copy(u_hbm.at[0, m, :, r, :], ub.at[m, r + 3], load_sem.at[m, r])

    def remote(src, dst, send, recv, t, s):
        return pltpu.make_async_remote_copy(
            src_ref=src, dst_ref=dst, send_sem=send, recv_sem=recv, device_id=(t, s), device_id_type=MESH
        )

    def edge_row(k):
        return jnp.where(k < 3, k, k + 10)

    def each(count, body):
        def step(k, carry):
            body(k)
            return carry

        lax.fori_loop(0, count, step, 0)

    def load_edges(k):
        for m in range(3):
            load(m, edge_row(k)).start()

    def load_inner(k):
        for m in range(3):
            load(m, k + 3).start()

    each(6, load_edges)
    each(10, load_inner)

    barrier = pltpu.get_barrier_semaphore()
    for s in (left, right):
        pl.semaphore_signal(barrier, inc=1, device_id=(tm, s), device_id_type=MESH)

    @pl.when(not_first)
    def _():
        for s in (left, sp, right):
            pl.semaphore_signal(barrier, inc=1, device_id=(tm - 1, s), device_id_type=MESH)

    @pl.when(not_last)
    def _():
        pl.semaphore_wait(barrier, 5)

    @pl.when(jnp.logical_not(not_last))
    def _():
        pl.semaphore_wait(barrier, 2)

    def wait_edges(k):
        for m in range(3):
            load(m, edge_row(k)).wait()

    def wait_inner(k):
        for m in range(3):
            load(m, k + 3).wait()

    each(6, wait_edges)
    u_up = remote(ub.at[:, pl.ds(16, 3)], ub.at[:, pl.ds(0, 3)], u_send.at[0], u_recv.at[0], tm, right)
    u_down = remote(ub.at[:, pl.ds(3, 3)], ub.at[:, pl.ds(19, 3)], u_send.at[1], u_recv.at[1], tm, left)
    u_up.start()
    u_down.start()
    each(10, wait_inner)

    def first_sweep(r):
        rates = [fine_rate(ub[m, r + 2], ub[m, r + 3], ub[m, r + 4]) for m in range(3)]
        (a, b, c), (d, e, f) = WEIGHTS
        v1[r + 2] = ub[0, r + 3] + (STEP * a) * rates[0] + (STEP * b) * rates[1] + (STEP * c) * rates[2]
        return rates, (STEP * d) * rates[0] + (STEP * e - half_step) * rates[1] + (STEP * f) * rates[2]

    def first_sweep_inner(r):
        rates, rest = first_sweep(r)
        f0[r] = rates[0]
        tt[r + 1] = rest

    def second_sweep(r):
        rate = fine_rate(v1[r + 1], v1[r + 2], v1[r + 3])
        v2[r + 1] = v1[r + 2] + half_step * rate + tt[r + 1]
        return rate

    def second_sweep_inner(r):
        g1[r] = second_sweep(r)

    def restrict_start(i):
        c0[i + 1] = restrict_row(ub[0, 2 * i + 3] + ub[0, 2 * i + 4], staging.at[0])
        c1[i + 1] = restrict_row(v1[2 * i + 2] + v1[2 * i + 3], staging.at[1])

    def third_sweep(i):
        r = 2 * i
        (a, b, c), (d, e, f) = WEIGHTS
        sums = [0.0, 0.0]
        for k in range(2):
            g2 = fine_rate(v2[r + k], v2[r + k + 1], v2[r + k + 2])
            sums[0] = sums[0] + (STEP * a) * f0[r + k] + (STEP * b) * g1[r + k] + (STEP * c) * g2
            sums[1] = sums[1] + (STEP * d) * f0[r + k] + (STEP * e) * g1[r + k] + (STEP * f) * g2
        a0[i + 2] = restrict_row(sums[0], staging.at[2])
        a1[i + 1] = restrict_row(sums[1], staging.at[3])
        c2[i + 1] = restrict_row(v2[r + 1] + v2[r + 2], staging.at[4])

    each(14, lambda k: first_sweep_inner(k + 1))
    each(12, lambda k: second_sweep_inner(k + 2))

    def inner_pairs(k):
        restrict_start(k + 2)
        third_sweep(k + 2)

    each(4, inner_pairs)

    u_up.wait_recv()
    u_down.wait_recv()

    def first_rim(k):
        first_sweep_inner(15 * k)

    def first_far(k):
        r = 17 * k - 1
        tt[r + 1] = first_sweep(r)[1]

    def first_farthest(k):
        first_sweep(19 * k - 2)

    each(2, first_rim)
    each(2, first_far)
    each(2, first_farthest)
    each(4, lambda k: second_sweep_inner(jnp.where(k < 2, k, k + 12)))
    each(2, lambda k: second_sweep(17 * k - 1))
    each(4, lambda k: third_sweep(jnp.where(k < 2, k, k + 4)))
    each(6, lambda k: restrict_start(jnp.where(k < 3, k - 1, k + 3)))

    def edge_sends(rows, t):
        up = remote(rows.at[pl.ds(5, 3)], w0.at[pl.ds(0, 3)], w_send.at[0], w_recv.at[0], t, right)
        down = remote(rows.at[pl.ds(0, 3)], w0.at[pl.ds(11, 3)], w_send.at[1], w_recv.at[1], t, left)
        return up, down

    own_c0, own_w2 = c0.at[pl.ds(1, 8)], w2.at[pl.ds(1, 8)]
    start_up, start_down = edge_sends(own_c0, tm)
    next_up, next_down = edge_sends(own_w2, tm + 1)
    next_own = remote(own_w2, w0.at[pl.ds(3, 8)], w_send.at[2], w_recv.at[2], tm + 1, sp)
    is_first = jnp.logical_not(not_first)

    @pl.when(is_first)
    def _():
        start_up.start()
        start_down.start()

    def halo_sends(index, field, rows, own):
        up = remote(field.at[pl.ds(own + 8 - rows, rows)], field.at[pl.ds(own - rows, rows)], h_send.at[index], h_recv.at[index], tm, right)
        down = remote(field.at[pl.ds(own, rows)], field.at[pl.ds(own + 8, rows)], h_send.at[index + 1], h_recv.at[index + 1], tm, left)
        return [up, down]

    c2_halos = halo_sends(0, c2, 1, 1)
    a_halos = halo_sends(2, a0, 2, 2) + halo_sends(4, a1, 1, 1)

    def add_start(k):
        a0[k + 2] = a0[k + 2] - half_step * coarse_rate(c0[k], c0[k + 1], c0[k + 2])
        a1[k + 1] = a1[k + 1] - half_step * coarse_rate(c1[k], c1[k + 1], c1[k + 2])

    each(8, add_start)
    for copy in a_halos + c2_halos:
        copy.start()

    v1_out = pltpu.make_async_copy(v1.at[pl.ds(2, 16)], vv_hbm.at[1], out_sem.at[0])
    v2_out = pltpu.make_async_copy(v2.at[pl.ds(1, 16)], vv_hbm.at[2], out_sem.at[1])
    u0_out = pltpu.make_async_copy(ub.at[0, pl.ds(3, 16)], vv_hbm.at[0], out_sem.at[2])
    v_next = remote(v2.at[pl.ds(1, 16)], vv_hbm.at[0], v_send.at[0], v_recv.at[0], tm + 1, sp)
    v1_out.start()
    v2_out.start()

    early = tm >= n_tm // 2

    @pl.when(is_first)
    def _():
        u0_out.start()
        w0[pl.ds(3, 8)] = c0[pl.ds(1, 8)]

    @pl.when(not_last & early)
    def _():
        v_next.start()

    for copy in a_halos + c2_halos:
        copy.wait_recv()
    p_next = remote(c2, c2p, p_send.at[0], p_recv.at[0], tm + 1, sp)

    @pl.when(not_last)
    def _():
        p_next.start()

    @pl.when(not_first)
    def _():
        next_own.wait_recv()

    start_up.wait_recv()
    start_down.wait_recv()

    def middle(k):
        w1[k] = w0[k + 1] + half_step * coarse_rate(w0[k], w0[k + 1], w0[k + 2]) + a0[k]

    def finish(k):
        w2[k] = w1[k + 1] + half_step * coarse_rate(w1[k], w1[k + 1], w1[k + 2]) + a1[k]

    each(12, middle)
    each(10, finish)

    @pl.when(not_last)
    def _():
        next_own.start()
        next_up.start()
        next_down.start()

    @pl.when(not_last & jnp.logical_not(early))
    def _():
        v_next.start()

    dd[1] = w1[pl.ds(1, 10)] - c1[...]
    dd[2] = w2[...] - c2[...]

    @pl.when(not_first)
    def _():
        p_next.wait_recv()
        dd[0] = w0[pl.ds(2, 10)] - c2p[...]

    @pl.when(is_first)
    def _():
        dd[0] = jnp.zeros(dd.shape[1:], F32)

    d_out = pltpu.make_async_copy(dd, d_hbm, out_sem.at[3])
    d_out.start()

    u_up.wait_send()
    u_down.wait_send()
    for copy in a_halos + c2_halos:
        copy.wait_send()

    @pl.when(is_first)
    def _():
        start_up.wait_send()
        start_down.wait_send()
        u0_out.wait()

    @pl.when(not_last)
    def _():
        next_own.wait_send()
        next_up.wait_send()
        next_down.wait_send()
        p_next.wait_send()
        v_next.wait_send()

    @pl.when(not_first)
    def _():
        v_next.wait_recv()

    v1_out.wait()
    v2_out.wait()
    d_out.wait()


def correct_kernel(vv_hbm, d_ref, o_hbm, vb, g75, g25, in_sem, out_sem):
    sub, lane = iotas()
    lanes = vb.shape[-1]
    half = lanes // 256

    def load(m):
        return pltpu.make_async_copy(vv_hbm.at[m], vb.at[m], in_sem.at[m])

    def store(m, r):
        return pltpu.make_async_copy(vb.at[m, r], o_hbm.at[0, m, :, r, :], out_sem.at[m, r])

    for m in range(3):
        load(m).start()

    def spread(m, k):
        tiles = split_tiles(d_ref[m, k])
        before, after = lane_neighbours(tiles, lane)
        for t in range(half):
            i, index = t // 2, (t % 2) * 64 + lane // 2
            low = 0.75 * tiles[i] + 0.25 * before[i]
            high = 0.75 * tiles[i] + 0.25 * after[i]
            fine = jnp.where(lane % 2 == 0, take(low, index, 1), take(high, index, 1))
            near_part, far_part = 0.75 * fine, 0.25 * fine
            for h in range(2):
                near = 4 * h + sub // 2
                far = 4 * h + (sub // 2 + 3 + 2 * (sub % 2)) % 4
                value = take(near_part, near, 0) + take(far_part, far, 0)
                columns = pl.ds(128 * (t + half * h), 128)
                g75[k, :, columns] = 0.75 * value
                g25[k, :, columns] = 0.25 * value

    def node(m, carry):
        def spread_step(k, inner):
            spread(m, k)
            return inner

        lax.fori_loop(0, 10, spread_step, 0)
        load(m).wait()

        def rows(k, inner):
            vb[m, 2 * k] = vb[m, 2 * k] + g75[k + 1] + g25[k]
            vb[m, 2 * k + 1] = vb[m, 2 * k + 1] + g75[k + 1] + g25[k + 2]
            store(m, 2 * k).start()
            store(m, 2 * k + 1).start()
            return inner

        lax.fori_loop(0, 8, rows, 0)
        return carry

    lax.fori_loop(0, 3, node, 0)

    def drain(k, carry):
        for m in range(3):
            store(m, k).wait()
        return carry

    lax.fori_loop(0, 16, drain, 0)


def on_device(node_values):
    _, _, depth, rows, lanes = node_values.shape
    half = lanes // 4
    fine = lambda n: pltpu.VMEM((n, 8, lanes), F32)
    coarse = lambda n: pltpu.VMEM((n, 8, half), F32)
    dma = lambda *n: pltpu.SemaphoreType.DMA(n)
    anywhere = pl.BlockSpec(memory_space=pl.ANY)
    vv, dd = pl.pallas_call(
        main_kernel,
        name="sweeps",
        out_shape=(
            jax.ShapeDtypeStruct((3, rows, depth, lanes), F32),
            jax.ShapeDtypeStruct((3, 10, 8, half), F32),
        ),
        in_specs=[anywhere],
        out_specs=(anywhere, anywhere),
        scratch_shapes=[
            pltpu.VMEM((3, 22, 8, lanes), F32), fine(20), fine(18), fine(16), fine(18), fine(16),
            coarse(10), coarse(10), coarse(10), coarse(10), coarse(12), coarse(10), coarse(14), coarse(12), coarse(10),
            pltpu.VMEM((3, 10, 8, half), F32), pltpu.VMEM((5, lanes // 16, 128), F32),
            dma(3, 16), dma(2), dma(2), dma(6), dma(6), dma(3), dma(3), dma(1), dma(1), dma(1), dma(1), dma(4),
        ],
        compiler_params=pltpu.CompilerParams(
            collective_id=0, has_side_effects=True, vmem_limit_bytes=48 * 1024 * 1024
        ),
    )(node_values)
    return pl.pallas_call(
        correct_kernel,
        name="correct",
        out_shape=jax.ShapeDtypeStruct(node_values.shape, F32),
        in_specs=[anywhere, pl.BlockSpec(memory_space=pltpu.VMEM)],
        out_specs=anywhere,
        scratch_shapes=[
            pltpu.VMEM((3, rows, 8, lanes), F32), pltpu.VMEM((10, 8, lanes), F32), pltpu.VMEM((10, 8, lanes), F32),
            dma(3), dma(3, 16),
        ],
        compiler_params=pltpu.CompilerParams(vmem_limit_bytes=48 * 1024 * 1024),
    )(vv, dd)


def solution(mesh):
    return jax.shard_map(
        on_device,
        mesh=mesh,
        in_specs=(P("tm", None, None, "space", None),),
        out_specs=P("tm", None, None, "space", None),
        check_vma=False,
    )
```

```python
import functools

import jax
import jax.numpy as jnp
from jax import lax
from jax.experimental import pallas as pl
from jax.experimental.pallas import tpu as pltpu
from jax.sharding import PartitionSpec as P

STEP = 0.25
WEIGHTS = ((5.0 / 24.0, 1.0 / 3.0, -1.0 / 24.0), (-1.0 / 24.0, 1.0 / 3.0, 5.0 / 24.0))
MESH = pl.DeviceIdType.MESH
F32 = jnp.float32


def neighbour_sum(above, center, below):
    lanes = center.shape[-1]
    beside = above + below + pltpu.roll(center, 1, 0) + pltpu.roll(center, 7, 0)
    return beside + pltpu.roll(center, 1, 1) + pltpu.roll(center, lanes - 1, 1)


def cube(value):
    return value * value * value


def combine(weights, terms):
    total = weights[0] * terms[0]
    for weight, term in zip(weights[1:], terms[1:]):
        total = total + weight * term
    return total


def each(count, body, unroll=1):
    def step(k, carry):
        body(k)
        return carry

    lax.fori_loop(0, count, step, 0, unroll=unroll)


def iotas():
    sub = lax.broadcasted_iota(jnp.int32, (8, 128), 0)
    lane = lax.broadcasted_iota(jnp.int32, (8, 128), 1)
    return sub, lane


def take(value, index, axis):
    return jnp.take_along_axis(value, index, axis=axis, mode="promise_in_bounds")


def split_tiles(value):
    return [value[:, 128 * t : 128 * (t + 1)] for t in range(value.shape[1] // 128)]


def lane_neighbours(tiles, lane):
    count = len(tiles)
    right_rolled = [pltpu.roll(t, 1, 1) for t in tiles]
    left_rolled = [pltpu.roll(t, 127, 1) for t in tiles]
    before = [pltpu.roll(right_rolled[-1], 4, 0)] + right_rolled[:-1]
    after = left_rolled[1:] + [pltpu.roll(left_rolled[0], 4, 0)]
    left = [jnp.where(lane == 0, before[i], right_rolled[i]) for i in range(count)]
    right = [jnp.where(lane == 127, after[i], left_rolled[i]) for i in range(count)]
    return left, right


def coarse_rate(above, center, below):
    sub, lane = iotas()
    up_index = (sub // 4) * 4 + (sub + 1) % 4
    down_index = (sub // 4) * 4 + (sub + 3) % 4
    a, c, b = split_tiles(above), split_tiles(center), split_tiles(below)
    left, right = lane_neighbours(c, lane)
    out = []
    for i in range(len(c)):
        beside = a[i] + b[i] + take(c[i], up_index, 0) + take(c[i], down_index, 0) + left[i] + right[i]
        out.append(0.25 * beside + c[i] * (0.5 - 2.0 * (c[i] * c[i])))
    return jnp.concatenate(out, axis=1)


def packed_halves(row, staging):
    tiles = split_tiles(row)
    half = len(tiles) // 2
    for t in range(half):
        staging[pl.ds(16 * t, 8), :] = tiles[t]
        staging[pl.ds(16 * t + 8, 8), :] = tiles[t + half]
    even = [staging[pl.ds(16 * t, 8, stride=2), :] for t in range(half)]
    odd = [staging[pl.ds(16 * t + 1, 8, stride=2), :] for t in range(half)]
    return even, odd


def decimate_index(lane):
    return jnp.where(lane < 64, 2 * lane, 2 * lane - 127)


def lane_pairs(packed, lane):
    out = []
    for t in range(len(packed) // 2):
        p, q = packed[2 * t], packed[2 * t + 1]
        mixed = jnp.where(lane % 2 == 0, p + pltpu.roll(p, 127, 1), q + pltpu.roll(q, 1, 1))
        out.append(take(mixed, decimate_index(lane), 1))
    return out


def lane_even_odd(packed, lane):
    even, odd = [], []
    for t in range(len(packed) // 2):
        p, q = packed[2 * t], packed[2 * t + 1]
        even.append(take(jnp.where(lane % 2 == 0, p, pltpu.roll(q, 1, 1)), decimate_index(lane), 1))
        odd.append(take(jnp.where(lane % 2 == 0, pltpu.roll(p, 127, 1), q), decimate_index(lane), 1))
    return even, odd


def restrict_row(pair_sum, staging):
    _, lane = iotas()
    even, odd = packed_halves(pair_sum, staging)
    sums = lane_pairs([a + b for a, b in zip(even, odd)], lane)
    return jnp.concatenate([0.125 * v for v in sums], axis=1)


def coarse_terms(fields, staging):
    sub, lane = iotas()
    up_index = (sub // 4) * 4 + (sub + 1) % 4
    down_index = (sub // 4) * 4 + (sub + 3) % 4
    nodes, inner, evens, odds = [], [], [], []
    for n, (before, a, b, after) in enumerate(fields):
        total = a + b
        rest = (before + after) - total - 2.0 * (cube(a) + cube(b))
        even, odd = packed_halves(total, staging.at[2 * n])
        rest_even, rest_odd = packed_halves(rest, staging.at[2 * n + 1])
        count = len(even)
        inner.append(
            [
                rest_even[t] + rest_odd[t] + take(odd[t], down_index, 0) + take(even[t], up_index, 0)
                for t in range(count)
            ]
        )
        lane_even, lane_odd = lane_even_odd([even[t] + odd[t] for t in range(count)], lane)
        evens.append(lane_even)
        odds.append(lane_odd)
        nodes.append(jnp.concatenate([0.125 * (p + q) for p, q in zip(lane_even, lane_odd)], axis=1))
    sums = []
    for weights in WEIGHTS:
        weights = [0.125 * STEP * w for w in weights]
        body = lane_pairs([combine(weights, v) for v in zip(*inner)], lane)
        left, _ = lane_neighbours([combine(weights, v) for v in zip(*odds)], lane)
        _, right = lane_neighbours([combine(weights, v) for v in zip(*evens)], lane)
        sums.append(jnp.concatenate([b + l + r for b, l, r in zip(body, left, right)], axis=1))
    return nodes, sums


def main_kernel(
    u_hbm, vv_hbm, d_hbm,
    ub, bb, p0, kk, q1, v1, mm, p2, v2, c0, c1, c2, c2p, a0, a1, w0, w1, w2, dd, staging,
    load_sem, u_send, u_recv, h_send, h_recv, w_send, w_recv, v_send, v_recv, p_send, p_recv, out_sem,
):
    tm, sp = lax.axis_index("tm"), lax.axis_index("space")
    n_tm, n_sp = lax.axis_size("tm"), lax.axis_size("space")
    left, right = lax.rem(sp + n_sp - 1, n_sp), lax.rem(sp + 1, n_sp)
    not_first, not_last = tm > 0, tm < n_tm - 1
    half_step = 0.5 * STEP

    def load(m, r):
        return pltpu.make_async_copy(u_hbm.at[0, m, :, r, :], ub.at[m, r + 3], load_sem.at[m, r])

    def remote(src, dst, send, recv, t, s):
        return pltpu.make_async_remote_copy(
            src_ref=src, dst_ref=dst, send_sem=send, recv_sem=recv, device_id=(t, s), device_id_type=MESH
        )

    def edge_row(k):
        return jnp.where(k < 3, k, k + 10)

    def load_edges(k):
        for m in range(3):
            load(m, edge_row(k)).start()

    def load_inner(k):
        for m in range(3):
            load(m, k + 3).start()

    each(6, load_edges)
    each(10, load_inner)

    barrier = pltpu.get_barrier_semaphore()
    for s in (left, right):
        pl.semaphore_signal(barrier, inc=1, device_id=(tm, s), device_id_type=MESH)

    @pl.when(not_first)
    def _():
        for s in (left, sp, right):
            pl.semaphore_signal(barrier, inc=1, device_id=(tm - 1, s), device_id_type=MESH)

    @pl.when(not_last)
    def _():
        pl.semaphore_wait(barrier, 5)

    @pl.when(jnp.logical_not(not_last))
    def _():
        pl.semaphore_wait(barrier, 2)

    def wait_edges(k):
        for m in range(3):
            load(m, edge_row(k)).wait()

    def wait_inner(k):
        for m in range(3):
            load(m, k + 3).wait()

    each(6, wait_edges)
    u_up = remote(ub.at[:, pl.ds(16, 3)], ub.at[:, pl.ds(0, 3)], u_send.at[0], u_recv.at[0], tm, right)
    u_down = remote(ub.at[:, pl.ds(3, 3)], ub.at[:, pl.ds(19, 3)], u_send.at[1], u_recv.at[1], tm, left)
    u_up.start()
    u_down.start()
    each(10, wait_inner)

    weights = [STEP * w for w in WEIGHTS[0]]
    later_weights = [STEP * w for w in WEIGHTS[1]]
    later_weights[1] = later_weights[1] - half_step

    def local_terms(r):
        nodes = [ub[m, r + 3] for m in range(3)]
        cubes = [cube(v) for v in nodes]
        mixed = combine(weights, nodes)
        bb[r + 3] = mixed
        return nodes[0] - 4.0 * mixed + combine([-2.0 * w for w in weights], cubes), nodes, cubes

    def local_terms_near(r):
        p0[r + 2], nodes, cubes = local_terms(r)
        kk[r + 2] = combine(later_weights, nodes)
        q1[r + 2] = combine([-2.0 * w for w in later_weights], cubes)

    def first_sweep(r):
        value = p0[r + 2] + neighbour_sum(bb[r + 2], bb[r + 3], bb[r + 4])
        mixed = half_step * value + kk[r + 2]
        v1[r + 2] = value
        mm[r + 2] = mixed
        p2[r + 2] = value + q1[r + 2] - 4.0 * mixed - STEP * cube(value)

    def second_sweep(r):
        v2[r + 1] = p2[r + 2] + neighbour_sum(mm[r + 1], mm[r + 2], mm[r + 3])

    def restrict_rim(k):
        i = 9 * k - 1
        c0[i + 1] = restrict_row(ub[0, 2 * i + 3] + ub[0, 2 * i + 4], staging.at[2 * k])
        c1[i + 1] = restrict_row(v1[2 * i + 2] + v1[2 * i + 3], staging.at[2 * k + 1])

    def coarse_row(i):
        r = 2 * i
        fields = [
            [ub[0, r + k] for k in range(2, 6)],
            [v1[r + k] for k in range(1, 5)],
            [v2[r + k] for k in range(4)],
        ]
        (c0[i + 1], c1[i + 1], c2[i + 1]), (a0[i + 2], a1[i + 1]) = coarse_terms(fields, staging)

    each(16, local_terms_near, 4)
    each(14, lambda k: first_sweep(k + 1), 7)
    each(12, lambda k: second_sweep(k + 2), 6)
    each(4, lambda k: coarse_row(k + 2), 2)

    u_up.wait_recv()
    u_down.wait_recv()

    each(4, lambda k: local_terms_near(jnp.where(k < 2, k - 2, k + 14)), 4)
    for r in (-3, 18):
        local_terms(r)
    each(6, lambda k: first_sweep(jnp.where(k < 3, k - 2, k + 12)), 6)
    each(6, lambda k: second_sweep(jnp.where(k < 3, k - 1, k + 11)), 6)
    each(4, lambda k: coarse_row(jnp.where(k < 2, k, k + 4)), 2)
    each(2, restrict_rim, 2)

    def edge_sends(rows, t):
        up = remote(rows.at[pl.ds(5, 3)], w0.at[pl.ds(0, 3)], w_send.at[0], w_recv.at[0], t, right)
        down = remote(rows.at[pl.ds(0, 3)], w0.at[pl.ds(11, 3)], w_send.at[1], w_recv.at[1], t, left)
        return up, down

    own_c0, own_w2 = c0.at[pl.ds(1, 8)], w2.at[pl.ds(1, 8)]
    start_up, start_down = edge_sends(own_c0, tm)
    next_up, next_down = edge_sends(own_w2, tm + 1)
    next_own = remote(own_w2, w0.at[pl.ds(3, 8)], w_send.at[2], w_recv.at[2], tm + 1, sp)
    is_first = jnp.logical_not(not_first)

    @pl.when(is_first)
    def _():
        start_up.start()
        start_down.start()

    def halo_sends(index, field, rows, own):
        up = remote(field.at[pl.ds(own + 8 - rows, rows)], field.at[pl.ds(own - rows, rows)], h_send.at[index], h_recv.at[index], tm, right)
        down = remote(field.at[pl.ds(own, rows)], field.at[pl.ds(own + 8, rows)], h_send.at[index + 1], h_recv.at[index + 1], tm, left)
        return [up, down]

    c2_halos = halo_sends(0, c2, 1, 1)
    a_halos = halo_sends(2, a0, 2, 2) + halo_sends(4, a1, 1, 1)

    def add_start(k):
        a0[k + 2] = a0[k + 2] - half_step * coarse_rate(c0[k], c0[k + 1], c0[k + 2])
        a1[k + 1] = a1[k + 1] - half_step * coarse_rate(c1[k], c1[k + 1], c1[k + 2])

    each(8, add_start, 8)
    for copy in a_halos + c2_halos:
        copy.start()

    v1_out = pltpu.make_async_copy(v1.at[pl.ds(2, 16)], vv_hbm.at[1], out_sem.at[0])
    v2_out = pltpu.make_async_copy(v2.at[pl.ds(1, 16)], vv_hbm.at[2], out_sem.at[1])
    u0_out = pltpu.make_async_copy(ub.at[0, pl.ds(3, 16)], vv_hbm.at[0], out_sem.at[2])
    v_next = remote(v2.at[pl.ds(1, 16)], vv_hbm.at[0], v_send.at[0], v_recv.at[0], tm + 1, sp)
    v1_out.start()
    v2_out.start()

    early = tm >= n_tm // 2

    @pl.when(is_first)
    def _():
        u0_out.start()
        w0[pl.ds(3, 8)] = c0[pl.ds(1, 8)]

    @pl.when(not_last & early)
    def _():
        v_next.start()

    for copy in a_halos + c2_halos:
        copy.wait_recv()
    p_next = remote(c2, c2p, p_send.at[0], p_recv.at[0], tm + 1, sp)

    @pl.when(not_last)
    def _():
        p_next.start()

    @pl.when(not_first)
    def _():
        next_own.wait_recv()

    start_up.wait_recv()
    start_down.wait_recv()

    def middle(k):
        w1[k] = w0[k + 1] + half_step * coarse_rate(w0[k], w0[k + 1], w0[k + 2]) + a0[k]

    def finish(k):
        w2[k] = w1[k + 1] + half_step * coarse_rate(w1[k], w1[k + 1], w1[k + 2]) + a1[k]

    each(12, middle, 12)
    each(10, finish, 10)

    @pl.when(not_last)
    def _():
        next_own.start()
        next_up.start()
        next_down.start()

    @pl.when(not_last & jnp.logical_not(early))
    def _():
        v_next.start()

    dd[1] = w1[pl.ds(1, 10)] - c1[...]
    dd[2] = w2[...] - c2[...]

    @pl.when(not_first)
    def _():
        p_next.wait_recv()
        dd[0] = w0[pl.ds(2, 10)] - c2p[...]

    @pl.when(is_first)
    def _():
        dd[0] = jnp.zeros(dd.shape[1:], F32)

    d_out = pltpu.make_async_copy(dd, d_hbm, out_sem.at[3])
    d_out.start()

    u_up.wait_send()
    u_down.wait_send()
    for copy in a_halos + c2_halos:
        copy.wait_send()

    @pl.when(is_first)
    def _():
        start_up.wait_send()
        start_down.wait_send()
        u0_out.wait()

    @pl.when(not_last)
    def _():
        next_own.wait_send()
        next_up.wait_send()
        next_down.wait_send()
        p_next.wait_send()
        v_next.wait_send()

    @pl.when(not_first)
    def _():
        v_next.wait_recv()

    v1_out.wait()
    v2_out.wait()
    d_out.wait()


def correct_kernel(vv_hbm, d_ref, o_hbm, vb, g75, g25, in_sem, out_sem):
    sub, lane = iotas()
    lanes = vb.shape[-1]
    half = lanes // 256

    def load(m):
        return pltpu.make_async_copy(vv_hbm.at[m], vb.at[m], in_sem.at[m])

    def store(m, r):
        return pltpu.make_async_copy(vb.at[m, r], o_hbm.at[0, m, :, r, :], out_sem.at[m, r])

    for m in range(3):
        load(m).start()

    def spread(m, k):
        tiles = split_tiles(d_ref[m, k])
        before, after = lane_neighbours(tiles, lane)
        for t in range(half):
            i, index = t // 2, (t % 2) * 64 + lane // 2
            low = 0.75 * tiles[i] + 0.25 * before[i]
            high = 0.75 * tiles[i] + 0.25 * after[i]
            fine = jnp.where(lane % 2 == 0, take(low, index, 1), take(high, index, 1))
            near_part, far_part = 0.75 * fine, 0.25 * fine
            for h in range(2):
                near = 4 * h + sub // 2
                far = 4 * h + (sub // 2 + 3 + 2 * (sub % 2)) % 4
                value = take(near_part, near, 0) + take(far_part, far, 0)
                columns = pl.ds(128 * (t + half * h), 128)
                g75[k, :, columns] = 0.75 * value
                g25[k, :, columns] = 0.25 * value

    def node(m):
        each(10, lambda k: spread(m, k), 2)
        load(m).wait()

        def rows(k):
            vb[m, 2 * k] = vb[m, 2 * k] + g75[k + 1] + g25[k]
            vb[m, 2 * k + 1] = vb[m, 2 * k + 1] + g75[k + 1] + g25[k + 2]
            store(m, 2 * k).start()
            store(m, 2 * k + 1).start()

        each(8, rows, 4)

    each(3, node)

    def drain(k):
        for m in range(3):
            store(m, k).wait()

    each(16, drain)


def on_device(node_values):
    _, _, depth, rows, lanes = node_values.shape
    half = lanes // 4
    fine = lambda n: pltpu.VMEM((n, 8, lanes), F32)
    coarse = lambda n: pltpu.VMEM((n, 8, half), F32)
    dma = lambda *n: pltpu.SemaphoreType.DMA(n)
    anywhere = pl.BlockSpec(memory_space=pl.ANY)
    vv, dd = pl.pallas_call(
        main_kernel,
        name="sweeps",
        out_shape=(
            jax.ShapeDtypeStruct((3, rows, depth, lanes), F32),
            jax.ShapeDtypeStruct((3, 10, 8, half), F32),
        ),
        in_specs=[anywhere],
        out_specs=(anywhere, anywhere),
        scratch_shapes=[
            pltpu.VMEM((3, 22, 8, lanes), F32), fine(22), fine(20), fine(20), fine(20), fine(20), fine(20), fine(20), fine(18),
            coarse(10), coarse(10), coarse(10), coarse(10), coarse(12), coarse(10), coarse(14), coarse(12), coarse(10),
            pltpu.VMEM((3, 10, 8, half), F32), pltpu.VMEM((6, lanes // 16, 128), F32),
            dma(3, 16), dma(2), dma(2), dma(6), dma(6), dma(3), dma(3), dma(1), dma(1), dma(1), dma(1), dma(4),
        ],
        compiler_params=pltpu.CompilerParams(
            collective_id=0, has_side_effects=True, vmem_limit_bytes=48 * 1024 * 1024
        ),
    )(node_values)
    return pl.pallas_call(
        correct_kernel,
        name="correct",
        out_shape=jax.ShapeDtypeStruct(node_values.shape, F32),
        in_specs=[anywhere, pl.BlockSpec(memory_space=pltpu.VMEM)],
        out_specs=anywhere,
        scratch_shapes=[
            pltpu.VMEM((3, rows, 8, lanes), F32), pltpu.VMEM((10, 8, lanes), F32), pltpu.VMEM((10, 8, lanes), F32),
            dma(3), dma(3, 16),
        ],
        compiler_params=pltpu.CompilerParams(vmem_limit_bytes=48 * 1024 * 1024),
    )(vv, dd)


def solution(mesh):
    return jax.shard_map(
        on_device,
        mesh=mesh,
        in_specs=(P("tm", None, None, "space", None),),
        out_specs=P("tm", None, None, "space", None),
        check_vma=False,
    )
```

```python
import functools

import jax
import jax.numpy as jnp
from jax import lax
from jax.experimental import pallas as pl
from jax.experimental.pallas import tpu as pltpu
from jax.sharding import PartitionSpec as P

STEP = 0.25
WEIGHTS = ((5.0 / 24.0, 1.0 / 3.0, -1.0 / 24.0), (-1.0 / 24.0, 1.0 / 3.0, 5.0 / 24.0))
MESH = pl.DeviceIdType.MESH
GROUP = 4
EARLY = 2
BLOCKS = ((2, 3, 4, 5), (0, 1, 6, 7))
PLACE = {r: (b, k) for b, rows in enumerate(BLOCKS) for k, r in enumerate(rows)}
F32 = jnp.float32


def neighbour_sum(above, center, below):
    lanes = center.shape[-1]
    beside = above + below + pltpu.roll(center, 1, 0) + pltpu.roll(center, 7, 0)
    return beside + pltpu.roll(center, 1, 1) + pltpu.roll(center, lanes - 1, 1)


def cube(value):
    return value * value * value


def combine(weights, terms):
    total = weights[0] * terms[0]
    for weight, term in zip(weights[1:], terms[1:]):
        total = total + weight * term
    return total


def each(count, body, unroll=1):
    def step(k, carry):
        body(k)
        return carry

    lax.fori_loop(0, count, step, 0, unroll=unroll)


def iotas():
    sub = lax.broadcasted_iota(jnp.int32, (8, 128), 0)
    lane = lax.broadcasted_iota(jnp.int32, (8, 128), 1)
    return sub, lane


def take(value, index, axis):
    return jnp.take_along_axis(value, index, axis=axis, mode="promise_in_bounds")


def split_tiles(value):
    return [value[:, 128 * t : 128 * (t + 1)] for t in range(value.shape[1] // 128)]


def lane_neighbours(tiles, lane):
    count = len(tiles)
    right_rolled = [pltpu.roll(t, 1, 1) for t in tiles]
    left_rolled = [pltpu.roll(t, 127, 1) for t in tiles]
    before = [pltpu.roll(right_rolled[-1], 4, 0)] + right_rolled[:-1]
    after = left_rolled[1:] + [pltpu.roll(left_rolled[0], 4, 0)]
    left = [jnp.where(lane == 0, before[i], right_rolled[i]) for i in range(count)]
    right = [jnp.where(lane == 127, after[i], left_rolled[i]) for i in range(count)]
    return left, right


def coarse_rate(above, center, below):
    sub, lane = iotas()
    up_index = (sub // 4) * 4 + (sub + 1) % 4
    down_index = (sub // 4) * 4 + (sub + 3) % 4
    a, c, b = split_tiles(above), split_tiles(center), split_tiles(below)
    left, right = lane_neighbours(c, lane)
    out = []
    for i in range(len(c)):
        beside = a[i] + b[i] + take(c[i], up_index, 0) + take(c[i], down_index, 0) + left[i] + right[i]
        out.append(0.25 * beside + c[i] * (0.5 - 2.0 * (c[i] * c[i])))
    return jnp.concatenate(out, axis=1)


def ring_rate(above, center, below):
    sub, _ = iotas()
    up_index = (sub // 4) * 4 + (sub + 1) % 4
    down_index = (sub // 4) * 4 + (sub + 3) % 4
    beside = above + below + pltpu.roll(center, 1, 1) + pltpu.roll(center, 255, 1)
    depth = [take(t, up_index, 0) + take(t, down_index, 0) for t in split_tiles(center)]
    beside = beside + jnp.concatenate(depth, axis=1)
    return 0.25 * beside + center * (0.5 - 2.0 * (center * center))


def strip_of(tiles, t, lane):
    after = tiles[t + 1] if t + 1 < len(tiles) else pltpu.roll(tiles[0], 4, 0)
    before = tiles[t - 1] if t > 0 else pltpu.roll(tiles[-1], 4, 0)
    return jnp.where(lane < 64, after, before)


def join_strips(strips, lane):
    block = ((lane + 16) // 32) % 4
    joined = strips[0]
    for k in range(1, 4):
        joined = jnp.where(block == k, pltpu.roll(strips[k], 32 * k, 1), joined)
    return joined


def put_block(ref, rows, strips, lane):
    ref[0] = join_strips(strips, lane)
    for k in range(4):
        ref[k + 1] = rows[k]


def get_row(ref, k):
    strip = pltpu.roll(ref[0], (128 - 32 * k) % 128, 1)
    return jnp.concatenate([ref[k + 1], strip], axis=1)


def packed_halves(row, staging):
    tiles = split_tiles(row)
    half = len(tiles) // 2
    for t in range(half):
        staging[pl.ds(16 * t, 8), :] = tiles[t]
        staging[pl.ds(16 * t + 8, 8), :] = tiles[t + half]
    even = [staging[pl.ds(16 * t, 8, stride=2), :] for t in range(half)]
    odd = [staging[pl.ds(16 * t + 1, 8, stride=2), :] for t in range(half)]
    return even, odd


def decimate_index(lane):
    return jnp.where(lane < 64, 2 * lane, 2 * lane - 127)


def lane_pairs(packed, lane):
    out = []
    for t in range(len(packed) // 2):
        p, q = packed[2 * t], packed[2 * t + 1]
        mixed = jnp.where(lane % 2 == 0, p + pltpu.roll(p, 127, 1), q + pltpu.roll(q, 1, 1))
        out.append(take(mixed, decimate_index(lane), 1))
    return out


def lane_even_odd(packed, lane):
    even, odd = [], []
    for t in range(len(packed) // 2):
        p, q = packed[2 * t], packed[2 * t + 1]
        even.append(take(jnp.where(lane % 2 == 0, p, pltpu.roll(q, 1, 1)), decimate_index(lane), 1))
        odd.append(take(jnp.where(lane % 2 == 0, pltpu.roll(p, 127, 1), q), decimate_index(lane), 1))
    return even, odd


def restrict_row(pair_sum, staging):
    _, lane = iotas()
    even, odd = packed_halves(pair_sum, staging)
    sums = lane_pairs([a + b for a, b in zip(even, odd)], lane)
    return jnp.concatenate([0.125 * v for v in sums], axis=1)


def coarse_terms(fields, staging):
    sub, lane = iotas()
    up_index = (sub // 4) * 4 + (sub + 1) % 4
    down_index = (sub // 4) * 4 + (sub + 3) % 4
    nodes, inner, evens, odds = [], [], [], []
    for n, (before, a, b, after) in enumerate(fields):
        total = a + b
        rest = (before + after) - total - 2.0 * (cube(a) + cube(b))
        even, odd = packed_halves(total, staging.at[2 * n])
        rest_even, rest_odd = packed_halves(rest, staging.at[2 * n + 1])
        count = len(even)
        inner.append(
            [
                rest_even[t] + rest_odd[t] + take(odd[t], down_index, 0) + take(even[t], up_index, 0)
                for t in range(count)
            ]
        )
        lane_even, lane_odd = lane_even_odd([even[t] + odd[t] for t in range(count)], lane)
        evens.append(lane_even)
        odds.append(lane_odd)
        nodes.append(jnp.concatenate([0.125 * (p + q) for p, q in zip(lane_even, lane_odd)], axis=1))
    sums = []
    for weights in WEIGHTS:
        weights = [0.125 * STEP * w for w in weights]
        body = lane_pairs([combine(weights, v) for v in zip(*inner)], lane)
        left, _ = lane_neighbours([combine(weights, v) for v in zip(*odds)], lane)
        _, right = lane_neighbours([combine(weights, v) for v in zip(*evens)], lane)
        sums.append(jnp.concatenate([b + l + r for b, l, r in zip(body, left, right)], axis=1))
    return nodes, sums


def main_kernel(
    u_hbm, vv_hbm, d_hbm,
    ub, bb, p0, kk, q1, v1, mm, p2, v2, vin, c0, c1, c2, c2p, a0, a1, pack, cpack, wpack, rx, wx, w0, w1, res, home, dd, staging,
    load_sem, u_send, u_recv, h_send, h_recv, a_send, a_recv, c_send, w_send, w_recv, r_send, r_recv, v_send, v_recv,
    p_send, p_recv, out_sem,
):
    tm, sp = lax.axis_index("tm"), lax.axis_index("space")
    n_tm, n_sp = lax.axis_size("tm"), lax.axis_size("space")
    left, right = lax.rem(sp + n_sp - 1, n_sp), lax.rem(sp + 1, n_sp)
    not_first, not_last = tm > 0, tm < n_tm - 1
    half_step = 0.5 * STEP
    team = GROUP * (tm // GROUP)
    spot = tm - team
    first_team = tm < GROUP
    sides = ((left, 2), (sp, 1), (right, 0))

    def load(m, r):
        return pltpu.make_async_copy(u_hbm.at[0, m, :, r, :], ub.at[m, r + 3], load_sem.at[m, r])

    def remote(src, dst, send, recv, t, s):
        return pltpu.make_async_remote_copy(
            src_ref=src, dst_ref=dst, send_sem=send, recv_sem=recv, device_id=(t, s), device_id_type=MESH
        )

    def edge_row(k):
        return jnp.where(k < 3, k, k + 10)

    def load_edges(k):
        for m in range(3):
            load(m, edge_row(k)).start()

    def load_inner(k):
        for m in range(3):
            load(m, k + 3).start()

    each(6, load_edges)
    each(10, load_inner)

    barrier = pltpu.get_barrier_semaphore()
    for d in range(GROUP):
        mate = team + lax.rem(spot + d, GROUP)
        for s, _ in sides:
            if d > 0 or s is not sp:
                pl.semaphore_signal(barrier, inc=1, device_id=(mate, s), device_id_type=MESH)

    @pl.when(jnp.logical_not(first_team))
    def _():
        for s, _ in sides:
            pl.semaphore_signal(barrier, inc=1, device_id=(tm - GROUP, s), device_id_type=MESH)

    @pl.when(tm == GROUP)
    def _():
        pl.semaphore_signal(barrier, inc=1, device_id=(tm - 1, sp), device_id_type=MESH)

    @pl.when(tm < GROUP - 1)
    def _():
        pl.semaphore_wait(barrier, 3 * GROUP + 2)

    @pl.when(tm == GROUP - 1)
    def _():
        pl.semaphore_wait(barrier, 3 * GROUP + 3)

    @pl.when(jnp.logical_not(first_team))
    def _():
        pl.semaphore_wait(barrier, 3 * GROUP - 1)

    def wait_edges(k):
        for m in range(3):
            load(m, edge_row(k)).wait()

    def wait_inner(k):
        for m in range(3):
            load(m, k + 3).wait()

    each(6, wait_edges)
    u_up = remote(ub.at[:, pl.ds(16, 3)], ub.at[:, pl.ds(0, 3)], u_send.at[0], u_recv.at[0], tm, right)
    u_down = remote(ub.at[:, pl.ds(3, 3)], ub.at[:, pl.ds(19, 3)], u_send.at[1], u_recv.at[1], tm, left)
    u_up.start()
    u_down.start()
    each(10, wait_inner)

    weights = [STEP * w for w in WEIGHTS[0]]
    later_weights = [STEP * w for w in WEIGHTS[1]]
    later_weights[1] = later_weights[1] - half_step

    def local_terms(r):
        nodes = [ub[m, r + 3] for m in range(3)]
        cubes = [cube(v) for v in nodes]
        mixed = combine(weights, nodes)
        bb[r + 3] = mixed
        return nodes[0] - 4.0 * mixed + combine([-2.0 * w for w in weights], cubes), nodes, cubes

    def local_terms_near(r):
        p0[r + 2], nodes, cubes = local_terms(r)
        kk[r + 2] = combine(later_weights, nodes)
        q1[r + 2] = combine([-2.0 * w for w in later_weights], cubes)

    def first_sweep(r):
        value = p0[r + 2] + neighbour_sum(bb[r + 2], bb[r + 3], bb[r + 4])
        mixed = half_step * value + kk[r + 2]
        v1[r + 2] = value
        mm[r + 2] = mixed
        p2[r + 2] = value + q1[r + 2] - 4.0 * mixed - STEP * cube(value)

    def second_sweep(r):
        v2[r + 1] = p2[r + 2] + neighbour_sum(mm[r + 1], mm[r + 2], mm[r + 3])

    def restrict_rim(k):
        i = 9 * k - 1
        c0[i + 1] = restrict_row(ub[0, 2 * i + 3] + ub[0, 2 * i + 4], staging.at[2 * k])
        c1[i + 1] = restrict_row(v1[2 * i + 2] + v1[2 * i + 3], staging.at[2 * k + 1])

    def coarse_row(i):
        r = 2 * i
        fields = [
            [ub[0, r + k] for k in range(2, 6)],
            [v1[r + k] for k in range(1, 5)],
            [v2[r + k] for k in range(4)],
        ]
        (c0[i + 1], c1[i + 1], c2[i + 1]), (a0[i + 2], a1[i + 1]) = coarse_terms(fields, staging)

    _, lane = iotas()
    is_first = jnp.logical_not(not_first)

    def pack_rows(rows, place):
        tiles = [split_tiles(row) for row in rows]
        for t in range(GROUP):
            put_block(place(t), [v[t] for v in tiles], [strip_of(v, t, lane) for v in tiles], lane)

    def start_copies(piece, go):
        for d in range(GROUP):
            keeper = lax.rem(spot + d, GROUP)
            for s, p in sides:
                if p == piece and (d > 0 or p != 1):
                    copy = remote(
                        cpack.at[keeper], wx.at[p], c_send.at[d, p], w_recv.at[p], team + keeper, s
                    )
                    go(copy)

    def terms_copy(block, fields, keeper, slot, m, piece, s):
        return remote(
            pack.at[block, keeper, pl.ds(0, fields)], rx.at[block, m, piece, pl.ds(0, fields)],
            a_send.at[block, slot, piece], a_recv.at[block, m, piece], team + keeper, s,
        )

    def sized(block, m, go):
        if block == 0:
            pl.when(m < 2)(lambda: go(2))
            pl.when(m == 2)(lambda: go(1))
        else:
            pl.when(m < 3)(lambda: go(2))
            pl.when(m == 3)(lambda: go(1))

    def terms_copies(block, go):
        def mate(d):
            keeper = lax.rem(spot + d, GROUP)

            @pl.when(d > 0)
            def _():
                go(terms_copy(block, 2, keeper, d, spot, 1, sp))

            def beside(fields):
                go(terms_copy(block, fields, keeper, d, spot, 2, left))
                go(terms_copy(block, fields, keeper, d, spot, 0, right))

            sized(block, spot, beside)

        each(GROUP, mate)

    def wait_terms(block):
        def slice_terms(m):
            @pl.when(m != spot)
            def _():
                terms_copy(block, 2, spot, 0, m, 1, left).wait_recv()

            def beside(fields):
                for piece in (0, 2):
                    terms_copy(block, fields, spot, 0, m, piece, left).wait_recv()

            sized(block, m, beside)

        each(GROUP, slice_terms)

    def send_terms(block):
        for k in BLOCKS[block]:
            a0[k + 2] = a0[k + 2] - half_step * coarse_rate(c0[k], c0[k + 1], c0[k + 2])
            a1[k + 1] = a1[k + 1] - half_step * coarse_rate(c1[k], c1[k + 1], c1[k + 2])
        pack_rows([a0[k + 2] for k in BLOCKS[block]], lambda t: pack.at[block, t, 0])
        pack_rows([a1[k + 1] for k in BLOCKS[block]], lambda t: pack.at[block, t, 1])
        terms_copies(block, lambda copy: copy.start())
        rx[block, spot, 1] = pack[block, spot]

    def restrict_first(i):
        c0[i + 1] = restrict_row(ub[0, 2 * i + 3] + ub[0, 2 * i + 4], staging.at[i % 4])

    for k in range(8):
        restrict_first(k)

    @pl.when(is_first)
    def _():
        for block in range(2):
            pack_rows([c0[k + 1] for k in BLOCKS[block]], lambda t: cpack.at[t, block])
        for piece in range(3):
            start_copies(piece, lambda copy: copy.start())
        wx[1] = cpack[0]

    each(16, local_terms_near, 4)
    each(14, lambda k: first_sweep(k + 1), 7)
    each(12, lambda k: second_sweep(k + 2), 6)

    def v_part(index, start, count):
        return remote(
            v2.at[pl.ds(start + 1, count)], vin.at[pl.ds(start, count)], v_send.at[index], v_recv.at[index], tm + 1, sp
        )

    v_ranges = ((2, EARLY), (0, 2), (2 + EARLY, 14 - EARLY))
    v_parts = [v_part(n, *rows) for n, rows in enumerate(v_ranges)]

    @pl.when(not_last)
    def _():
        v_parts[0].start()


    each(4, lambda k: coarse_row(k + 2), 2)
    for n, i in enumerate((1, 6)):
        c1[i + 1] = restrict_row(v1[2 * i + 2] + v1[2 * i + 3], staging.at[n])
    send_terms(0)

    u_up.wait_recv()
    u_down.wait_recv()

    each(4, lambda k: local_terms_near(jnp.where(k < 2, k - 2, k + 14)), 4)
    for r in (-3, 18):
        local_terms(r)
    each(6, lambda k: first_sweep(jnp.where(k < 3, k - 2, k + 12)), 6)
    each(6, lambda k: second_sweep(jnp.where(k < 3, k - 1, k + 11)), 6)
    each(4, lambda k: coarse_row(jnp.where(k < 2, k, k + 4)), 2)
    each(2, restrict_rim, 2)

    send_terms(1)

    @pl.when(not_last)
    def _():
        for copy in v_parts[1:]:
            copy.start()


    c2_up = remote(c2.at[pl.ds(8, 1)], c2.at[pl.ds(0, 1)], h_send.at[0], h_recv.at[0], tm, right)
    c2_down = remote(c2.at[pl.ds(1, 1)], c2.at[pl.ds(9, 1)], h_send.at[1], h_recv.at[1], tm, left)
    c2_up.start()
    c2_down.start()
    v1_out = pltpu.make_async_copy(v1.at[pl.ds(2, 16)], vv_hbm.at[1], out_sem.at[0])
    v2_out = pltpu.make_async_copy(v2.at[pl.ds(1, 16)], vv_hbm.at[2], out_sem.at[1])
    u0_out = pltpu.make_async_copy(ub.at[0, pl.ds(3, 16)], vv_hbm.at[0], out_sem.at[2])
    p_next = [
        remote(c2.at[pl.ds(k, 1)], c2p.at[pl.ds(k, 1)], p_send.at[n], p_recv.at[n], tm + 1, sp) for n, k in enumerate((0, 9))
    ]
    v1_out.start()
    v2_out.start()

    @pl.when(is_first)
    def _():
        u0_out.start()

    wait_terms(0)
    wait_terms(1)
    c2_up.wait_recv()
    c2_down.wait_recv()

    @pl.when(not_last)
    def _():
        for copy in p_next:
            copy.start()

    for piece in (0, 2):
        remote(wpack, wx.at[piece], w_send.at[piece], w_recv.at[piece], tm, left).wait_recv()

    @pl.when(not_first)
    def _():
        remote(wpack, wx.at[1], w_send.at[1], w_recv.at[1], tm, left).wait_recv()

    for piece in range(3):
        for r in range(8):
            block, k = PLACE[r]
            w0[8 * piece + r] = get_row(wx.at[piece, block], k)

    def go_home(m, go, here):
        owner = team + m
        own = remote(res.at[m], home.at[:, pl.ds(1, 8), spot], r_send.at[m, 1], r_recv.at[spot, 1], owner, sp)
        up = remote(res.at[m, :, 7], home.at[:, 0, spot], r_send.at[m, 0], r_recv.at[spot, 0], owner, right)
        down = remote(res.at[m, :, 0], home.at[:, 9, spot], r_send.at[m, 2], r_recv.at[spot, 2], owner, left)
        go(up)
        go(down)

        @pl.when(m != spot)
        def _():
            go(own)

        @pl.when(m == spot)
        def _():
            here()

    def sweep(m):
        def term(field, k):
            block, place = PLACE[k % 8]
            return get_row(rx.at[block, m, k // 8, field], place)

        def keep(field, k, value):
            if 8 <= k < 16:
                res[m, field, k - 8] = value[:, :128]

        for k in range(8, 16):
            keep(0, k, w0[k])
        for k in range(1, 23):
            value = w0[k] + half_step * ring_rate(w0[k - 1], w0[k], w0[k + 1]) + term(0, k)
            w1[k] = value
            keep(1, k, value)
        for k in range(2, 22):
            value = w1[k] + half_step * ring_rate(w1[k - 1], w1[k], w1[k + 1]) + term(1, k)
            w0[k] = value
            keep(2, k, value)

        def here():
            home[:, pl.ds(1, 8), spot] = res[m]

        go_home(m, lambda copy: copy.start(), here)

    each(GROUP, sweep)

    group_sends = [
        remote(wpack, wx.at[piece], w_send.at[piece], w_recv.at[piece], tm + GROUP, s) for s, piece in sides
    ]

    @pl.when(first_team)
    def _():
        rows = [split_tiles(w0[k]) for k in range(8, 16)]
        for block in range(2):
            put_block(wpack.at[block], [rows[r][0] for r in BLOCKS[block]], [rows[r][1] for r in BLOCKS[block]], lane)
        for copy in group_sends:
            copy.start()

    def wait_home(t):
        for piece, source, target in (
            (0, res.at[0, :, 7], home.at[:, 0, t]),
            (2, res.at[0, :, 0], home.at[:, 9, t]),
        ):
            remote(source, target, r_send.at[0, piece], r_recv.at[t, piece], tm, left).wait_recv()

        @pl.when(t != spot)
        def _():
            remote(res.at[0], home.at[:, pl.ds(1, 8), t], r_send.at[0, 1], r_recv.at[t, 1], tm, left).wait_recv()

    each(GROUP, wait_home)

    for t in range(GROUP):
        columns = pl.ds(128 * t, 128)
        dd[1, :, :, columns] = home[1, :, t] - c1[:, :, columns]
        dd[2, :, :, columns] = home[2, :, t] - c2[:, :, columns]

    d_out = [
        pltpu.make_async_copy(dd.at[pl.ds(1, 2)], d_hbm.at[pl.ds(1, 2)], out_sem.at[3]),
        pltpu.make_async_copy(dd.at[pl.ds(0, 1)], d_hbm.at[pl.ds(0, 1)], out_sem.at[4]),
    ]
    d_out[0].start()

    @pl.when(is_first)
    def _():
        dd[0] = jnp.zeros(dd.shape[1:], F32)

    @pl.when(not_first)
    def _():
        for copy in v_parts:
            copy.wait_recv()
        pltpu.make_async_copy(vin, vv_hbm.at[0], out_sem.at[2]).start()
        for i in range(8):
            c2p[i + 1] = restrict_row(vin[2 * i] + vin[2 * i + 1], staging.at[i % 4])
        for copy in p_next:
            copy.wait_recv()
        for t in range(GROUP):
            columns = pl.ds(128 * t, 128)
            dd[0, :, :, columns] = home[0, :, t] - c2p[:, :, columns]

    d_out[1].start()

    for copy in (u_up, u_down, c2_up, c2_down):
        copy.wait_send()
    for block in range(2):
        terms_copies(block, lambda copy: copy.wait_send())
    each(GROUP, lambda m: go_home(m, lambda copy: copy.wait_send(), lambda: None))

    @pl.when(is_first)
    def _():
        for piece in range(3):
            start_copies(piece, lambda copy: copy.wait_send())
        u0_out.wait()

    @pl.when(first_team)
    def _():
        for copy in group_sends:
            copy.wait_send()

    @pl.when(not_last)
    def _():
        for copy in p_next:
            copy.wait_send()
        for copy in v_parts:
            copy.wait_send()

    @pl.when(not_first)
    def _():
        pltpu.make_async_copy(vin, vv_hbm.at[0], out_sem.at[2]).wait()

    v1_out.wait()
    v2_out.wait()
    for copy in d_out:
        copy.wait()


def correct_kernel(vv_hbm, d_ref, o_hbm, vb, g75, g25, in_sem, out_sem):
    sub, lane = iotas()
    lanes = vb.shape[-1]
    half = lanes // 256

    def load(m):
        return pltpu.make_async_copy(vv_hbm.at[m], vb.at[m], in_sem.at[m])

    def store(m, r):
        return pltpu.make_async_copy(vb.at[m, r], o_hbm.at[0, m, :, r, :], out_sem.at[m, r])

    for m in range(3):
        load(m).start()

    def spread(m, k):
        tiles = split_tiles(d_ref[m, k])
        before, after = lane_neighbours(tiles, lane)
        for t in range(half):
            i, index = t // 2, (t % 2) * 64 + lane // 2
            low = 0.75 * tiles[i] + 0.25 * before[i]
            high = 0.75 * tiles[i] + 0.25 * after[i]
            fine = jnp.where(lane % 2 == 0, take(low, index, 1), take(high, index, 1))
            near_part, far_part = 0.75 * fine, 0.25 * fine
            for h in range(2):
                near = 4 * h + sub // 2
                far = 4 * h + (sub // 2 + 3 + 2 * (sub % 2)) % 4
                value = take(near_part, near, 0) + take(far_part, far, 0)
                columns = pl.ds(128 * (t + half * h), 128)
                g75[k, :, columns] = 0.75 * value
                g25[k, :, columns] = 0.25 * value

    def node(m):
        each(10, lambda k: spread(m, k), 2)
        load(m).wait()

        def rows(k):
            vb[m, 2 * k] = vb[m, 2 * k] + g75[k + 1] + g25[k]
            vb[m, 2 * k + 1] = vb[m, 2 * k + 1] + g75[k + 1] + g25[k + 2]
            store(m, 2 * k).start()
            store(m, 2 * k + 1).start()

        each(8, rows, 4)

    each(3, node)

    def drain(k):
        for m in range(3):
            store(m, k).wait()

    each(16, drain)


def on_device(node_values):
    _, _, depth, rows, lanes = node_values.shape
    half = lanes // 4
    fine = lambda n: pltpu.VMEM((n, 8, lanes), F32)
    coarse = lambda n: pltpu.VMEM((n, 8, half), F32)
    tiles = lambda *n: pltpu.VMEM(n + (8, 128), F32)
    dma = lambda *n: pltpu.SemaphoreType.DMA(n)
    anywhere = pl.BlockSpec(memory_space=pl.ANY)
    vv, dd = pl.pallas_call(
        main_kernel,
        name="sweeps",
        out_shape=(
            jax.ShapeDtypeStruct((3, rows, depth, lanes), F32),
            jax.ShapeDtypeStruct((3, 10, 8, half), F32),
        ),
        in_specs=[anywhere],
        out_specs=(anywhere, anywhere),
        scratch_shapes=[
            pltpu.VMEM((3, 22, 8, lanes), F32), fine(22), fine(20), fine(20), fine(20), fine(20), fine(20), fine(20), fine(18), fine(16),
            coarse(10), coarse(10), coarse(10), coarse(10), coarse(12), coarse(10),
            tiles(2, GROUP, 2, 5), tiles(GROUP, 2, 5), tiles(2, 5), tiles(2, GROUP, 3, 2, 5), tiles(3, 2, 5),
            pltpu.VMEM((24, 8, 256), F32), pltpu.VMEM((24, 8, 256), F32), tiles(GROUP, 3, 8), tiles(3, 10, GROUP),
            pltpu.VMEM((3, 10, 8, half), F32), pltpu.VMEM((6, lanes // 16, 128), F32),
            dma(3, 16), dma(2), dma(2), dma(2), dma(2), dma(2, GROUP, 3), dma(2, GROUP, 3), dma(GROUP, 3), dma(3), dma(3),
            dma(GROUP, 3), dma(GROUP, 3), dma(3), dma(3), dma(2), dma(2), dma(5),
        ],
        compiler_params=pltpu.CompilerParams(
            collective_id=0, has_side_effects=True, vmem_limit_bytes=48 * 1024 * 1024
        ),
    )(node_values)
    return pl.pallas_call(
        correct_kernel,
        name="correct",
        out_shape=jax.ShapeDtypeStruct(node_values.shape, F32),
        in_specs=[anywhere, pl.BlockSpec(memory_space=pltpu.VMEM)],
        out_specs=anywhere,
        scratch_shapes=[
            pltpu.VMEM((3, rows, 8, lanes), F32), pltpu.VMEM((10, 8, lanes), F32), pltpu.VMEM((10, 8, lanes), F32),
            dma(3), dma(3, 16),
        ],
        compiler_params=pltpu.CompilerParams(vmem_limit_bytes=48 * 1024 * 1024),
    )(vv, dd)


def solution(mesh):
    return jax.shard_map(
        on_device,
        mesh=mesh,
        in_specs=(P("tm", None, None, "space", None),),
        out_specs=P("tm", None, None, "space", None),
        check_vma=False,
    )
```

```python
import functools

import jax
import jax.numpy as jnp
from jax import lax
from jax.experimental import pallas as pl
from jax.experimental.pallas import tpu as pltpu
from jax.sharding import PartitionSpec as P

STEP = 0.25
WEIGHTS = ((5.0 / 24.0, 1.0 / 3.0, -1.0 / 24.0), (-1.0 / 24.0, 1.0 / 3.0, 5.0 / 24.0))
MESH = pl.DeviceIdType.MESH
GROUP = 4
ROWS = ((2, 2), (4, 4), (8, 4), (12, 4), (0, 2))
BLOCKS = ((2, 3, 4, 5), (0, 1, 6, 7))
PLACE = {r: (b, k) for b, rows in enumerate(BLOCKS) for k, r in enumerate(rows)}
F32 = jnp.float32


def neighbour_sum(above, center, below):
    lanes = center.shape[-1]
    beside = above + below + pltpu.roll(center, 1, 0) + pltpu.roll(center, 7, 0)
    return beside + pltpu.roll(center, 1, 1) + pltpu.roll(center, lanes - 1, 1)


def cube(value):
    return value * value * value


def combine(weights, terms):
    total = weights[0] * terms[0]
    for weight, term in zip(weights[1:], terms[1:]):
        total = total + weight * term
    return total


def each(count, body, unroll=1):
    def step(k, carry):
        body(k)
        return carry

    lax.fori_loop(0, count, step, 0, unroll=unroll)


def iotas():
    sub = lax.broadcasted_iota(jnp.int32, (8, 128), 0)
    lane = lax.broadcasted_iota(jnp.int32, (8, 128), 1)
    return sub, lane


def take(value, index, axis):
    return jnp.take_along_axis(value, index, axis=axis, mode="promise_in_bounds")


def split_tiles(value):
    return [value[:, 128 * t : 128 * (t + 1)] for t in range(value.shape[1] // 128)]


def lane_neighbours(tiles, lane):
    count = len(tiles)
    right_rolled = [pltpu.roll(t, 1, 1) for t in tiles]
    left_rolled = [pltpu.roll(t, 127, 1) for t in tiles]
    before = [pltpu.roll(right_rolled[-1], 4, 0)] + right_rolled[:-1]
    after = left_rolled[1:] + [pltpu.roll(left_rolled[0], 4, 0)]
    left = [jnp.where(lane == 0, before[i], right_rolled[i]) for i in range(count)]
    right = [jnp.where(lane == 127, after[i], left_rolled[i]) for i in range(count)]
    return left, right


def coarse_rate(above, center, below):
    sub, lane = iotas()
    up_index = (sub // 4) * 4 + (sub + 1) % 4
    down_index = (sub // 4) * 4 + (sub + 3) % 4
    a, c, b = split_tiles(above), split_tiles(center), split_tiles(below)
    left, right = lane_neighbours(c, lane)
    out = []
    for i in range(len(c)):
        beside = a[i] + b[i] + take(c[i], up_index, 0) + take(c[i], down_index, 0) + left[i] + right[i]
        out.append(0.25 * beside + c[i] * (0.5 - 2.0 * (c[i] * c[i])))
    return jnp.concatenate(out, axis=1)


def ring_rate(above, center, below):
    sub, _ = iotas()
    up_index = (sub // 4) * 4 + (sub + 1) % 4
    down_index = (sub // 4) * 4 + (sub + 3) % 4
    beside = above + below + pltpu.roll(center, 1, 1) + pltpu.roll(center, 255, 1)
    depth = [take(t, up_index, 0) + take(t, down_index, 0) for t in split_tiles(center)]
    beside = beside + jnp.concatenate(depth, axis=1)
    return 0.25 * beside + center * (0.5 - 2.0 * (center * center))


def strip_of(tiles, t, lane):
    after = tiles[t + 1] if t + 1 < len(tiles) else pltpu.roll(tiles[0], 4, 0)
    before = tiles[t - 1] if t > 0 else pltpu.roll(tiles[-1], 4, 0)
    return jnp.where(lane < 64, after, before)


def join_strips(strips, lane):
    block = ((lane + 16) // 32) % 4
    joined = strips[0]
    for k in range(1, 4):
        joined = jnp.where(block == k, pltpu.roll(strips[k], 32 * k, 1), joined)
    return joined


def put_block(ref, rows, strips, lane):
    ref[0] = join_strips(strips, lane)
    for k in range(4):
        ref[k + 1] = rows[k]


def get_row(ref, k):
    strip = pltpu.roll(ref[0], (128 - 32 * k) % 128, 1)
    return jnp.concatenate([ref[k + 1], strip], axis=1)


def packed_halves(row, staging):
    tiles = split_tiles(row)
    half = len(tiles) // 2
    for t in range(half):
        staging[pl.ds(16 * t, 8), :] = tiles[t]
        staging[pl.ds(16 * t + 8, 8), :] = tiles[t + half]
    even = [staging[pl.ds(16 * t, 8, stride=2), :] for t in range(half)]
    odd = [staging[pl.ds(16 * t + 1, 8, stride=2), :] for t in range(half)]
    return even, odd


def decimate_index(lane):
    return jnp.where(lane < 64, 2 * lane, 2 * lane - 127)


def lane_pairs(packed, lane):
    out = []
    for t in range(len(packed) // 2):
        p, q = packed[2 * t], packed[2 * t + 1]
        mixed = jnp.where(lane % 2 == 0, p + pltpu.roll(p, 127, 1), q + pltpu.roll(q, 1, 1))
        out.append(take(mixed, decimate_index(lane), 1))
    return out


def lane_even_odd(packed, lane):
    even, odd = [], []
    for t in range(len(packed) // 2):
        p, q = packed[2 * t], packed[2 * t + 1]
        even.append(take(jnp.where(lane % 2 == 0, p, pltpu.roll(q, 1, 1)), decimate_index(lane), 1))
        odd.append(take(jnp.where(lane % 2 == 0, pltpu.roll(p, 127, 1), q), decimate_index(lane), 1))
    return even, odd


def restrict_row(pair_sum, staging):
    _, lane = iotas()
    even, odd = packed_halves(pair_sum, staging)
    sums = lane_pairs([a + b for a, b in zip(even, odd)], lane)
    return jnp.concatenate([0.125 * v for v in sums], axis=1)


def coarse_terms(fields, staging):
    sub, lane = iotas()
    up_index = (sub // 4) * 4 + (sub + 1) % 4
    down_index = (sub // 4) * 4 + (sub + 3) % 4
    nodes, inner, evens, odds = [], [], [], []
    for n, (before, a, b, after) in enumerate(fields):
        total = a + b
        rest = (before + after) - total - 2.0 * (cube(a) + cube(b))
        even, odd = packed_halves(total, staging.at[2 * n])
        rest_even, rest_odd = packed_halves(rest, staging.at[2 * n + 1])
        count = len(even)
        inner.append(
            [
                rest_even[t] + rest_odd[t] + take(odd[t], down_index, 0) + take(even[t], up_index, 0)
                for t in range(count)
            ]
        )
        lane_even, lane_odd = lane_even_odd([even[t] + odd[t] for t in range(count)], lane)
        evens.append(lane_even)
        odds.append(lane_odd)
        nodes.append(jnp.concatenate([0.125 * (p + q) for p, q in zip(lane_even, lane_odd)], axis=1))
    sums = []
    for weights in WEIGHTS:
        weights = [0.125 * STEP * w for w in weights]
        body = lane_pairs([combine(weights, v) for v in zip(*inner)], lane)
        left, _ = lane_neighbours([combine(weights, v) for v in zip(*odds)], lane)
        _, right = lane_neighbours([combine(weights, v) for v in zip(*evens)], lane)
        sums.append(jnp.concatenate([b + l + r for b, l, r in zip(body, left, right)], axis=1))
    return nodes, sums


def main_kernel(
    u_hbm, vv_hbm, d_hbm,
    ub, bb, p0, kk, q1, v1, mm, p2, v2, vin, around, relay, c0, c1, c2, c2p, a0, a1, pack, cpack, wpack, rx, wx, w0, w1, res, home, edges, dd, staging,
    load_sem, u_send, u_recv, e_send, e_recv, h_send, h_recv, a_send, a_recv, c_send, w_send, w_recv, r_send, r_recv, g_send, g_recv, v_send, v_recv, o_send, o_recv, q_send, q_recv,
    p_send, p_recv, out_sem,
):
    tm, sp = lax.axis_index("tm"), lax.axis_index("space")
    n_tm, n_sp = lax.axis_size("tm"), lax.axis_size("space")
    left, right = lax.rem(sp + n_sp - 1, n_sp), lax.rem(sp + 1, n_sp)
    not_first, not_last = tm > 0, tm < n_tm - 1
    half_step = 0.5 * STEP
    team = GROUP * (tm // GROUP)
    spot = tm - team
    first_team = tm < GROUP
    sides = ((left, 2), (sp, 1), (right, 0))

    def load(m, r):
        return pltpu.make_async_copy(u_hbm.at[0, m, :, r, :], ub.at[m, r + 3], load_sem.at[m, r])

    def remote(src, dst, send, recv, t, s):
        return pltpu.make_async_remote_copy(
            src_ref=src, dst_ref=dst, send_sem=send, recv_sem=recv, device_id=(t, s), device_id_type=MESH
        )

    def edge_row(k):
        return jnp.where(k < 3, k, k + 10)

    def load_edges(k):
        for m in range(3):
            load(m, edge_row(k)).start()

    def load_inner(k):
        for m in range(3):
            load(m, k + 3).start()

    each(6, load_edges)
    each(10, load_inner)

    barrier = pltpu.get_barrier_semaphore()
    for d in range(GROUP):
        mate = team + lax.rem(spot + d, GROUP)
        for s, _ in sides:
            if d > 0 or s is not sp:
                pl.semaphore_signal(barrier, inc=1, device_id=(mate, s), device_id_type=MESH)

    @pl.when(jnp.logical_not(first_team))
    def _():
        for s, _ in sides:
            pl.semaphore_signal(barrier, inc=1, device_id=(tm - GROUP, s), device_id_type=MESH)

    @pl.when(tm == GROUP)
    def _():
        pl.semaphore_signal(barrier, inc=1, device_id=(tm - 1, sp), device_id_type=MESH)

    @pl.when(tm < GROUP - 1)
    def _():
        pl.semaphore_wait(barrier, 3 * GROUP + 2)

    @pl.when(tm == GROUP - 1)
    def _():
        pl.semaphore_wait(barrier, 3 * GROUP + 3)

    @pl.when(jnp.logical_not(first_team))
    def _():
        pl.semaphore_wait(barrier, 3 * GROUP - 1)

    def wait_edges(k):
        for m in range(3):
            load(m, edge_row(k)).wait()

    def wait_inner(k):
        for m in range(3):
            load(m, k + 3).wait()

    each(6, wait_edges)
    u_copies = [
        remote(ub.at[:, pl.ds(18, 1)], ub.at[:, pl.ds(2, 1)], u_send.at[0], u_recv.at[0], tm, right),
        remote(ub.at[:, pl.ds(3, 1)], ub.at[:, pl.ds(19, 1)], u_send.at[1], u_recv.at[1], tm, left),
    ]
    for copy in u_copies:
        copy.start()

    weights = [STEP * w for w in WEIGHTS[0]]
    later_weights = [STEP * w for w in WEIGHTS[1]]
    later_weights[1] = later_weights[1] - half_step

    def local_terms(r):
        nodes = [ub[m, r + 3] for m in range(3)]
        cubes = [cube(v) for v in nodes]
        mixed = combine(weights, nodes)
        bb[r + 3] = mixed
        p0[r + 2] = nodes[0] - 4.0 * mixed + combine([-2.0 * w for w in weights], cubes)
        kk[r + 2] = combine(later_weights, nodes)
        q1[r + 2] = combine([-2.0 * w for w in later_weights], cubes)

    def first_sweep(r):
        value = p0[r + 2] + neighbour_sum(bb[r + 2], bb[r + 3], bb[r + 4])
        mixed = half_step * value + kk[r + 2]
        v1[r + 2] = value
        mm[r + 2] = mixed
        p2[r + 2] = value + q1[r + 2] - 4.0 * mixed - STEP * cube(value)

    def second_sweep(r):
        v2[r + 1] = p2[r + 2] + neighbour_sum(mm[r + 1], mm[r + 2], mm[r + 3])

    def restrict_rim(k):
        i = 9 * k - 1
        c1[i + 1] = restrict_row(v1[2 * i + 2] + v1[2 * i + 3], staging.at[k])

    def coarse_row(i):
        r = 2 * i
        fields = [
            [ub[0, r + k] for k in range(2, 6)],
            [v1[r + k] for k in range(1, 5)],
            [v2[r + k] for k in range(4)],
        ]
        (_, c1[i + 1], c2[i + 1]), (a0[i + 2], a1[i + 1]) = coarse_terms(fields, staging)

    _, lane = iotas()
    is_first = jnp.logical_not(not_first)

    def pack_rows(rows, place):
        tiles = [split_tiles(row) for row in rows]
        for t in range(GROUP):
            put_block(place(t), [v[t] for v in tiles], [strip_of(v, t, lane) for v in tiles], lane)

    def start_copies(piece, go):
        for d in range(GROUP):
            keeper = lax.rem(spot + d, GROUP)
            for s, p in sides:
                if p == piece and (d > 0 or p != 1):
                    copy = remote(
                        cpack.at[keeper], wx.at[p], c_send.at[d, p], w_recv.at[p], team + keeper, s
                    )
                    go(copy)

    def terms_copy(block, fields, keeper, slot, m, piece, s):
        return remote(
            pack.at[block, keeper, pl.ds(0, fields)], rx.at[block, m, piece, pl.ds(0, fields)],
            a_send.at[block, slot, piece], a_recv.at[block, m, piece], team + keeper, s,
        )

    def sized(block, m, go):
        if block == 0:
            pl.when(m < 2)(lambda: go(2))
            pl.when(m == 2)(lambda: go(1))
        else:
            pl.when(m < 3)(lambda: go(2))
            pl.when(m == 3)(lambda: go(1))

    def terms_copies(block, go):
        def mate(d):
            keeper = lax.rem(spot + d, GROUP)

            @pl.when(d > 0)
            def _():
                go(terms_copy(block, 2, keeper, d, spot, 1, sp))

            def beside(fields):
                go(terms_copy(block, fields, keeper, d, spot, 2, left))
                go(terms_copy(block, fields, keeper, d, spot, 0, right))

            sized(block, spot, beside)

        each(GROUP, mate)

    def wait_terms(block):
        def slice_terms(m):
            @pl.when(m != spot)
            def _():
                terms_copy(block, 2, spot, 0, m, 1, left).wait_recv()

            def beside(fields):
                for piece in (0, 2):
                    terms_copy(block, fields, spot, 0, m, piece, left).wait_recv()

            sized(block, m, beside)

        each(GROUP, slice_terms)

    def send_terms(block):
        for k in BLOCKS[block]:
            a0[k + 2] = a0[k + 2] - half_step * coarse_rate(c0[k], c0[k + 1], c0[k + 2])
            a1[k + 1] = a1[k + 1] - half_step * coarse_rate(c1[k], c1[k + 1], c1[k + 2])
        pack_rows([a0[k + 2] for k in BLOCKS[block]], lambda t: pack.at[block, t, 0])
        pack_rows([a1[k + 1] for k in BLOCKS[block]], lambda t: pack.at[block, t, 1])
        terms_copies(block, lambda copy: copy.start())
        rx[block, spot, 1] = pack[block, spot]

    def restrict_first(i):
        c0[i + 1] = restrict_row(ub[0, 2 * i + 3] + ub[0, 2 * i + 4], staging.at[i % 4])

    each(6, lambda k: local_terms(edge_row(k)), 3)
    for k in (0, 7):
        restrict_first(k)
    for r in (1, 14):
        first_sweep(r)
    rim_copies, rows_of = [], (16, 16, 16, 8)
    for n, (field, offset, up, down) in enumerate(((bb, 3, 14, 1), (v1, 2, 14, 1), (mm, 2, 14, 1), (c0, 1, 7, 0))):
        up_target, down_target = up + offset - rows_of[n], down + offset + rows_of[n]
        rim_copies += [
            remote(field.at[pl.ds(up + offset, 1)], field.at[pl.ds(up_target, 1)], e_send.at[0, n], e_recv.at[0, n], tm, right),
            remote(field.at[pl.ds(down + offset, 1)], field.at[pl.ds(down_target, 1)], e_send.at[1, n], e_recv.at[1, n], tm, left),
        ]
    for copy in rim_copies:
        copy.start()
    each(10, wait_inner)
    for k in range(1, 7):
        restrict_first(k)

    @pl.when(is_first)
    def _():
        for block in range(2):
            pack_rows([c0[k + 1] for k in BLOCKS[block]], lambda t: cpack.at[t, block])
        for piece in range(3):
            start_copies(piece, lambda copy: copy.start())
        wx[1] = cpack[0]

    each(10, lambda k: local_terms(k + 3), 5)
    each(12, lambda k: first_sweep(k + 2), 6)
    each(12, lambda k: second_sweep(k + 2), 6)

    def v_part(index, start, count):
        return remote(
            v2.at[pl.ds(start + 1, count)], vin.at[pl.ds(start, count)], v_send.at[index], v_recv.at[index], tm + 1, sp
        )

    v_parts = [v_part(n, *rows) for n, rows in enumerate(ROWS)]
    behind = team + lax.rem(spot + GROUP - 1, GROUP)
    start, count = ROWS[1]
    hops = [
        remote(v2.at[pl.ds(start + 1, count)], around.at[0], o_send.at[0], o_recv.at[0], behind, sp),
        remote(around.at[0], around.at[1], o_send.at[1], o_recv.at[1], behind, sp),
        remote(around.at[1], vin.at[pl.ds(start, count)], o_send.at[2], v_recv.at[1], behind, sp),
    ]
    goes = [spot != GROUP - 1, spot != GROUP - 2, spot != GROUP - 3]

    def start_hop(n):
        @pl.when(goes[n])
        def _():
            if n > 0:
                hops[n - 1].wait_recv()
            hops[n].start()

    @pl.when(not_last)
    def _():
        v_parts[0].start()

    start_hop(0)

    relay_in, relay_out = [], []
    for k, n in enumerate((1, 3)):
        first, count = ROWS[n]
        held = relay.at[k]
        relay_in.append(remote(v2.at[pl.ds(first + 1, count)], held, q_send.at[k], q_recv.at[k], team, sp))
        relay_out.append(remote(held, vin.at[pl.ds(first, count)], q_send.at[2 + k], v_recv.at[n], tm + GROUP, sp))

    def start_relay(k):
        @pl.when(is_first)
        def _():
            relay_in[k].wait_recv()
            relay_out[k].start()

    @pl.when(tm == GROUP - 1)
    def _():
        relay_in[0].start()

    each(4, lambda k: coarse_row(k + 2), 2)
    for n, i in enumerate((1, 6)):
        c1[i + 1] = restrict_row(v1[2 * i + 2] + v1[2 * i + 3], staging.at[n])
    send_terms(0)

    for copy in u_copies:
        copy.wait_recv()
    for r in (-1, 16):
        local_terms(r)
    for r in (0, 15):
        first_sweep(r)
    for r in (1, 14):
        second_sweep(r)
    for i in (1, 6):
        coarse_row(i)
    for copy in rim_copies:
        copy.wait_recv()
    for r in (-1, 16):
        first_sweep(r)
    for r in (-1, 0, 15, 16):
        second_sweep(r)
    for i in (0, 7):
        coarse_row(i)
    each(2, restrict_rim, 2)

    send_terms(1)

    @pl.when(not_last)
    def _():
        v_parts[2].start()


    c2_up = remote(c2.at[pl.ds(8, 1)], c2.at[pl.ds(0, 1)], h_send.at[0], h_recv.at[0], tm, right)
    c2_down = remote(c2.at[pl.ds(1, 1)], c2.at[pl.ds(9, 1)], h_send.at[1], h_recv.at[1], tm, left)
    c2_up.start()
    c2_down.start()
    v1_out = pltpu.make_async_copy(v1.at[pl.ds(2, 16)], vv_hbm.at[1], out_sem.at[0])
    v2_out = pltpu.make_async_copy(v2.at[pl.ds(1, 16)], vv_hbm.at[2], out_sem.at[1])
    u0_out = pltpu.make_async_copy(ub.at[0, pl.ds(3, 16)], vv_hbm.at[0], out_sem.at[2])
    p_next = [
        remote(c2.at[pl.ds(k, 1)], c2p.at[pl.ds(k, 1)], p_send.at[n], p_recv.at[n], tm + 1, sp) for n, k in enumerate((0, 9))
    ]
    v1_out.start()
    v2_out.start()

    @pl.when(is_first)
    def _():
        u0_out.start()

    start_hop(1)
    start_relay(0)
    wait_terms(0)
    wait_terms(1)

    def late_parts():
        for copy in v_parts[3:]:
            copy.start()

    @pl.when(not_last & (tm != GROUP - 1))
    def _():
        late_parts()

    @pl.when(tm == GROUP - 1)
    def _():
        relay_in[1].start()

    c2_up.wait_recv()
    c2_down.wait_recv()

    @pl.when(not_last)
    def _():
        for copy in p_next:
            copy.start()

    @pl.when(jnp.logical_not(first_team))
    def _():
        start_hop(2)

    for piece in (0, 2):
        remote(wpack, wx.at[piece], w_send.at[piece], w_recv.at[piece], tm, left).wait_recv()

    @pl.when(not_first)
    def _():
        remote(wpack, wx.at[1], w_send.at[1], w_recv.at[1], tm, left).wait_recv()

    for piece in range(3):
        for r in range(8):
            block, k = PLACE[r]
            w0[8 * piece + r] = get_row(wx.at[piece, block], k)

    last_m = GROUP - 1

    def go_home(m, go, here):
        owner = team + m

        @pl.when(m != spot)
        def _():
            go(remote(res.at[m], home.at[spot], r_send.at[m], r_recv.at[spot], owner, sp))

        @pl.when(m == spot)
        def _():
            here()

    end_copies = [
        remote(res.at[last_m, 2, 8], edges.at[0, spot], g_send.at[0], g_recv.at[spot, 0], team + last_m, right),
        remote(res.at[last_m, 2, 1], edges.at[1, spot], g_send.at[1], g_recv.at[spot, 1], team + last_m, left),
    ]

    def sweep(m):
        def term(field, k):
            block, place = PLACE[k % 8]
            return get_row(rx.at[block, m, k // 8, field], place)

        def keep(field, k, value):
            if 7 <= k < 17:
                res[m, field, k - 7] = value[:, :128]

        for k in range(7, 17):
            keep(0, k, w0[k])
        for k in range(1, 23):
            value = w0[k] + half_step * ring_rate(w0[k - 1], w0[k], w0[k + 1]) + term(0, k)
            w1[k] = value
            keep(1, k, value)
        for k in range(2, 22):
            value = w1[k] + half_step * ring_rate(w1[k - 1], w1[k], w1[k + 1]) + term(1, k)
            w0[k] = value
            keep(2, k, value)

        def here():
            home[spot] = res[m]

        go_home(m, lambda copy: copy.start(), here)

    each(GROUP, sweep)
    for copy in end_copies:
        copy.start()

    group_sends = [
        remote(wpack, wx.at[piece], w_send.at[piece], w_recv.at[piece], tm + GROUP, s) for s, piece in sides
    ]

    @pl.when(first_team)
    def _():
        rows = [split_tiles(w0[k]) for k in range(8, 16)]
        for block in range(2):
            put_block(wpack.at[block], [rows[r][0] for r in BLOCKS[block]], [rows[r][1] for r in BLOCKS[block]], lane)
        for copy in group_sends:
            copy.start()

    @pl.when(tm == GROUP - 1)
    def _():
        for copy in group_sends:
            copy.wait_send()
        v_parts[4].start()

    @pl.when(first_team)
    def _():
        start_hop(2)


    def wait_home(t):
        @pl.when(t != spot)
        def _():
            remote(res.at[0], home.at[t], r_send.at[0], r_recv.at[t], tm, left).wait_recv()

    def vin_out(n):
        rows = pl.ds(*ROWS[n])
        return pltpu.make_async_copy(vin.at[rows], vv_hbm.at[0, rows], out_sem.at[5 + n])

    def take_parts(which):
        for n in which:
            v_parts[n].wait_recv()
            vin_out(n).start()
        for n in which:
            first, count = ROWS[n]
            for i in range(first // 2, (first + count) // 2):
                c2p[i + 1] = restrict_row(vin[2 * i] + vin[2 * i + 1], staging.at[i % 6])

    start_relay(1)

    @pl.when(not_first)
    def _():
        take_parts((0, 2))
        take_parts((1, 3, 4))

    each(GROUP, wait_home)

    for t in range(GROUP):
        columns = pl.ds(128 * t, 128)
        dd[1, :, :, columns] = home[t, 1] - c1[:, :, columns]
        dd[2, :, :, columns] = home[t, 2] - c2[:, :, columns]

    @pl.when(spot == last_m)
    def _():
        for t in range(GROUP):
            columns = pl.ds(128 * t, 128)
            for side in range(2):
                remote(res.at[0, 2, 8], edges.at[side, t], g_send.at[side], g_recv.at[t, side], tm, left).wait_recv()
                dd[2, 9 * side, :, columns] = edges[side, t] - c2[9 * side, :, columns]

    d_out = [
        pltpu.make_async_copy(dd.at[pl.ds(1, 2)], d_hbm.at[pl.ds(1, 2)], out_sem.at[3]),
        pltpu.make_async_copy(dd.at[pl.ds(0, 1)], d_hbm.at[pl.ds(0, 1)], out_sem.at[4]),
    ]
    d_out[0].start()

    @pl.when(is_first)
    def _():
        dd[0] = jnp.zeros(dd.shape[1:], F32)

    @pl.when(not_first)
    def _():
        for copy in p_next:
            copy.wait_recv()
        for t in range(GROUP):
            columns = pl.ds(128 * t, 128)
            dd[0, :, :, columns] = home[t, 0] - c2p[:, :, columns]

    d_out[1].start()

    for copy in (*u_copies, *rim_copies, c2_up, c2_down):
        copy.wait_send()
    for block in range(2):
        terms_copies(block, lambda copy: copy.wait_send())
    each(GROUP, lambda m: go_home(m, lambda copy: copy.wait_send(), lambda: None))
    for copy in end_copies:
        copy.wait_send()

    @pl.when(is_first)
    def _():
        for piece in range(3):
            start_copies(piece, lambda copy: copy.wait_send())
        u0_out.wait()

    @pl.when(tm < GROUP - 1)
    def _():
        for copy in group_sends:
            copy.wait_send()

    @pl.when(not_last)
    def _():
        for copy in p_next:
            copy.wait_send()
        for n in (0, 2, 4):
            v_parts[n].wait_send()

    @pl.when(not_last & (tm != GROUP - 1))
    def _():
        v_parts[3].wait_send()

    @pl.when(tm == GROUP - 1)
    def _():
        for copy in relay_in:
            copy.wait_send()

    @pl.when(is_first)
    def _():
        for copy in relay_out:
            copy.wait_send()

    for n in range(3):

        @pl.when(goes[n])
        def _():
            hops[n].wait_send()

    @pl.when(not_first)
    def _():
        for n in range(5):
            vin_out(n).wait()

    v1_out.wait()
    v2_out.wait()
    for copy in d_out:
        copy.wait()


def correct_kernel(vv_hbm, d_ref, o_hbm, vb, refined, in_sem, out_sem):
    sub, lane = iotas()
    lanes = vb.shape[-1]
    half = lanes // 256
    up_index = (sub // 4) * 4 + (sub + 1) % 4
    down_index = (sub // 4) * 4 + (sub + 3) % 4

    def load(m):
        return pltpu.make_async_copy(vv_hbm.at[m], vb.at[m], in_sem.at[m])

    def store(m, r):
        return pltpu.make_async_copy(vb.at[m, r], o_hbm.at[0, m, :, r, :], out_sem.at[m, r])

    for m in range(3):
        load(m).start()

    def spread(m, k):
        tiles = split_tiles(d_ref[m, k])
        before, after = lane_neighbours(tiles, lane)
        for t in range(half):
            i, index = t // 2, (t % 2) * 64 + lane // 2
            low = 0.75 * tiles[i] + 0.25 * before[i]
            high = 0.75 * tiles[i] + 0.25 * after[i]
            fine = jnp.where(lane % 2 == 0, take(low, index, 1), take(high, index, 1))
            near_part, far_part = 0.75 * fine, 0.25 * fine
            refined.at[k][pl.ds(16 * t, 8, stride=2), :] = near_part + take(far_part, down_index, 0)
            refined.at[k][pl.ds(16 * t + 1, 8, stride=2), :] = near_part + take(far_part, up_index, 0)

    def refined_row(k):
        return jnp.concatenate(
            [refined[k, pl.ds(16 * t + 8 * h, 8), :] for h in range(2) for t in range(half)], axis=1
        )

    def node(m):
        each(10, lambda k: spread(m, k), 5)
        load(m).wait()

        def rows(k):
            own = 0.75 * refined_row(k + 1)
            vb[m, 2 * k] = vb[m, 2 * k] + (own + 0.25 * refined_row(k))
            vb[m, 2 * k + 1] = vb[m, 2 * k + 1] + (own + 0.25 * refined_row(k + 2))
            store(m, 2 * k).start()
            store(m, 2 * k + 1).start()

        each(8, rows, 4)

    each(3, node)

    def drain(k):
        for m in range(3):
            store(m, k).wait()

    each(16, drain)


def on_device(node_values):
    _, _, depth, rows, lanes = node_values.shape
    half = lanes // 4
    fine = lambda n: pltpu.VMEM((n, 8, lanes), F32)
    coarse = lambda n: pltpu.VMEM((n, 8, half), F32)
    tiles = lambda *n: pltpu.VMEM(n + (8, 128), F32)
    dma = lambda *n: pltpu.SemaphoreType.DMA(n)
    anywhere = pl.BlockSpec(memory_space=pl.ANY)
    vv, dd = pl.pallas_call(
        main_kernel,
        name="sweeps",
        out_shape=(
            jax.ShapeDtypeStruct((3, rows, depth, lanes), F32),
            jax.ShapeDtypeStruct((3, 10, 8, half), F32),
        ),
        in_specs=[anywhere],
        out_specs=(anywhere, anywhere),
        scratch_shapes=[
            pltpu.VMEM((3, 22, 8, lanes), F32), fine(22), fine(20), fine(20), fine(20), fine(20), fine(20), fine(20), fine(18), fine(16), pltpu.VMEM((2, ROWS[1][1], 8, lanes), F32), pltpu.VMEM((2, ROWS[1][1], 8, lanes), F32),
            coarse(10), coarse(10), coarse(10), coarse(10), coarse(12), coarse(10),
            tiles(2, GROUP, 2, 5), tiles(GROUP, 2, 5), tiles(2, 5), tiles(2, GROUP, 3, 2, 5), tiles(3, 2, 5),
            pltpu.VMEM((24, 8, 256), F32), pltpu.VMEM((24, 8, 256), F32), tiles(GROUP, 3, 10), tiles(GROUP, 3, 10), tiles(2, GROUP),
            pltpu.VMEM((3, 10, 8, half), F32), pltpu.VMEM((6, lanes // 16, 128), F32),
            dma(3, 16), dma(2), dma(2), dma(2, 4), dma(2, 4), dma(2), dma(2), dma(2, GROUP, 3), dma(2, GROUP, 3), dma(GROUP, 3), dma(3), dma(3),
            dma(GROUP), dma(GROUP), dma(2), dma(GROUP, 2), dma(5), dma(5), dma(3), dma(2), dma(4), dma(2), dma(2), dma(2), dma(10),
        ],
        compiler_params=pltpu.CompilerParams(
            collective_id=0, has_side_effects=True, vmem_limit_bytes=48 * 1024 * 1024
        ),
    )(node_values)
    return pl.pallas_call(
        correct_kernel,
        name="correct",
        out_shape=jax.ShapeDtypeStruct(node_values.shape, F32),
        in_specs=[anywhere, pl.BlockSpec(memory_space=pltpu.VMEM)],
        out_specs=anywhere,
        scratch_shapes=[
            pltpu.VMEM((3, rows, 8, lanes), F32), pltpu.VMEM((10, lanes // 16, 128), F32),
            dma(3), dma(3, 16),
        ],
        compiler_params=pltpu.CompilerParams(vmem_limit_bytes=48 * 1024 * 1024),
    )(vv, dd)


def solution(mesh):
    return jax.shard_map(
        on_device,
        mesh=mesh,
        in_specs=(P("tm", None, None, "space", None),),
        out_specs=P("tm", None, None, "space", None),
        check_vma=False,
    )
```

```python
import functools

import jax
import jax.numpy as jnp
from jax import lax
from jax.experimental import pallas as pl
from jax.experimental.pallas import tpu as pltpu
from jax.sharding import PartitionSpec as P

STEP = 0.25
WEIGHTS = ((5.0 / 24.0, 1.0 / 3.0, -1.0 / 24.0), (-1.0 / 24.0, 1.0 / 3.0, 5.0 / 24.0))
MESH = pl.DeviceIdType.MESH
GROUP = 4
ROWS = ((2, 2), (4, 4), (8, 4), (12, 4), (0, 2))
BLOCKS = ((2, 3, 4, 5), (0, 1, 6, 7))
PLACE = {r: (b, k) for b, rows in enumerate(BLOCKS) for k, r in enumerate(rows)}
F32 = jnp.float32


def neighbour_sum(above, center, below):
    lanes = center.shape[-1]
    beside = above + below + pltpu.roll(center, 1, 0) + pltpu.roll(center, 7, 0)
    return beside + pltpu.roll(center, 1, 1) + pltpu.roll(center, lanes - 1, 1)


def cube(value):
    return value * value * value


def combine(weights, terms):
    total = weights[0] * terms[0]
    for weight, term in zip(weights[1:], terms[1:]):
        total = total + weight * term
    return total


def each(count, body, unroll=1):
    def step(k, carry):
        body(k)
        return carry

    lax.fori_loop(0, count, step, 0, unroll=unroll)


def iotas():
    sub = lax.broadcasted_iota(jnp.int32, (8, 128), 0)
    lane = lax.broadcasted_iota(jnp.int32, (8, 128), 1)
    return sub, lane


def take(value, index, axis):
    return jnp.take_along_axis(value, index, axis=axis, mode="promise_in_bounds")


def split_tiles(value):
    return [value[:, 128 * t : 128 * (t + 1)] for t in range(value.shape[1] // 128)]


def lane_neighbours(tiles, lane):
    count = len(tiles)
    right_rolled = [pltpu.roll(t, 1, 1) for t in tiles]
    left_rolled = [pltpu.roll(t, 127, 1) for t in tiles]
    before = [pltpu.roll(right_rolled[-1], 4, 0)] + right_rolled[:-1]
    after = left_rolled[1:] + [pltpu.roll(left_rolled[0], 4, 0)]
    left = [jnp.where(lane == 0, before[i], right_rolled[i]) for i in range(count)]
    right = [jnp.where(lane == 127, after[i], left_rolled[i]) for i in range(count)]
    return left, right


def coarse_rate(above, center, below):
    sub, lane = iotas()
    up_index = (sub // 4) * 4 + (sub + 1) % 4
    down_index = (sub // 4) * 4 + (sub + 3) % 4
    a, c, b = split_tiles(above), split_tiles(center), split_tiles(below)
    left, right = lane_neighbours(c, lane)
    out = []
    for i in range(len(c)):
        beside = a[i] + b[i] + take(c[i], up_index, 0) + take(c[i], down_index, 0) + left[i] + right[i]
        out.append(0.25 * beside + c[i] * (0.5 - 2.0 * (c[i] * c[i])))
    return jnp.concatenate(out, axis=1)


def ring_rate(above, center, below):
    sub, _ = iotas()
    up_index = (sub // 4) * 4 + (sub + 1) % 4
    down_index = (sub // 4) * 4 + (sub + 3) % 4
    beside = above + below + pltpu.roll(center, 1, 1) + pltpu.roll(center, 255, 1)
    depth = [take(t, up_index, 0) + take(t, down_index, 0) for t in split_tiles(center)]
    beside = beside + jnp.concatenate(depth, axis=1)
    return 0.25 * beside + center * (0.5 - 2.0 * (center * center))


def strip_of(tiles, t, lane):
    after = tiles[t + 1] if t + 1 < len(tiles) else pltpu.roll(tiles[0], 4, 0)
    before = tiles[t - 1] if t > 0 else pltpu.roll(tiles[-1], 4, 0)
    return jnp.where(lane < 64, after, before)


def join_strips(strips, lane):
    block = ((lane + 16) // 32) % 4
    joined = strips[0]
    for k in range(1, 4):
        joined = jnp.where(block == k, pltpu.roll(strips[k], 32 * k, 1), joined)
    return joined


def put_block(ref, rows, strips, lane):
    ref[0] = join_strips(strips, lane)
    for k in range(4):
        ref[k + 1] = rows[k]


def get_row(ref, k):
    strip = pltpu.roll(ref[0], (128 - 32 * k) % 128, 1)
    return jnp.concatenate([ref[k + 1], strip], axis=1)


def packed_halves(row, staging):
    tiles = split_tiles(row)
    half = len(tiles) // 2
    for t in range(half):
        staging[pl.ds(16 * t, 8), :] = tiles[t]
        staging[pl.ds(16 * t + 8, 8), :] = tiles[t + half]
    even = [staging[pl.ds(16 * t, 8, stride=2), :] for t in range(half)]
    odd = [staging[pl.ds(16 * t + 1, 8, stride=2), :] for t in range(half)]
    return even, odd


def decimate_index(lane):
    return jnp.where(lane < 64, 2 * lane, 2 * lane - 127)


def lane_pairs(packed, lane):
    out = []
    for t in range(len(packed) // 2):
        p, q = packed[2 * t], packed[2 * t + 1]
        mixed = jnp.where(lane % 2 == 0, p + pltpu.roll(p, 127, 1), q + pltpu.roll(q, 1, 1))
        out.append(take(mixed, decimate_index(lane), 1))
    return out


def lane_even_odd(packed, lane):
    even, odd = [], []
    for t in range(len(packed) // 2):
        p, q = packed[2 * t], packed[2 * t + 1]
        even.append(take(jnp.where(lane % 2 == 0, p, pltpu.roll(q, 1, 1)), decimate_index(lane), 1))
        odd.append(take(jnp.where(lane % 2 == 0, pltpu.roll(p, 127, 1), q), decimate_index(lane), 1))
    return even, odd


def restrict_row(pair_sum, staging):
    _, lane = iotas()
    even, odd = packed_halves(pair_sum, staging)
    sums = lane_pairs([a + b for a, b in zip(even, odd)], lane)
    return jnp.concatenate([0.125 * v for v in sums], axis=1)


def coarse_terms(fields, staging):
    sub, lane = iotas()
    up_index = (sub // 4) * 4 + (sub + 1) % 4
    down_index = (sub // 4) * 4 + (sub + 3) % 4
    nodes, inner, evens, odds = [], [], [], []
    for n, (before, a, b, after) in enumerate(fields):
        total = a + b
        rest = (before + after) - total - 2.0 * (cube(a) + cube(b))
        even, odd = packed_halves(total, staging.at[2 * n])
        rest_even, rest_odd = packed_halves(rest, staging.at[2 * n + 1])
        count = len(even)
        inner.append(
            [
                rest_even[t] + rest_odd[t] + take(odd[t], down_index, 0) + take(even[t], up_index, 0)
                for t in range(count)
            ]
        )
        lane_even, lane_odd = lane_even_odd([even[t] + odd[t] for t in range(count)], lane)
        evens.append(lane_even)
        odds.append(lane_odd)
        nodes.append(jnp.concatenate([0.125 * (p + q) for p, q in zip(lane_even, lane_odd)], axis=1))
    sums = []
    for weights in WEIGHTS:
        weights = [0.125 * STEP * w for w in weights]
        body = lane_pairs([combine(weights, v) for v in zip(*inner)], lane)
        left, _ = lane_neighbours([combine(weights, v) for v in zip(*odds)], lane)
        _, right = lane_neighbours([combine(weights, v) for v in zip(*evens)], lane)
        sums.append(jnp.concatenate([b + l + r for b, l, r in zip(body, left, right)], axis=1))
    return nodes, sums


def main_kernel(
    u_hbm, vv_hbm, d_hbm,
    ub, bb, p0, kk, q1, v1, mm, p2, v2, vin, around, relay, c0, c1, c2, c2p, a0, a1, pack, cpack, wpack, rx, wx, w0, w1, res, home, edges, meter, dd, staging,
    load_sem, u_send, u_recv, e_send, e_recv, h_send, h_recv, a_send, a_recv, w_send, w_recv, r_send, r_recv, g_send, g_recv, v_send, v_recv, o_send, o_recv, q_send, q_recv,
    p_send, p_recv, out_sem,
):
    tm, sp = lax.axis_index("tm"), lax.axis_index("space")
    n_tm, n_sp = lax.axis_size("tm"), lax.axis_size("space")
    left, right = lax.rem(sp + n_sp - 1, n_sp), lax.rem(sp + 1, n_sp)
    not_first, not_last = tm > 0, tm < n_tm - 1
    half_step = 0.5 * STEP
    team = GROUP * (tm // GROUP)
    spot = tm - team
    first_team = tm < GROUP
    sides = ((left, 2), (sp, 1), (right, 0))

    def load(m, r):
        return u_hbm.at[0, m, :, r, :], ub.at[m, r + 3]

    def remote(src, dst, send, recv, t, s):
        return pltpu.make_async_remote_copy(
            src_ref=src, dst_ref=dst, send_sem=send, recv_sem=recv, device_id=(t, s), device_id_type=MESH
        )

    def all_tiles(count, sem):
        return remote(meter.at[pl.ds(0, count)], meter.at[pl.ds(0, count)], sem, sem, tm, left)

    def edge_row(k):
        return jnp.where(k < 3, k, k + 10)

    def load_edges(k):
        for m in range(3):
            pltpu.make_async_copy(*load(m, edge_row(k)), load_sem.at[0]).start()

    def load_inner(k):
        for m in range(3):
            pltpu.make_async_copy(*load(m, k + 3), load_sem.at[1]).start()

    each(6, load_edges)
    each(10, load_inner)

    barrier = pltpu.get_barrier_semaphore()
    for d in range(GROUP):
        mate = team + lax.rem(spot + d, GROUP)
        for s, _ in sides:
            if d > 0 or s is not sp:
                pl.semaphore_signal(barrier, inc=1, device_id=(mate, s), device_id_type=MESH)

    @pl.when(jnp.logical_not(first_team))
    def _():
        for s, _ in sides:
            pl.semaphore_signal(barrier, inc=1, device_id=(tm - GROUP, s), device_id_type=MESH)

    @pl.when(tm == GROUP)
    def _():
        pl.semaphore_signal(barrier, inc=1, device_id=(tm - 1, sp), device_id_type=MESH)

    @pl.when(tm < GROUP - 1)
    def _():
        pl.semaphore_wait(barrier, 3 * GROUP + 2)

    @pl.when(tm == GROUP - 1)
    def _():
        pl.semaphore_wait(barrier, 3 * GROUP + 3)

    @pl.when(jnp.logical_not(first_team))
    def _():
        pl.semaphore_wait(barrier, 3 * GROUP - 1)

    def wait_rows(count, sem):
        rows = ub.at[:, pl.ds(3, count)]
        pltpu.make_async_copy(rows, rows, sem).wait()

    wait_rows(6, load_sem.at[0])
    u_copies = [
        remote(ub.at[:, pl.ds(18, 1)], ub.at[:, pl.ds(2, 1)], u_send.at[0], u_recv.at[0], tm, right),
        remote(ub.at[:, pl.ds(3, 1)], ub.at[:, pl.ds(19, 1)], u_send.at[0], u_recv.at[0], tm, left),
    ]
    for copy in u_copies:
        copy.start()

    weights = [STEP * w for w in WEIGHTS[0]]
    later_weights = [STEP * w for w in WEIGHTS[1]]
    later_weights[1] = later_weights[1] - half_step

    def local_terms(r):
        nodes = [ub[m, r + 3] for m in range(3)]
        cubes = [cube(v) for v in nodes]
        mixed = combine(weights, nodes)
        bb[r + 3] = mixed
        p0[r + 2] = nodes[0] - 4.0 * mixed + combine([-2.0 * w for w in weights], cubes)
        kk[r + 2] = combine(later_weights, nodes)
        q1[r + 2] = combine([-2.0 * w for w in later_weights], cubes)

    def first_sweep(r):
        value = p0[r + 2] + neighbour_sum(bb[r + 2], bb[r + 3], bb[r + 4])
        mixed = half_step * value + kk[r + 2]
        v1[r + 2] = value
        mm[r + 2] = mixed
        p2[r + 2] = value + q1[r + 2] - 4.0 * mixed - STEP * cube(value)

    def second_sweep(r):
        v2[r + 1] = p2[r + 2] + neighbour_sum(mm[r + 1], mm[r + 2], mm[r + 3])

    def restrict_rim(k):
        i = 9 * k - 1
        c1[i + 1] = restrict_row(v1[2 * i + 2] + v1[2 * i + 3], staging.at[k])

    def coarse_row(i):
        r = 2 * i
        fields = [
            [ub[0, r + k] for k in range(2, 6)],
            [v1[r + k] for k in range(1, 5)],
            [v2[r + k] for k in range(4)],
        ]
        (_, c1[i + 1], c2[i + 1]), (a0[i + 2], a1[i + 1]) = coarse_terms(fields, staging)

    _, lane = iotas()
    is_first = jnp.logical_not(not_first)

    def pack_rows(rows, place):
        tiles = [split_tiles(row) for row in rows]
        for t in range(GROUP):
            put_block(place(t), [v[t] for v in tiles], [strip_of(v, t, lane) for v in tiles], lane)

    def start_copies(piece, go):
        for d in range(GROUP):
            keeper = lax.rem(spot + d, GROUP)
            for s, p in sides:
                if p == piece and (d > 0 or p != 1):
                    copy = remote(
                        cpack.at[keeper], wx.at[p], a_send.at[1], w_recv.at[0], team + keeper, s
                    )
                    go(copy)

    def terms_copy(block, fields, keeper, slot, m, piece, s):
        return remote(
            pack.at[block, keeper, pl.ds(0, fields)], rx.at[block, m, piece, pl.ds(0, fields)],
            a_send.at[block], a_recv.at[block], team + keeper, s,
        )

    def sized(block, m, go):
        if block == 0:
            pl.when(m < 2)(lambda: go(2))
            pl.when(m == 2)(lambda: go(1))
        else:
            pl.when(m < 3)(lambda: go(2))
            pl.when(m == 3)(lambda: go(1))

    def terms_copies(block, go):
        def mate(d):
            keeper = lax.rem(spot + d, GROUP)

            @pl.when(d > 0)
            def _():
                go(terms_copy(block, 2, keeper, d, spot, 1, sp))

            def beside(fields):
                go(terms_copy(block, fields, keeper, d, spot, 2, left))
                go(terms_copy(block, fields, keeper, d, spot, 0, right))

            sized(block, spot, beside)

        each(GROUP, mate)

    def fields_beside(block, m):
        return jnp.where(m < 2 + block, 2, jnp.where(m == 2 + block, 1, 0))

    def wait_terms(block):
        all_tiles(10 * (GROUP - 1) + 10 * (5 + 2 * block), a_recv.at[block]).wait_recv()

    def send_terms(block):
        for k in BLOCKS[block]:
            a0[k + 2] = a0[k + 2] - half_step * coarse_rate(c0[k], c0[k + 1], c0[k + 2])
            a1[k + 1] = a1[k + 1] - half_step * coarse_rate(c1[k], c1[k + 1], c1[k + 2])
        pack_rows([a0[k + 2] for k in BLOCKS[block]], lambda t: pack.at[block, t, 0])
        pack_rows([a1[k + 1] for k in BLOCKS[block]], lambda t: pack.at[block, t, 1])
        terms_copies(block, lambda copy: copy.start())
        rx[block, spot, 1] = pack[block, spot]

    def restrict_first(i):
        c0[i + 1] = restrict_row(ub[0, 2 * i + 3] + ub[0, 2 * i + 4], staging.at[i % 4])

    each(6, lambda k: local_terms(edge_row(k)), 3)
    for k in (0, 7):
        restrict_first(k)
    for r in (1, 14):
        first_sweep(r)
    rim_copies, rows_of = [], (16, 16, 16, 8)
    for n, (field, offset, up, down) in enumerate(((bb, 3, 14, 1), (v1, 2, 14, 1), (mm, 2, 14, 1), (c0, 1, 7, 0))):
        up_target, down_target = up + offset - rows_of[n], down + offset + rows_of[n]
        rim_copies += [
            remote(field.at[pl.ds(up + offset, 1)], field.at[pl.ds(up_target, 1)], e_send.at[0], e_recv.at[0], tm, right),
            remote(field.at[pl.ds(down + offset, 1)], field.at[pl.ds(down_target, 1)], e_send.at[0], e_recv.at[0], tm, left),
        ]
    for copy in rim_copies:
        copy.start()
    wait_rows(10, load_sem.at[1])
    for k in range(1, 7):
        restrict_first(k)

    @pl.when(is_first)
    def _():
        for block in range(2):
            pack_rows([c0[k + 1] for k in BLOCKS[block]], lambda t: cpack.at[t, block])
        for piece in range(3):
            start_copies(piece, lambda copy: copy.start())
        wx[1] = cpack[0]

    each(10, lambda k: local_terms(k + 3), 5)
    each(12, lambda k: first_sweep(k + 2), 6)
    each(12, lambda k: second_sweep(k + 2), 6)

    def v_part(index, start, count):
        return remote(
            v2.at[pl.ds(start + 1, count)], vin.at[pl.ds(start, count)], v_send.at[index], v_recv.at[index], tm + 1, sp
        )

    v_parts = [v_part(n, *rows) for n, rows in enumerate(ROWS)]
    behind = team + lax.rem(spot + GROUP - 1, GROUP)
    start, count = ROWS[1]
    hops = [
        remote(v2.at[pl.ds(start + 1, count)], around.at[0], o_send.at[0], o_recv.at[0], behind, sp),
        remote(around.at[0], around.at[1], o_send.at[1], o_recv.at[1], behind, sp),
        remote(around.at[1], vin.at[pl.ds(start, count)], o_send.at[2], v_recv.at[1], behind, sp),
    ]
    goes = [spot != GROUP - 1, spot != GROUP - 2, spot != GROUP - 3]

    def start_hop(n):
        @pl.when(goes[n])
        def _():
            if n > 0:
                hops[n - 1].wait_recv()
            hops[n].start()

    @pl.when(not_last)
    def _():
        v_parts[0].start()

    start_hop(0)

    relay_in, relay_out = [], []
    for k, n in enumerate((1, 3)):
        first, count = ROWS[n]
        held = relay.at[k]
        relay_in.append(remote(v2.at[pl.ds(first + 1, count)], held, q_send.at[k], q_recv.at[k], team, sp))
        relay_out.append(remote(held, vin.at[pl.ds(first, count)], q_send.at[2 + k], v_recv.at[n], tm + GROUP, sp))

    def start_relay(k):
        @pl.when(is_first)
        def _():
            relay_in[k].wait_recv()
            relay_out[k].start()

    @pl.when(tm == GROUP - 1)
    def _():
        relay_in[0].start()

    each(4, lambda k: coarse_row(k + 2), 2)
    for n, i in enumerate((1, 6)):
        c1[i + 1] = restrict_row(v1[2 * i + 2] + v1[2 * i + 3], staging.at[n])
    send_terms(0)

    all_tiles(6 * 16, u_recv.at[0]).wait_recv()
    for r in (-1, 16):
        local_terms(r)
    for r in (0, 15):
        first_sweep(r)
    for r in (1, 14):
        second_sweep(r)
    for i in (1, 6):
        coarse_row(i)
    all_tiles(2 * (3 * 16 + 4), e_recv.at[0]).wait_recv()
    for r in (-1, 16):
        first_sweep(r)
    for r in (-1, 0, 15, 16):
        second_sweep(r)
    for i in (0, 7):
        coarse_row(i)
    each(2, restrict_rim, 2)


    @pl.when(is_first)
    def _():
        all_tiles(10 * (3 * GROUP - 1), a_send.at[1]).wait_send()

    send_terms(1)

    @pl.when(not_last)
    def _():
        v_parts[2].start()


    c2_up = remote(c2.at[pl.ds(8, 1)], c2.at[pl.ds(0, 1)], h_send.at[0], h_recv.at[0], tm, right)
    c2_down = remote(c2.at[pl.ds(1, 1)], c2.at[pl.ds(9, 1)], h_send.at[0], h_recv.at[0], tm, left)
    c2_up.start()
    c2_down.start()
    v1_out = pltpu.make_async_copy(v1.at[pl.ds(2, 16)], vv_hbm.at[1], out_sem.at[0])
    v2_out = pltpu.make_async_copy(v2.at[pl.ds(1, 16)], vv_hbm.at[2], out_sem.at[1])
    u0_out = pltpu.make_async_copy(ub.at[0, pl.ds(3, 16)], vv_hbm.at[0], out_sem.at[2])
    p_next = [
        remote(c2.at[pl.ds(k, 1)], c2p.at[pl.ds(k, 1)], p_send.at[0], p_recv.at[0], tm + 1, sp) for n, k in enumerate((0, 9))
    ]
    v1_out.start()
    v2_out.start()

    @pl.when(is_first)
    def _():
        u0_out.start()

    start_hop(1)
    start_relay(0)
    wait_terms(0)
    wait_terms(1)

    def late_parts():
        for copy in v_parts[3:]:
            copy.start()

    @pl.when(not_last & (tm != GROUP - 1))
    def _():
        late_parts()

    @pl.when(tm == GROUP - 1)
    def _():
        relay_in[1].start()

    all_tiles(2 * 4, h_recv.at[0]).wait_recv()

    @pl.when(not_last)
    def _():
        for copy in p_next:
            copy.start()

    @pl.when(jnp.logical_not(first_team))
    def _():
        start_hop(2)

    @pl.when(is_first)
    def _():
        all_tiles(20, w_recv.at[0]).wait_recv()

    @pl.when(not_first)
    def _():
        all_tiles(30, w_recv.at[0]).wait_recv()

    for piece in range(3):
        for r in range(8):
            block, k = PLACE[r]
            w0[8 * piece + r] = get_row(wx.at[piece, block], k)

    last_m = GROUP - 1

    def go_home(m, go, here):
        owner = team + m

        @pl.when(m != spot)
        def _():
            go(remote(res.at[m], home.at[spot], r_send.at[0], r_recv.at[0], owner, sp))

        @pl.when(m == spot)
        def _():
            here()

    end_copies = [
        remote(res.at[last_m, 2, 8], edges.at[0, spot], g_send.at[0], g_recv.at[0], team + last_m, right),
        remote(res.at[last_m, 2, 1], edges.at[1, spot], g_send.at[0], g_recv.at[0], team + last_m, left),
    ]

    def sweep(m):
        def term(field, k):
            block, place = PLACE[k % 8]
            return get_row(rx.at[block, m, k // 8, field], place)

        def keep(field, k, value):
            if 7 <= k < 17:
                res[m, field, k - 7] = value[:, :128]

        for k in range(7, 17):
            keep(0, k, w0[k])
        for k in range(1, 23):
            value = w0[k] + half_step * ring_rate(w0[k - 1], w0[k], w0[k + 1]) + term(0, k)
            w1[k] = value
            keep(1, k, value)
        for k in range(2, 22):
            value = w1[k] + half_step * ring_rate(w1[k - 1], w1[k], w1[k + 1]) + term(1, k)
            w0[k] = value
            keep(2, k, value)

        def here():
            home[spot] = res[m]

        go_home(m, lambda copy: copy.start(), here)

    each(GROUP, sweep)
    for copy in end_copies:
        copy.start()

    group_sends = [
        remote(wpack, wx.at[piece], w_send.at[0], w_recv.at[0], tm + GROUP, s) for s, piece in sides
    ]

    @pl.when(first_team)
    def _():
        rows = [split_tiles(w0[k]) for k in range(8, 16)]
        for block in range(2):
            put_block(wpack.at[block], [rows[r][0] for r in BLOCKS[block]], [rows[r][1] for r in BLOCKS[block]], lane)
        for copy in group_sends:
            copy.start()

    @pl.when(tm == GROUP - 1)
    def _():
        all_tiles(30, w_send.at[0]).wait_send()
        v_parts[4].start()

    @pl.when(first_team)
    def _():
        start_hop(2)


    def vin_out(n):
        rows = pl.ds(*ROWS[n])
        return pltpu.make_async_copy(vin.at[rows], vv_hbm.at[0, rows], out_sem.at[5 + n])

    def take_parts(which):
        for n in which:
            v_parts[n].wait_recv()
            vin_out(n).start()
        for n in which:
            first, count = ROWS[n]
            for i in range(first // 2, (first + count) // 2):
                c2p[i + 1] = restrict_row(vin[2 * i] + vin[2 * i + 1], staging.at[i % 6])

    all_tiles(6 * 16, u_send.at[0]).wait_send()
    all_tiles(2 * (3 * 16 + 4), e_send.at[0]).wait_send()
    all_tiles(2 * 4, h_send.at[0]).wait_send()
    for block in range(2):
        for fields in range(3):
            pl.when(fields_beside(block, spot) == fields)(
                lambda: all_tiles(10 * (GROUP - 1) + 10 * GROUP * fields, a_send.at[block]).wait_send()
            )

    @pl.when(is_first)
    def _():
        u0_out.wait()

    @pl.when(tm < GROUP - 1)
    def _():
        all_tiles(30, w_send.at[0]).wait_send()

    v1_out.wait()
    v2_out.wait()

    start_relay(1)

    @pl.when(not_first)
    def _():
        take_parts((0, 2))
        take_parts((1, 3, 4))

    all_tiles(30 * (GROUP - 1), r_recv.at[0]).wait_recv()

    for t in range(GROUP):
        columns = pl.ds(128 * t, 128)
        dd[1, :, :, columns] = home[t, 1] - c1[:, :, columns]
        dd[2, :, :, columns] = home[t, 2] - c2[:, :, columns]

    @pl.when(spot == last_m)
    def _():
        all_tiles(2 * GROUP, g_recv.at[0]).wait_recv()
        for t in range(GROUP):
            columns = pl.ds(128 * t, 128)
            for side in range(2):
                dd[2, 9 * side, :, columns] = edges[side, t] - c2[9 * side, :, columns]

    d_out = [
        pltpu.make_async_copy(dd.at[pl.ds(1, 2)], d_hbm.at[pl.ds(1, 2)], out_sem.at[3]),
        pltpu.make_async_copy(dd.at[pl.ds(0, 1)], d_hbm.at[pl.ds(0, 1)], out_sem.at[4]),
    ]
    d_out[0].start()

    @pl.when(is_first)
    def _():
        dd[0] = jnp.zeros(dd.shape[1:], F32)

    @pl.when(not_first)
    def _():
        all_tiles(8, p_recv.at[0]).wait_recv()
        for t in range(GROUP):
            columns = pl.ds(128 * t, 128)
            dd[0, :, :, columns] = home[t, 0] - c2p[:, :, columns]

    d_out[1].start()

    all_tiles(30 * (GROUP - 1), r_send.at[0]).wait_send()
    all_tiles(2, g_send.at[0]).wait_send()

    @pl.when(not_last)
    def _():
        all_tiles(8, p_send.at[0]).wait_send()
        for n in (0, 2, 4):
            v_parts[n].wait_send()

    @pl.when(not_last & (tm != GROUP - 1))
    def _():
        v_parts[3].wait_send()

    @pl.when(tm == GROUP - 1)
    def _():
        for copy in relay_in:
            copy.wait_send()

    @pl.when(is_first)
    def _():
        for copy in relay_out:
            copy.wait_send()

    for n in range(3):

        @pl.when(goes[n])
        def _():
            hops[n].wait_send()

    @pl.when(not_first)
    def _():
        for n in range(5):
            vin_out(n).wait()

    for copy in d_out:
        copy.wait()


def correct_kernel(vv_hbm, d_ref, o_hbm, vb, refined, in_sem, out_sem):
    sub, lane = iotas()
    lanes = vb.shape[-1]
    half = lanes // 256
    up_index = (sub // 4) * 4 + (sub + 1) % 4
    down_index = (sub // 4) * 4 + (sub + 3) % 4

    def load(m):
        return pltpu.make_async_copy(vv_hbm.at[m], vb.at[m], in_sem.at[m])

    def store(m, r):
        return pltpu.make_async_copy(vb.at[m, r], o_hbm.at[0, m, :, r, :], out_sem)

    for m in range(3):
        load(m).start()

    def spread(m, k):
        tiles = split_tiles(d_ref[m, k])
        before, after = lane_neighbours(tiles, lane)
        for t in range(half):
            i, index = t // 2, (t % 2) * 64 + lane // 2
            low = 0.75 * tiles[i] + 0.25 * before[i]
            high = 0.75 * tiles[i] + 0.25 * after[i]
            fine = jnp.where(lane % 2 == 0, take(low, index, 1), take(high, index, 1))
            near_part, far_part = 0.75 * fine, 0.25 * fine
            refined.at[k][pl.ds(16 * t, 8, stride=2), :] = near_part + take(far_part, down_index, 0)
            refined.at[k][pl.ds(16 * t + 1, 8, stride=2), :] = near_part + take(far_part, up_index, 0)

    def refined_row(k):
        return jnp.concatenate(
            [refined[k, pl.ds(16 * t + 8 * h, 8), :] for h in range(2) for t in range(half)], axis=1
        )

    def node(m):
        each(10, lambda k: spread(m, k), 5)
        load(m).wait()

        def rows(k):
            own = 0.75 * refined_row(k + 1)
            vb[m, 2 * k] = vb[m, 2 * k] + (own + 0.25 * refined_row(k))
            vb[m, 2 * k + 1] = vb[m, 2 * k + 1] + (own + 0.25 * refined_row(k + 2))
            store(m, 2 * k).start()
            store(m, 2 * k + 1).start()

        each(8, rows, 4)

    each(3, node)

    pltpu.make_async_copy(vb, vb, out_sem).wait()


def on_device(node_values):
    _, _, depth, rows, lanes = node_values.shape
    half = lanes // 4
    fine = lambda n: pltpu.VMEM((n, 8, lanes), F32)
    coarse = lambda n: pltpu.VMEM((n, 8, half), F32)
    tiles = lambda *n: pltpu.VMEM(n + (8, 128), F32)
    dma = lambda *n: pltpu.SemaphoreType.DMA(n)
    anywhere = pl.BlockSpec(memory_space=pl.ANY)
    vv, dd = pl.pallas_call(
        main_kernel,
        name="sweeps",
        out_shape=(
            jax.ShapeDtypeStruct((3, rows, depth, lanes), F32),
            jax.ShapeDtypeStruct((3, 10, 8, half), F32),
        ),
        in_specs=[anywhere],
        out_specs=(anywhere, anywhere),
        scratch_shapes=[
            pltpu.VMEM((3, 22, 8, lanes), F32), fine(22), fine(20), fine(20), fine(20), fine(20), fine(20), fine(20), fine(18), fine(16), pltpu.VMEM((2, ROWS[1][1], 8, lanes), F32), pltpu.VMEM((2, ROWS[1][1], 8, lanes), F32),
            coarse(10), coarse(10), coarse(10), coarse(10), coarse(12), coarse(10),
            tiles(2, GROUP, 2, 5), tiles(GROUP, 2, 5), tiles(2, 5), tiles(2, GROUP, 3, 2, 5), tiles(3, 2, 5),
            pltpu.VMEM((24, 8, 256), F32), pltpu.VMEM((24, 8, 256), F32), tiles(GROUP, 3, 10), tiles(GROUP, 3, 10), tiles(2, GROUP), tiles(110),
            pltpu.VMEM((3, 10, 8, half), F32), pltpu.VMEM((6, lanes // 16, 128), F32),
            dma(2), dma(1), dma(1), dma(1), dma(1), dma(1), dma(1), dma(2), dma(2), dma(1), dma(1), dma(1), dma(1),
            dma(1), dma(1), dma(5), dma(5), dma(3), dma(2), dma(4), dma(2), dma(1), dma(1), dma(10),
        ],
        compiler_params=pltpu.CompilerParams(
            collective_id=0, has_side_effects=True, vmem_limit_bytes=48 * 1024 * 1024
        ),
    )(node_values)
    return pl.pallas_call(
        correct_kernel,
        name="correct",
        out_shape=jax.ShapeDtypeStruct(node_values.shape, F32),
        in_specs=[anywhere, pl.BlockSpec(memory_space=pltpu.VMEM)],
        out_specs=anywhere,
        scratch_shapes=[
            pltpu.VMEM((3, rows, 8, lanes), F32), pltpu.VMEM((10, lanes // 16, 128), F32),
            dma(3), pltpu.SemaphoreType.DMA,
        ],
        compiler_params=pltpu.CompilerParams(vmem_limit_bytes=48 * 1024 * 1024),
    )(vv, dd)


def solution(mesh):
    return jax.shard_map(
        on_device,
        mesh=mesh,
        in_specs=(P("tm", None, None, "space", None),),
        out_specs=P("tm", None, None, "space", None),
        check_vma=False,
    )
```

```python
import functools

import jax
import jax.numpy as jnp
from jax import lax
from jax.experimental import pallas as pl
from jax.experimental.pallas import tpu as pltpu
from jax.sharding import PartitionSpec as P

STEP = 0.25
WEIGHTS = ((5.0 / 24.0, 1.0 / 3.0, -1.0 / 24.0), (-1.0 / 24.0, 1.0 / 3.0, 5.0 / 24.0))
MESH = pl.DeviceIdType.MESH
GROUP = 4
ROWS = ((2, 2), (4, 4), (8, 4), (12, 4), (0, 2))
BLOCKS = ((2, 3, 4, 5), (0, 1, 6, 7))
PLACE = {r: (b, k) for b, rows in enumerate(BLOCKS) for k, r in enumerate(rows)}
F32 = jnp.float32


def neighbour_sum(above, center, below):
    lanes = center.shape[-1]
    beside = above + below + pltpu.roll(center, 1, 0) + pltpu.roll(center, 7, 0)
    return beside + pltpu.roll(center, 1, 1) + pltpu.roll(center, lanes - 1, 1)


def cube(value):
    return value * value * value


def combine(weights, terms):
    total = weights[0] * terms[0]
    for weight, term in zip(weights[1:], terms[1:]):
        total = total + weight * term
    return total


def each(count, body, unroll=1):
    def step(k, carry):
        body(k)
        return carry

    lax.fori_loop(0, count, step, 0, unroll=unroll)


def iotas():
    sub = lax.broadcasted_iota(jnp.int32, (8, 128), 0)
    lane = lax.broadcasted_iota(jnp.int32, (8, 128), 1)
    return sub, lane


def take(value, index, axis):
    return jnp.take_along_axis(value, index, axis=axis, mode="promise_in_bounds")


def split_tiles(value):
    return [value[:, 128 * t : 128 * (t + 1)] for t in range(value.shape[1] // 128)]


def lane_neighbours(tiles, lane):
    count = len(tiles)
    right_rolled = [pltpu.roll(t, 1, 1) for t in tiles]
    left_rolled = [pltpu.roll(t, 127, 1) for t in tiles]
    before = [pltpu.roll(right_rolled[-1], 4, 0)] + right_rolled[:-1]
    after = left_rolled[1:] + [pltpu.roll(left_rolled[0], 4, 0)]
    left = [jnp.where(lane == 0, before[i], right_rolled[i]) for i in range(count)]
    right = [jnp.where(lane == 127, after[i], left_rolled[i]) for i in range(count)]
    return left, right


def coarse_rate(above, center, below):
    sub, lane = iotas()
    up_index = (sub // 4) * 4 + (sub + 1) % 4
    down_index = (sub // 4) * 4 + (sub + 3) % 4
    a, c, b = split_tiles(above), split_tiles(center), split_tiles(below)
    left, right = lane_neighbours(c, lane)
    out = []
    for i in range(len(c)):
        beside = a[i] + b[i] + take(c[i], up_index, 0) + take(c[i], down_index, 0) + left[i] + right[i]
        out.append(0.25 * beside + c[i] * (0.5 - 2.0 * (c[i] * c[i])))
    return jnp.concatenate(out, axis=1)


def ring_rate(above, center, below):
    sub, _ = iotas()
    up_index = (sub // 4) * 4 + (sub + 1) % 4
    down_index = (sub // 4) * 4 + (sub + 3) % 4
    beside = above + below + pltpu.roll(center, 1, 1) + pltpu.roll(center, 255, 1)
    depth = [take(t, up_index, 0) + take(t, down_index, 0) for t in split_tiles(center)]
    beside = beside + jnp.concatenate(depth, axis=1)
    return 0.25 * beside + center * (0.5 - 2.0 * (center * center))


def strip_of(tiles, t, lane):
    after = tiles[t + 1] if t + 1 < len(tiles) else pltpu.roll(tiles[0], 4, 0)
    before = tiles[t - 1] if t > 0 else pltpu.roll(tiles[-1], 4, 0)
    return jnp.where(lane < 64, after, before)


def join_strips(strips, lane):
    block = ((lane + 16) // 32) % 4
    joined = strips[0]
    for k in range(1, 4):
        joined = jnp.where(block == k, pltpu.roll(strips[k], 32 * k, 1), joined)
    return joined


def put_block(ref, rows, strips, lane):
    ref[0] = join_strips(strips, lane)
    for k in range(4):
        ref[k + 1] = rows[k]


def get_row(ref, k):
    strip = pltpu.roll(ref[0], (128 - 32 * k) % 128, 1)
    return jnp.concatenate([ref[k + 1], strip], axis=1)


def packed_halves(row, staging):
    tiles = split_tiles(row)
    half = len(tiles) // 2
    for t in range(half):
        staging[pl.ds(16 * t, 8), :] = tiles[t]
        staging[pl.ds(16 * t + 8, 8), :] = tiles[t + half]
    even = [staging[pl.ds(16 * t, 8, stride=2), :] for t in range(half)]
    odd = [staging[pl.ds(16 * t + 1, 8, stride=2), :] for t in range(half)]
    return even, odd


def decimate_index(lane):
    return jnp.where(lane < 64, 2 * lane, 2 * lane - 127)


def lane_pairs(packed, lane):
    out = []
    for t in range(len(packed) // 2):
        p, q = packed[2 * t], packed[2 * t + 1]
        mixed = jnp.where(lane % 2 == 0, p + pltpu.roll(p, 127, 1), q + pltpu.roll(q, 1, 1))
        out.append(take(mixed, decimate_index(lane), 1))
    return out


def lane_even_odd(packed, lane):
    even, odd = [], []
    for t in range(len(packed) // 2):
        p, q = packed[2 * t], packed[2 * t + 1]
        even.append(take(jnp.where(lane % 2 == 0, p, pltpu.roll(q, 1, 1)), decimate_index(lane), 1))
        odd.append(take(jnp.where(lane % 2 == 0, pltpu.roll(p, 127, 1), q), decimate_index(lane), 1))
    return even, odd


def restrict_row(pair_sum, staging):
    _, lane = iotas()
    even, odd = packed_halves(pair_sum, staging)
    sums = lane_pairs([a + b for a, b in zip(even, odd)], lane)
    return jnp.concatenate([0.125 * v for v in sums], axis=1)


def coarse_terms(fields, staging):
    sub, lane = iotas()
    up_index = (sub // 4) * 4 + (sub + 1) % 4
    down_index = (sub // 4) * 4 + (sub + 3) % 4
    nodes, inner, evens, odds = [], [], [], []
    for n, (before, a, b, after) in enumerate(fields):
        total = a + b
        rest = (before + after) - total - 2.0 * (cube(a) + cube(b))
        even, odd = packed_halves(total, staging.at[2 * n])
        rest_even, rest_odd = packed_halves(rest, staging.at[2 * n + 1])
        count = len(even)
        inner.append(
            [
                rest_even[t] + rest_odd[t] + take(odd[t], down_index, 0) + take(even[t], up_index, 0)
                for t in range(count)
            ]
        )
        lane_even, lane_odd = lane_even_odd([even[t] + odd[t] for t in range(count)], lane)
        evens.append(lane_even)
        odds.append(lane_odd)
        nodes.append(jnp.concatenate([0.125 * (p + q) for p, q in zip(lane_even, lane_odd)], axis=1))
    sums = []
    for weights in WEIGHTS:
        weights = [0.125 * STEP * w for w in weights]
        body = lane_pairs([combine(weights, v) for v in zip(*inner)], lane)
        left, _ = lane_neighbours([combine(weights, v) for v in zip(*odds)], lane)
        _, right = lane_neighbours([combine(weights, v) for v in zip(*evens)], lane)
        sums.append(jnp.concatenate([b + l + r for b, l, r in zip(body, left, right)], axis=1))
    return nodes, sums


def main_kernel(
    u_hbm, vv_hbm, d_hbm,
    ub, bb, p0, kk, q1, v1, mm, p2, v2, vin, around, relay, c0, c1, c2, c2p, a0, a1, pack, cpack, wpack, rx, wx, w0, w1, res, home, edges, meter, dd, staging,
    load_sem, u_send, u_recv, e_send, e_recv, h_send, h_recv, a_send, a_recv, w_send, w_recv, r_send, r_recv, g_send, g_recv, v_send, v_recv, o_send, o_recv, q_send, q_recv,
    p_send, p_recv, out_sem,
):
    tm, sp = lax.axis_index("tm"), lax.axis_index("space")
    n_tm, n_sp = lax.axis_size("tm"), lax.axis_size("space")
    left, right = lax.rem(sp + n_sp - 1, n_sp), lax.rem(sp + 1, n_sp)
    not_first, not_last = tm > 0, tm < n_tm - 1
    half_step = 0.5 * STEP
    team = GROUP * (tm // GROUP)
    spot = tm - team
    first_team = tm < GROUP
    sides = ((left, 2), (sp, 1), (right, 0))

    def load(m, r):
        return u_hbm.at[0, m, :, r, :], ub.at[m, r + 3]

    def remote(src, dst, send, recv, t, s):
        return pltpu.make_async_remote_copy(
            src_ref=src, dst_ref=dst, send_sem=send, recv_sem=recv, device_id=(t, s), device_id_type=MESH
        )

    def all_tiles(count, sem):
        return remote(meter.at[pl.ds(0, count)], meter.at[pl.ds(0, count)], sem, sem, tm, left)

    def edge_row(k):
        return jnp.where(k < 3, k, k + 10)

    def load_edges(k):
        for m in range(3):
            pltpu.make_async_copy(*load(m, edge_row(k)), load_sem.at[0]).start()

    def load_inner(k):
        for m in range(3):
            pltpu.make_async_copy(*load(m, k + 3), load_sem.at[1]).start()

    each(6, load_edges)
    each(10, load_inner)

    barrier = pltpu.get_barrier_semaphore()
    for d in range(GROUP):
        mate = team + lax.rem(spot + d, GROUP)
        for s, _ in sides:
            if d > 0 or s is not sp:
                pl.semaphore_signal(barrier, inc=1, device_id=(mate, s), device_id_type=MESH)

    @pl.when(jnp.logical_not(first_team))
    def _():
        for s, _ in sides:
            pl.semaphore_signal(barrier, inc=1, device_id=(tm - GROUP, s), device_id_type=MESH)

    @pl.when(tm == GROUP)
    def _():
        pl.semaphore_signal(barrier, inc=1, device_id=(tm - 1, sp), device_id_type=MESH)

    @pl.when(tm < GROUP - 1)
    def _():
        pl.semaphore_wait(barrier, 3 * GROUP + 2)

    @pl.when(tm == GROUP - 1)
    def _():
        pl.semaphore_wait(barrier, 3 * GROUP + 3)

    @pl.when(jnp.logical_not(first_team))
    def _():
        pl.semaphore_wait(barrier, 3 * GROUP - 1)

    def wait_rows(count, sem):
        rows = ub.at[:, pl.ds(3, count)]
        pltpu.make_async_copy(rows, rows, sem).wait()

    wait_rows(6, load_sem.at[0])
    u_copies = [
        remote(ub.at[:, pl.ds(18, 1)], ub.at[:, pl.ds(2, 1)], u_send.at[0], u_recv.at[0], tm, right),
        remote(ub.at[:, pl.ds(3, 1)], ub.at[:, pl.ds(19, 1)], u_send.at[0], u_recv.at[0], tm, left),
    ]
    for copy in u_copies:
        copy.start()

    weights = [STEP * w for w in WEIGHTS[0]]
    later_weights = [STEP * w for w in WEIGHTS[1]]
    later_weights[1] = later_weights[1] - half_step

    def local_terms(r):
        nodes = [ub[m, r + 3] for m in range(3)]
        cubes = [cube(v) for v in nodes]
        mixed = combine(weights, nodes)
        bb[r + 3] = mixed
        p0[r + 2] = nodes[0] - 4.0 * mixed + combine([-2.0 * w for w in weights], cubes)
        kk[r + 2] = combine(later_weights, nodes)
        q1[r + 2] = combine([-2.0 * w for w in later_weights], cubes)

    def first_sweep(r):
        value = p0[r + 2] + neighbour_sum(bb[r + 2], bb[r + 3], bb[r + 4])
        mixed = half_step * value + kk[r + 2]
        v1[r + 2] = value
        mm[r + 2] = mixed
        p2[r + 2] = value + q1[r + 2] - 4.0 * mixed - STEP * cube(value)

    def second_sweep(r):
        v2[r + 1] = p2[r + 2] + neighbour_sum(mm[r + 1], mm[r + 2], mm[r + 3])

    def restrict_rim(k):
        i = 9 * k - 1
        c1[i + 1] = restrict_row(v1[2 * i + 2] + v1[2 * i + 3], staging.at[k])

    def coarse_row(i):
        r = 2 * i
        fields = [
            [ub[0, r + k] for k in range(2, 6)],
            [v1[r + k] for k in range(1, 5)],
            [v2[r + k] for k in range(4)],
        ]
        (_, c1[i + 1], c2[i + 1]), (a0[i + 2], a1[i + 1]) = coarse_terms(fields, staging)

    _, lane = iotas()
    is_first = jnp.logical_not(not_first)

    def pack_rows(rows, place):
        tiles = [split_tiles(row) for row in rows]
        for t in range(GROUP):
            put_block(place(t), [v[t] for v in tiles], [strip_of(v, t, lane) for v in tiles], lane)

    def start_copies(piece, go):
        for d in range(GROUP):
            keeper = lax.rem(spot + d, GROUP)
            for s, p in sides:
                if p == piece and (d > 0 or p != 1):
                    copy = remote(
                        cpack.at[keeper], wx.at[p], a_send.at[1], w_recv.at[0], team + keeper, s
                    )
                    go(copy)

    def terms_copy(block, fields, keeper, slot, m, piece, s):
        return remote(
            pack.at[block, keeper, pl.ds(0, fields)], rx.at[block, m, piece, pl.ds(0, fields)],
            a_send.at[block], a_recv.at[block], team + keeper, s,
        )

    def sized(block, m, go):
        if block == 0:
            pl.when(m < 2)(lambda: go(2))
            pl.when(m == 2)(lambda: go(1))
        else:
            pl.when(m < 3)(lambda: go(2))
            pl.when(m == 3)(lambda: go(1))

    def terms_copies(block, go):
        def mate(d):
            keeper = lax.rem(spot + d, GROUP)

            @pl.when(d > 0)
            def _():
                go(terms_copy(block, 2, keeper, d, spot, 1, sp))

            def beside(fields):
                go(terms_copy(block, fields, keeper, d, spot, 2, left))
                go(terms_copy(block, fields, keeper, d, spot, 0, right))

            sized(block, spot, beside)

        each(GROUP, mate)

    def fields_beside(block, m):
        return jnp.where(m < 2 + block, 2, jnp.where(m == 2 + block, 1, 0))

    def wait_terms(block):
        all_tiles(10 * (GROUP - 1) + 10 * (5 + 2 * block), a_recv.at[block]).wait_recv()

    def send_terms(block):
        for k in BLOCKS[block]:
            a0[k + 2] = a0[k + 2] - half_step * coarse_rate(c0[k], c0[k + 1], c0[k + 2])
            a1[k + 1] = a1[k + 1] - half_step * coarse_rate(c1[k], c1[k + 1], c1[k + 2])
        pack_rows([a0[k + 2] for k in BLOCKS[block]], lambda t: pack.at[block, t, 0])
        pack_rows([a1[k + 1] for k in BLOCKS[block]], lambda t: pack.at[block, t, 1])
        terms_copies(block, lambda copy: copy.start())
        rx[block, spot, 1] = pack[block, spot]

    def restrict_first(i):
        c0[i + 1] = restrict_row(ub[0, 2 * i + 3] + ub[0, 2 * i + 4], staging.at[i % 4])

    each(6, lambda k: local_terms(edge_row(k)), 3)
    for k in (0, 7):
        restrict_first(k)
    for r in (1, 14):
        first_sweep(r)
    rim_copies, rows_of = [], (16, 16, 16, 8)
    for n, (field, offset, up, down) in enumerate(((bb, 3, 14, 1), (v1, 2, 14, 1), (mm, 2, 14, 1), (c0, 1, 7, 0))):
        up_target, down_target = up + offset - rows_of[n], down + offset + rows_of[n]
        rim_copies += [
            remote(field.at[pl.ds(up + offset, 1)], field.at[pl.ds(up_target, 1)], e_send.at[0], e_recv.at[0], tm, right),
            remote(field.at[pl.ds(down + offset, 1)], field.at[pl.ds(down_target, 1)], e_send.at[0], e_recv.at[0], tm, left),
        ]
    for copy in rim_copies:
        copy.start()
    wait_rows(10, load_sem.at[1])
    for k in range(1, 7):
        restrict_first(k)

    @pl.when(is_first)
    def _():
        for block in range(2):
            pack_rows([c0[k + 1] for k in BLOCKS[block]], lambda t: cpack.at[t, block])
        for piece in range(3):
            start_copies(piece, lambda copy: copy.start())
        wx[1] = cpack[0]

    each(10, lambda k: local_terms(k + 3), 5)
    each(12, lambda k: first_sweep(k + 2), 6)
    each(12, lambda k: second_sweep(k + 2), 6)

    def v_part(index, start, count):
        return remote(
            v2.at[pl.ds(start + 1, count)], vin.at[pl.ds(start, count)], v_send.at[index], v_recv.at[index], tm + 1, sp
        )

    v_parts = [v_part(n, *rows) for n, rows in enumerate(ROWS)]
    behind = team + lax.rem(spot + GROUP - 1, GROUP)
    start, count = ROWS[1]
    hops = [
        remote(v2.at[pl.ds(start + 1, count)], around.at[0], o_send.at[0], o_recv.at[0], behind, sp),
        remote(around.at[0], around.at[1], o_send.at[1], o_recv.at[1], behind, sp),
        remote(around.at[1], vin.at[pl.ds(start, count)], o_send.at[2], v_recv.at[1], behind, sp),
    ]
    goes = [spot != GROUP - 1, spot != GROUP - 2, spot != GROUP - 3]

    def start_hop(n):
        @pl.when(goes[n])
        def _():
            if n > 0:
                hops[n - 1].wait_recv()
            hops[n].start()

    @pl.when(not_last)
    def _():
        v_parts[0].start()

    start_hop(0)

    relay_in, relay_out = [], []
    for k, n in enumerate((1, 3)):
        first, count = ROWS[n]
        held = relay.at[k]
        relay_in.append(remote(v2.at[pl.ds(first + 1, count)], held, q_send.at[k], q_recv.at[k], team, sp))
        relay_out.append(remote(held, vin.at[pl.ds(first, count)], q_send.at[2 + k], v_recv.at[n], tm + GROUP, sp))

    def start_relay(k):
        @pl.when(is_first)
        def _():
            relay_in[k].wait_recv()
            relay_out[k].start()

    @pl.when(tm == GROUP - 1)
    def _():
        relay_in[0].start()

    each(4, lambda k: coarse_row(k + 2), 2)
    for n, i in enumerate((1, 6)):
        c1[i + 1] = restrict_row(v1[2 * i + 2] + v1[2 * i + 3], staging.at[n])
    send_terms(0)

    all_tiles(6 * 16, u_recv.at[0]).wait_recv()
    for r in (-1, 16):
        local_terms(r)
    for r in (0, 15):
        first_sweep(r)
    for r in (1, 14):
        second_sweep(r)
    for i in (1, 6):
        coarse_row(i)
    all_tiles(2 * (3 * 16 + 4), e_recv.at[0]).wait_recv()
    for r in (-1, 16):
        first_sweep(r)
    for r in (-1, 0, 15, 16):
        second_sweep(r)
    for i in (0, 7):
        coarse_row(i)
    each(2, restrict_rim, 2)


    @pl.when(is_first)
    def _():
        all_tiles(10 * (3 * GROUP - 1), a_send.at[1]).wait_send()

    send_terms(1)

    @pl.when(not_last)
    def _():
        v_parts[2].start()


    c2_up = remote(c2.at[pl.ds(8, 1)], c2.at[pl.ds(0, 1)], h_send.at[0], h_recv.at[0], tm, right)
    c2_down = remote(c2.at[pl.ds(1, 1)], c2.at[pl.ds(9, 1)], h_send.at[0], h_recv.at[0], tm, left)
    c2_up.start()
    c2_down.start()
    v1_out = pltpu.make_async_copy(v1.at[pl.ds(2, 16)], vv_hbm.at[1], out_sem.at[0])
    v2_out = pltpu.make_async_copy(v2.at[pl.ds(1, 16)], vv_hbm.at[2], out_sem.at[1])
    u0_out = pltpu.make_async_copy(ub.at[0, pl.ds(3, 16)], vv_hbm.at[0], out_sem.at[2])
    p_next = [
        remote(c2.at[pl.ds(k, 1)], c2p.at[pl.ds(k, 1)], p_send.at[0], p_recv.at[0], tm + 1, sp) for n, k in enumerate((0, 9))
    ]
    v1_out.start()
    v2_out.start()

    @pl.when(is_first)
    def _():
        u0_out.start()

    start_hop(1)
    start_relay(0)
    wait_terms(0)
    wait_terms(1)

    def late_parts():
        for copy in v_parts[3:]:
            copy.start()

    @pl.when(not_last & (tm != GROUP - 1))
    def _():
        late_parts()

    @pl.when(tm == GROUP - 1)
    def _():
        relay_in[1].start()

    all_tiles(2 * 4, h_recv.at[0]).wait_recv()

    @pl.when(not_last)
    def _():
        for copy in p_next:
            copy.start()

    @pl.when(jnp.logical_not(first_team))
    def _():
        start_hop(2)

    @pl.when(is_first)
    def _():
        all_tiles(20, w_recv.at[0]).wait_recv()

    @pl.when(not_first)
    def _():
        all_tiles(30, w_recv.at[0]).wait_recv()

    for piece in range(3):
        for r in range(8):
            block, k = PLACE[r]
            w0[8 * piece + r] = get_row(wx.at[piece, block], k)

    last_m = GROUP - 1

    def go_home(m, go, here):
        owner = team + m

        @pl.when(m != spot)
        def _():
            go(remote(res.at[m], home.at[spot], r_send.at[0], r_recv.at[0], owner, sp))

        @pl.when(m == spot)
        def _():
            here()

    end_copies = [
        remote(res.at[last_m, 2, 8], edges.at[0, spot], g_send.at[0], g_recv.at[0], team + last_m, right),
        remote(res.at[last_m, 2, 1], edges.at[1, spot], g_send.at[0], g_recv.at[0], team + last_m, left),
    ]

    def sweep(m):
        def term(field, k):
            block, place = PLACE[k % 8]
            return get_row(rx.at[block, m, k // 8, field], place)

        def keep(field, k, value):
            if 7 <= k < 17:
                res[m, field, k - 7] = value[:, :128]

        for k in range(7, 17):
            keep(0, k, w0[k])
        for k in range(1, 23):
            value = w0[k] + half_step * ring_rate(w0[k - 1], w0[k], w0[k + 1]) + term(0, k)
            w1[k] = value
            keep(1, k, value)
        for k in range(2, 22):
            value = w1[k] + half_step * ring_rate(w1[k - 1], w1[k], w1[k + 1]) + term(1, k)
            w0[k] = value
            keep(2, k, value)

        def here():
            home[spot] = res[m]

        go_home(m, lambda copy: copy.start(), here)

    each(GROUP, sweep)
    for copy in end_copies:
        copy.start()

    group_sends = [
        remote(wpack, wx.at[piece], w_send.at[0], w_recv.at[0], tm + GROUP, s) for s, piece in sides
    ]

    @pl.when(first_team)
    def _():
        rows = [split_tiles(w0[k]) for k in range(8, 16)]
        for block in range(2):
            put_block(wpack.at[block], [rows[r][0] for r in BLOCKS[block]], [rows[r][1] for r in BLOCKS[block]], lane)
        for copy in group_sends:
            copy.start()

    @pl.when(tm == GROUP - 1)
    def _():
        all_tiles(30, w_send.at[0]).wait_send()
        v_parts[4].start()

    @pl.when(first_team)
    def _():
        start_hop(2)


    def vin_out(n):
        rows = pl.ds(*ROWS[n])
        return pltpu.make_async_copy(vin.at[rows], vv_hbm.at[0, rows], out_sem.at[5 + n])

    def take_parts(which):
        for n in which:
            v_parts[n].wait_recv()
            vin_out(n).start()
        for n in which:
            first, count = ROWS[n]
            for i in range(first // 2, (first + count) // 2):
                c2p[i + 1] = restrict_row(vin[2 * i] + vin[2 * i + 1], staging.at[i % 6])

    all_tiles(6 * 16, u_send.at[0]).wait_send()
    all_tiles(2 * (3 * 16 + 4), e_send.at[0]).wait_send()
    all_tiles(2 * 4, h_send.at[0]).wait_send()
    for block in range(2):
        for fields in range(3):
            pl.when(fields_beside(block, spot) == fields)(
                lambda: all_tiles(10 * (GROUP - 1) + 10 * GROUP * fields, a_send.at[block]).wait_send()
            )

    @pl.when(is_first)
    def _():
        u0_out.wait()

    @pl.when(tm < GROUP - 1)
    def _():
        all_tiles(30, w_send.at[0]).wait_send()

    v1_out.wait()
    v2_out.wait()

    start_relay(1)

    @pl.when(not_first)
    def _():
        take_parts((0, 2))
        take_parts((1, 3, 4))

    all_tiles(30 * (GROUP - 1), r_recv.at[0]).wait_recv()

    for t in range(GROUP):
        columns = pl.ds(128 * t, 128)
        dd[1, :, :, columns] = home[t, 1] - c1[:, :, columns]
        dd[2, :, :, columns] = home[t, 2] - c2[:, :, columns]

    @pl.when(spot == last_m)
    def _():
        all_tiles(2 * GROUP, g_recv.at[0]).wait_recv()
        for t in range(GROUP):
            columns = pl.ds(128 * t, 128)
            for side in range(2):
                dd[2, 9 * side, :, columns] = edges[side, t] - c2[9 * side, :, columns]

    d_out = [
        pltpu.make_async_copy(dd.at[pl.ds(1, 2)], d_hbm.at[pl.ds(1, 2)], out_sem.at[3]),
        pltpu.make_async_copy(dd.at[pl.ds(0, 1)], d_hbm.at[pl.ds(0, 1)], out_sem.at[4]),
    ]
    d_out[0].start()

    @pl.when(is_first)
    def _():
        dd[0] = jnp.zeros(dd.shape[1:], F32)

    @pl.when(not_first)
    def _():
        all_tiles(8, p_recv.at[0]).wait_recv()
        for t in range(GROUP):
            columns = pl.ds(128 * t, 128)
            dd[0, :, :, columns] = home[t, 0] - c2p[:, :, columns]

    d_out[1].start()

    all_tiles(30 * (GROUP - 1), r_send.at[0]).wait_send()
    all_tiles(2, g_send.at[0]).wait_send()

    @pl.when(not_last)
    def _():
        all_tiles(8, p_send.at[0]).wait_send()
        for n in (0, 2, 4):
            v_parts[n].wait_send()

    @pl.when(not_last & (tm != GROUP - 1))
    def _():
        v_parts[3].wait_send()

    @pl.when(tm == GROUP - 1)
    def _():
        for copy in relay_in:
            copy.wait_send()

    @pl.when(is_first)
    def _():
        for copy in relay_out:
            copy.wait_send()

    for n in range(3):

        @pl.when(goes[n])
        def _():
            hops[n].wait_send()

    @pl.when(not_first)
    def _():
        for n in range(5):
            vin_out(n).wait()

    for copy in d_out:
        copy.wait()


def correct_kernel(vv_hbm, d_ref, o_hbm, vb, refined, in_sem, out_sem):
    sub, lane = iotas()
    lanes = vb.shape[-1]
    half = lanes // 256
    up_index = (sub // 4) * 4 + (sub + 1) % 4
    down_index = (sub // 4) * 4 + (sub + 3) % 4

    def load(m):
        return pltpu.make_async_copy(vv_hbm.at[m], vb.at[m], in_sem.at[m])

    def store(m, r):
        return pltpu.make_async_copy(vb.at[m, r], o_hbm.at[0, m, :, r, :], out_sem)

    for m in range(3):
        load(m).start()

    def spread_lanes(m, t):
        rows = [split_tiles(d_ref[m, k]) for k in range(10)]
        wide = jnp.concatenate(
            [jnp.concatenate([v[t], strip_of(v, t, lane)], axis=1) for v in rows], axis=0
        )
        total = None
        for _ in range(3):
            part = wide.astype(jnp.bfloat16)
            wide = wide - part.astype(F32)
            product = jnp.dot(part, weights, preferred_element_type=F32)
            total = product if total is None else total + product
        return total

    row_index = lax.broadcasted_iota(jnp.int32, (256, 256), 0)
    fine_index = lax.broadcasted_iota(jnp.int32, (256, 256), 1)
    near = fine_index // 2
    far = lax.rem(near + 255 + 2 * (fine_index % 2), 256)
    weights = jnp.where(row_index == near, 0.75, jnp.where(row_index == far, 0.25, 0.0)).astype(jnp.bfloat16)

    def spread_all(m):
        for i in range(half // 2):
            refined_lanes = spread_lanes(m, i)
            for k in range(10):
                for t in (2 * i, 2 * i + 1):
                    fine = refined_lanes[8 * k : 8 * k + 8, 128 * (t - 2 * i) : 128 * (t - 2 * i) + 128]
                    near_part, far_part = 0.75 * fine, 0.25 * fine
                    refined.at[k][pl.ds(16 * t, 8, stride=2), :] = near_part + take(far_part, down_index, 0)
                    refined.at[k][pl.ds(16 * t + 1, 8, stride=2), :] = near_part + take(far_part, up_index, 0)

    def refined_row(k):
        return jnp.concatenate(
            [refined[k, pl.ds(16 * t + 8 * h, 8), :] for h in range(2) for t in range(half)], axis=1
        )

    def node(m):
        spread_all(m)
        load(m).wait()

        def rows(k):
            own = 0.75 * refined_row(k + 1)
            vb[m, 2 * k] = vb[m, 2 * k] + (own + 0.25 * refined_row(k))
            vb[m, 2 * k + 1] = vb[m, 2 * k + 1] + (own + 0.25 * refined_row(k + 2))
            store(m, 2 * k).start()
            store(m, 2 * k + 1).start()

        each(8, rows, 4)

    each(3, node)

    pltpu.make_async_copy(vb, vb, out_sem).wait()


def on_device(node_values):
    _, _, depth, rows, lanes = node_values.shape
    half = lanes // 4
    fine = lambda n: pltpu.VMEM((n, 8, lanes), F32)
    coarse = lambda n: pltpu.VMEM((n, 8, half), F32)
    tiles = lambda *n: pltpu.VMEM(n + (8, 128), F32)
    dma = lambda *n: pltpu.SemaphoreType.DMA(n)
    anywhere = pl.BlockSpec(memory_space=pl.ANY)
    vv, dd = pl.pallas_call(
        main_kernel,
        name="sweeps",
        out_shape=(
            jax.ShapeDtypeStruct((3, rows, depth, lanes), F32),
            jax.ShapeDtypeStruct((3, 10, 8, half), F32),
        ),
        in_specs=[anywhere],
        out_specs=(anywhere, anywhere),
        scratch_shapes=[
            pltpu.VMEM((3, 22, 8, lanes), F32), fine(22), fine(20), fine(20), fine(20), fine(20), fine(20), fine(20), fine(18), fine(16), pltpu.VMEM((2, ROWS[1][1], 8, lanes), F32), pltpu.VMEM((2, ROWS[1][1], 8, lanes), F32),
            coarse(10), coarse(10), coarse(10), coarse(10), coarse(12), coarse(10),
            tiles(2, GROUP, 2, 5), tiles(GROUP, 2, 5), tiles(2, 5), tiles(2, GROUP, 3, 2, 5), tiles(3, 2, 5),
            pltpu.VMEM((24, 8, 256), F32), pltpu.VMEM((24, 8, 256), F32), tiles(GROUP, 3, 10), tiles(GROUP, 3, 10), tiles(2, GROUP), tiles(110),
            pltpu.VMEM((3, 10, 8, half), F32), pltpu.VMEM((6, lanes // 16, 128), F32),
            dma(2), dma(1), dma(1), dma(1), dma(1), dma(1), dma(1), dma(2), dma(2), dma(1), dma(1), dma(1), dma(1),
            dma(1), dma(1), dma(5), dma(5), dma(3), dma(2), dma(4), dma(2), dma(1), dma(1), dma(10),
        ],
        compiler_params=pltpu.CompilerParams(
            collective_id=0, has_side_effects=True, vmem_limit_bytes=48 * 1024 * 1024
        ),
    )(node_values)
    return pl.pallas_call(
        correct_kernel,
        name="correct",
        out_shape=jax.ShapeDtypeStruct(node_values.shape, F32),
        in_specs=[anywhere, pl.BlockSpec(memory_space=pltpu.VMEM)],
        out_specs=anywhere,
        scratch_shapes=[
            pltpu.VMEM((3, rows, 8, lanes), F32), pltpu.VMEM((10, lanes // 16, 128), F32),
            dma(3), pltpu.SemaphoreType.DMA,
        ],
        compiler_params=pltpu.CompilerParams(vmem_limit_bytes=48 * 1024 * 1024),
    )(vv, dd)


def solution(mesh):
    return jax.shard_map(
        on_device,
        mesh=mesh,
        in_specs=(P("tm", None, None, "space", None),),
        out_specs=P("tm", None, None, "space", None),
        check_vma=False,
    )
```

```python
import functools

import jax
import jax.numpy as jnp
from jax import lax
from jax.experimental import pallas as pl
from jax.experimental.pallas import tpu as pltpu
from jax.sharding import PartitionSpec as P

STEP = 0.25
WEIGHTS = ((5.0 / 24.0, 1.0 / 3.0, -1.0 / 24.0), (-1.0 / 24.0, 1.0 / 3.0, 5.0 / 24.0))
MESH = pl.DeviceIdType.MESH
GROUP = 4
ROWS = ((2, 2), (4, 4), (8, 4), (12, 4), (0, 2))
BLOCKS = ((2, 3, 4, 5), (0, 1, 6, 7))
PLACE = {r: (b, k) for b, rows in enumerate(BLOCKS) for k, r in enumerate(rows)}
F32 = jnp.float32


def neighbour_sum(above, center, below):
    lanes = center.shape[-1]
    beside = above + below + pltpu.roll(center, 1, 0) + pltpu.roll(center, 7, 0)
    return beside + pltpu.roll(center, 1, 1) + pltpu.roll(center, lanes - 1, 1)


def cube(value):
    return value * value * value


def combine(weights, terms):
    total = weights[0] * terms[0]
    for weight, term in zip(weights[1:], terms[1:]):
        total = total + weight * term
    return total


def each(count, body, unroll=1):
    def step(k, carry):
        body(k)
        return carry

    lax.fori_loop(0, count, step, 0, unroll=unroll)


def iotas():
    sub = lax.broadcasted_iota(jnp.int32, (8, 128), 0)
    lane = lax.broadcasted_iota(jnp.int32, (8, 128), 1)
    return sub, lane


def take(value, index, axis):
    return jnp.take_along_axis(value, index, axis=axis, mode="promise_in_bounds")


def split_tiles(value):
    return [value[:, 128 * t : 128 * (t + 1)] for t in range(value.shape[1] // 128)]


def lane_neighbours(tiles, lane):
    count = len(tiles)
    right_rolled = [pltpu.roll(t, 1, 1) for t in tiles]
    left_rolled = [pltpu.roll(t, 127, 1) for t in tiles]
    before = [pltpu.roll(right_rolled[-1], 4, 0)] + right_rolled[:-1]
    after = left_rolled[1:] + [pltpu.roll(left_rolled[0], 4, 0)]
    left = [jnp.where(lane == 0, before[i], right_rolled[i]) for i in range(count)]
    right = [jnp.where(lane == 127, after[i], left_rolled[i]) for i in range(count)]
    return left, right


def coarse_rate(above, center, below):
    sub, lane = iotas()
    up_index = (sub // 4) * 4 + (sub + 1) % 4
    down_index = (sub // 4) * 4 + (sub + 3) % 4
    a, c, b = split_tiles(above), split_tiles(center), split_tiles(below)
    left, right = lane_neighbours(c, lane)
    out = []
    for i in range(len(c)):
        beside = a[i] + b[i] + take(c[i], up_index, 0) + take(c[i], down_index, 0) + left[i] + right[i]
        out.append(0.25 * beside + c[i] * (0.5 - 2.0 * (c[i] * c[i])))
    return jnp.concatenate(out, axis=1)


def ring_rate(above, center, below):
    sub, _ = iotas()
    up_index = (sub // 4) * 4 + (sub + 1) % 4
    down_index = (sub // 4) * 4 + (sub + 3) % 4
    beside = above + below + pltpu.roll(center, 1, 1) + pltpu.roll(center, 255, 1)
    depth = [take(t, up_index, 0) + take(t, down_index, 0) for t in split_tiles(center)]
    beside = beside + jnp.concatenate(depth, axis=1)
    return 0.25 * beside + center * (0.5 - 2.0 * (center * center))


def strip_of(tiles, t, lane):
    after = tiles[t + 1] if t + 1 < len(tiles) else pltpu.roll(tiles[0], 4, 0)
    before = tiles[t - 1] if t > 0 else pltpu.roll(tiles[-1], 4, 0)
    return jnp.where(lane < 64, after, before)


def join_strips(strips, lane):
    block = ((lane + 16) // 32) % 4
    joined = strips[0]
    for k in range(1, 4):
        joined = jnp.where(block == k, pltpu.roll(strips[k], 32 * k, 1), joined)
    return joined


def put_block(ref, rows, strips, lane):
    for k, place in enumerate((0, 1, 3, 4)):
        ref[place] = rows[k]
    ref[2] = join_strips(strips, lane)


def get_row(ref, k):
    strip = pltpu.roll(ref[2], (128 - 32 * k) % 128, 1)
    return jnp.concatenate([ref[k if k < 2 else k + 1], strip], axis=1)


def packed_halves(row, staging):
    tiles = split_tiles(row)
    half = len(tiles) // 2
    for t in range(half):
        staging[pl.ds(16 * t, 8), :] = tiles[t]
        staging[pl.ds(16 * t + 8, 8), :] = tiles[t + half]
    even = [staging[pl.ds(16 * t, 8, stride=2), :] for t in range(half)]
    odd = [staging[pl.ds(16 * t + 1, 8, stride=2), :] for t in range(half)]
    return even, odd


def decimate_index(lane):
    return jnp.where(lane < 64, 2 * lane, 2 * lane - 127)


def lane_pairs(packed, lane):
    out = []
    for t in range(len(packed) // 2):
        p, q = packed[2 * t], packed[2 * t + 1]
        mixed = jnp.where(lane % 2 == 0, p + pltpu.roll(p, 127, 1), q + pltpu.roll(q, 1, 1))
        out.append(take(mixed, decimate_index(lane), 1))
    return out


def lane_even_odd(packed, lane):
    even, odd = [], []
    for t in range(len(packed) // 2):
        p, q = packed[2 * t], packed[2 * t + 1]
        even.append(take(jnp.where(lane % 2 == 0, p, pltpu.roll(q, 1, 1)), decimate_index(lane), 1))
        odd.append(take(jnp.where(lane % 2 == 0, pltpu.roll(p, 127, 1), q), decimate_index(lane), 1))
    return even, odd


def restrict_row(pair_sum, staging):
    _, lane = iotas()
    even, odd = packed_halves(pair_sum, staging)
    sums = lane_pairs([a + b for a, b in zip(even, odd)], lane)
    return jnp.concatenate([0.125 * v for v in sums], axis=1)


def coarse_terms(fields, staging):
    sub, lane = iotas()
    up_index = (sub // 4) * 4 + (sub + 1) % 4
    down_index = (sub // 4) * 4 + (sub + 3) % 4
    nodes, inner, evens, odds = [], [], [], []
    for n, (before, a, b, after) in enumerate(fields):
        total = a + b
        rest = (before + after) - total - 2.0 * (cube(a) + cube(b))
        even, odd = packed_halves(total, staging.at[2 * n])
        rest_even, rest_odd = packed_halves(rest, staging.at[2 * n + 1])
        count = len(even)
        inner.append(
            [
                rest_even[t] + rest_odd[t] + take(odd[t], down_index, 0) + take(even[t], up_index, 0)
                for t in range(count)
            ]
        )
        lane_even, lane_odd = lane_even_odd([even[t] + odd[t] for t in range(count)], lane)
        evens.append(lane_even)
        odds.append(lane_odd)
        nodes.append(jnp.concatenate([0.125 * (p + q) for p, q in zip(lane_even, lane_odd)], axis=1))
    sums = []
    for weights in WEIGHTS:
        weights = [0.125 * STEP * w for w in weights]
        body = lane_pairs([combine(weights, v) for v in zip(*inner)], lane)
        left, _ = lane_neighbours([combine(weights, v) for v in zip(*odds)], lane)
        _, right = lane_neighbours([combine(weights, v) for v in zip(*evens)], lane)
        sums.append(jnp.concatenate([b + l + r for b, l, r in zip(body, left, right)], axis=1))
    return nodes, sums


def main_kernel(
    u_hbm, vv_hbm, d_hbm,
    ub, bb, p0, kk, q1, v1, mm, p2, v2, vin, around, relay, c0, c1, c2, c2p, a0, a1, pack, cpack, wpack, rx, wx, w0, w1, res, home, edges, meter, dd, staging,
    load_sem, u_send, u_recv, e_send, e_recv, h_send, h_recv, a_send, a_recv, w_send, w_recv, r_send, r_recv, g_send, g_recv, v_send, v_recv, o_send, o_recv, q_send, q_recv,
    p_send, p_recv, out_sem,
):
    tm, sp = lax.axis_index("tm"), lax.axis_index("space")
    n_tm, n_sp = lax.axis_size("tm"), lax.axis_size("space")
    left, right = lax.rem(sp + n_sp - 1, n_sp), lax.rem(sp + 1, n_sp)
    not_first, not_last = tm > 0, tm < n_tm - 1
    half_step = 0.5 * STEP
    team = GROUP * (tm // GROUP)
    spot = tm - team
    first_team = tm < GROUP
    sides = ((left, 2), (sp, 1), (right, 0))

    def load(m, r):
        return u_hbm.at[0, m, :, r, :], ub.at[m, r + 3]

    def remote(src, dst, send, recv, t, s):
        return pltpu.make_async_remote_copy(
            src_ref=src, dst_ref=dst, send_sem=send, recv_sem=recv, device_id=(t, s), device_id_type=MESH
        )

    def all_tiles(count, sem):
        return remote(meter.at[pl.ds(0, count)], meter.at[pl.ds(0, count)], sem, sem, tm, left)

    def edge_row(k):
        return jnp.where(k < 3, k, k + 10)

    def load_edges(k):
        for m in range(3):
            pltpu.make_async_copy(*load(m, edge_row(k)), load_sem.at[0]).start()

    def load_inner(k):
        for m in range(3):
            pltpu.make_async_copy(*load(m, k + 3), load_sem.at[1]).start()

    each(6, load_edges)
    each(10, load_inner)

    barrier = pltpu.get_barrier_semaphore()
    for d in range(GROUP):
        mate = team + lax.rem(spot + d, GROUP)
        for s, _ in sides:
            if d > 0 or s is not sp:
                pl.semaphore_signal(barrier, inc=1, device_id=(mate, s), device_id_type=MESH)

    @pl.when(jnp.logical_not(first_team))
    def _():
        for s, _ in sides:
            pl.semaphore_signal(barrier, inc=1, device_id=(tm - GROUP, s), device_id_type=MESH)

    @pl.when(tm == GROUP)
    def _():
        pl.semaphore_signal(barrier, inc=1, device_id=(tm - 1, sp), device_id_type=MESH)

    @pl.when(tm < GROUP - 1)
    def _():
        pl.semaphore_wait(barrier, 3 * GROUP + 2)

    @pl.when(tm == GROUP - 1)
    def _():
        pl.semaphore_wait(barrier, 3 * GROUP + 3)

    @pl.when(jnp.logical_not(first_team))
    def _():
        pl.semaphore_wait(barrier, 3 * GROUP - 1)

    def wait_rows(count, sem):
        rows = ub.at[:, pl.ds(3, count)]
        pltpu.make_async_copy(rows, rows, sem).wait()

    wait_rows(6, load_sem.at[0])
    u_copies = [
        remote(ub.at[:, pl.ds(18, 1)], ub.at[:, pl.ds(2, 1)], u_send.at[0], u_recv.at[0], tm, right),
        remote(ub.at[:, pl.ds(3, 1)], ub.at[:, pl.ds(19, 1)], u_send.at[0], u_recv.at[0], tm, left),
    ]
    for copy in u_copies:
        copy.start()

    weights = [STEP * w for w in WEIGHTS[0]]
    later_weights = [STEP * w for w in WEIGHTS[1]]
    later_weights[1] = later_weights[1] - half_step

    def local_terms(r):
        nodes = [ub[m, r + 3] for m in range(3)]
        cubes = [cube(v) for v in nodes]
        mixed = combine(weights, nodes)
        bb[r + 3] = mixed
        p0[r + 2] = nodes[0] - 4.0 * mixed + combine([-2.0 * w for w in weights], cubes)
        kk[r + 2] = combine(later_weights, nodes)
        q1[r + 2] = combine([-2.0 * w for w in later_weights], cubes)

    def first_sweep(r):
        value = p0[r + 2] + neighbour_sum(bb[r + 2], bb[r + 3], bb[r + 4])
        mixed = half_step * value + kk[r + 2]
        v1[r + 2] = value
        mm[r + 2] = mixed
        p2[r + 2] = value + q1[r + 2] - 4.0 * mixed - STEP * cube(value)

    def second_sweep(r):
        v2[r + 1] = p2[r + 2] + neighbour_sum(mm[r + 1], mm[r + 2], mm[r + 3])

    def restrict_rim(k):
        i = 9 * k - 1
        c1[i + 1] = restrict_row(v1[2 * i + 2] + v1[2 * i + 3], staging.at[k])

    def coarse_row(i):
        r = 2 * i
        fields = [
            [ub[0, r + k] for k in range(2, 6)],
            [v1[r + k] for k in range(1, 5)],
            [v2[r + k] for k in range(4)],
        ]
        (_, c1[i + 1], c2[i + 1]), (a0[i + 2], a1[i + 1]) = coarse_terms(fields, staging)

    _, lane = iotas()
    is_first = jnp.logical_not(not_first)

    def pack_rows(rows, place):
        tiles = [split_tiles(row) for row in rows]
        for t in range(GROUP):
            put_block(place(t), [v[t] for v in tiles], [strip_of(v, t, lane) for v in tiles], lane)

    def start_copies(piece, go):
        for d in range(GROUP):
            keeper = lax.rem(spot + d, GROUP)
            for s, p in sides:
                if p == piece and (d > 0 or p != 1):
                    copy = remote(
                        cpack.at[keeper], wx.at[p], a_send.at[1], w_recv.at[0], team + keeper, s
                    )
                    go(copy)

    def terms_copy(block, fields, keeper, m, piece, s, entries=(0, 5)):
        where = (pl.ds(0, fields), pl.ds(*entries))
        return remote(
            pack.at[(block, keeper, *where)], rx.at[(block, m, piece, *where)],
            a_send.at[block], a_recv.at[block], team + keeper, s,
        )

    def sized(block, m, go):
        if block == 0:
            pl.when(m < 2)(lambda: go(2, False))
            pl.when(m == 2)(lambda: go(1, True))
        else:
            pl.when(m == 0)(lambda: go(2, False))
            pl.when((m == 1) | (m == 2))(lambda: go(2, True))
            pl.when(m == 3)(lambda: go(1, True))

    def terms_copies(block, go):
        def mate(d):
            keeper = lax.rem(spot + d, GROUP)

            @pl.when(d > 0)
            def _():
                go(terms_copy(block, 2, keeper, spot, 1, sp))

            def beside(fields, half):
                go(terms_copy(block, fields, keeper, spot, 2, left, (0, 3) if half else (0, 5)))
                go(terms_copy(block, fields, keeper, spot, 0, right, (2, 3) if half else (0, 5)))

            sized(block, spot, beside)

        each(GROUP, mate)

    def tiles_beside(block, m):
        if block == 0:
            return jnp.where(m < 2, 10, jnp.where(m == 2, 3, 0))
        return jnp.where(m == 0, 10, jnp.where(m < 3, 6, 3))

    def wait_terms(block):
        all_tiles(10 * (GROUP - 1) + 2 * (23, 25)[block], a_recv.at[block]).wait_recv()

    def send_terms(block):
        for k in BLOCKS[block]:
            a0[k + 2] = a0[k + 2] - half_step * coarse_rate(c0[k], c0[k + 1], c0[k + 2])
            a1[k + 1] = a1[k + 1] - half_step * coarse_rate(c1[k], c1[k + 1], c1[k + 2])
        pack_rows([a0[k + 2] for k in BLOCKS[block]], lambda t: pack.at[block, t, 0])
        pack_rows([a1[k + 1] for k in BLOCKS[block]], lambda t: pack.at[block, t, 1])
        terms_copies(block, lambda copy: copy.start())
        rx[block, spot, 1] = pack[block, spot]

    def restrict_first(i):
        c0[i + 1] = restrict_row(ub[0, 2 * i + 3] + ub[0, 2 * i + 4], staging.at[i % 4])

    each(6, lambda k: local_terms(edge_row(k)), 3)
    for k in (0, 7):
        restrict_first(k)
    for r in (1, 14):
        first_sweep(r)
    rim_copies, rows_of = [], (16, 16, 16, 8)
    for n, (field, offset, up, down) in enumerate(((bb, 3, 14, 1), (v1, 2, 14, 1), (mm, 2, 14, 1), (c0, 1, 7, 0))):
        up_target, down_target = up + offset - rows_of[n], down + offset + rows_of[n]
        rim_copies += [
            remote(field.at[pl.ds(up + offset, 1)], field.at[pl.ds(up_target, 1)], e_send.at[0], e_recv.at[0], tm, right),
            remote(field.at[pl.ds(down + offset, 1)], field.at[pl.ds(down_target, 1)], e_send.at[0], e_recv.at[0], tm, left),
        ]
    for copy in rim_copies:
        copy.start()
    wait_rows(10, load_sem.at[1])
    for k in range(1, 7):
        restrict_first(k)

    @pl.when(is_first)
    def _():
        for block in range(2):
            pack_rows([c0[k + 1] for k in BLOCKS[block]], lambda t: cpack.at[t, block])
        for piece in range(3):
            start_copies(piece, lambda copy: copy.start())
        wx[1] = cpack[0]

    each(10, lambda k: local_terms(k + 3), 5)
    each(12, lambda k: first_sweep(k + 2), 6)
    each(12, lambda k: second_sweep(k + 2), 6)

    def v_part(index, start, count):
        return remote(
            v2.at[pl.ds(start + 1, count)], vin.at[pl.ds(start, count)], v_send.at[index], v_recv.at[index], tm + 1, sp
        )

    v_parts = [v_part(n, *rows) for n, rows in enumerate(ROWS)]
    behind = team + lax.rem(spot + GROUP - 1, GROUP)
    start, count = ROWS[1]
    hops = [
        remote(v2.at[pl.ds(start + 1, count)], around.at[0], o_send.at[0], o_recv.at[0], behind, sp),
        remote(around.at[0], around.at[1], o_send.at[1], o_recv.at[1], behind, sp),
        remote(around.at[1], vin.at[pl.ds(start, count)], o_send.at[2], v_recv.at[1], behind, sp),
    ]
    goes = [spot != GROUP - 1, spot != GROUP - 2, spot != GROUP - 3]

    def start_hop(n):
        @pl.when(goes[n])
        def _():
            if n > 0:
                hops[n - 1].wait_recv()
            hops[n].start()

    @pl.when(not_last)
    def _():
        v_parts[0].start()

    start_hop(0)

    relay_in, relay_out = [], []
    for k, n in enumerate((1, 3)):
        first, count = ROWS[n]
        held = relay.at[k]
        relay_in.append(remote(v2.at[pl.ds(first + 1, count)], held, q_send.at[k], q_recv.at[k], team, sp))
        relay_out.append(remote(held, vin.at[pl.ds(first, count)], q_send.at[2 + k], v_recv.at[n], tm + GROUP, sp))

    def start_relay(k):
        @pl.when(is_first)
        def _():
            relay_in[k].wait_recv()
            relay_out[k].start()

    @pl.when(tm == GROUP - 1)
    def _():
        relay_in[0].start()

    each(4, lambda k: coarse_row(k + 2), 2)
    for n, i in enumerate((1, 6)):
        c1[i + 1] = restrict_row(v1[2 * i + 2] + v1[2 * i + 3], staging.at[n])
    send_terms(0)

    all_tiles(6 * 16, u_recv.at[0]).wait_recv()
    for r in (-1, 16):
        local_terms(r)
    for r in (0, 15):
        first_sweep(r)
    for r in (1, 14):
        second_sweep(r)
    for i in (1, 6):
        coarse_row(i)
    all_tiles(2 * (3 * 16 + 4), e_recv.at[0]).wait_recv()
    for r in (-1, 16):
        first_sweep(r)
    for r in (-1, 0, 15, 16):
        second_sweep(r)
    for i in (0, 7):
        coarse_row(i)
    each(2, restrict_rim, 2)


    @pl.when(is_first)
    def _():
        all_tiles(10 * (3 * GROUP - 1), a_send.at[1]).wait_send()

    send_terms(1)

    @pl.when(not_last)
    def _():
        v_parts[2].start()


    c2_up = remote(c2.at[pl.ds(8, 1)], c2.at[pl.ds(0, 1)], h_send.at[0], h_recv.at[0], tm, right)
    c2_down = remote(c2.at[pl.ds(1, 1)], c2.at[pl.ds(9, 1)], h_send.at[0], h_recv.at[0], tm, left)
    c2_up.start()
    c2_down.start()
    v1_out = pltpu.make_async_copy(v1.at[pl.ds(2, 16)], vv_hbm.at[1], out_sem.at[0])
    v2_out = pltpu.make_async_copy(v2.at[pl.ds(1, 16)], vv_hbm.at[2], out_sem.at[1])
    u0_out = pltpu.make_async_copy(ub.at[0, pl.ds(3, 16)], vv_hbm.at[0], out_sem.at[2])
    p_next = [
        remote(c2.at[pl.ds(k, 1)], c2p.at[pl.ds(k, 1)], p_send.at[0], p_recv.at[0], tm + 1, sp) for n, k in enumerate((0, 9))
    ]
    v1_out.start()
    v2_out.start()

    @pl.when(is_first)
    def _():
        u0_out.start()

    start_hop(1)
    start_relay(0)
    wait_terms(0)
    wait_terms(1)

    def late_parts():
        for copy in v_parts[3:]:
            copy.start()

    @pl.when(not_last & (tm != GROUP - 1))
    def _():
        late_parts()

    @pl.when(tm == GROUP - 1)
    def _():
        relay_in[1].start()

    all_tiles(2 * 4, h_recv.at[0]).wait_recv()

    @pl.when(not_last)
    def _():
        for copy in p_next:
            copy.start()

    @pl.when(jnp.logical_not(first_team))
    def _():
        start_hop(2)

    @pl.when(is_first)
    def _():
        all_tiles(20, w_recv.at[0]).wait_recv()

    @pl.when(not_first)
    def _():
        all_tiles(30, w_recv.at[0]).wait_recv()

    for piece in range(3):
        for r in range(8):
            block, k = PLACE[r]
            w0[8 * piece + r] = get_row(wx.at[piece, block], k)

    last_m = GROUP - 1

    def go_home(m, go, here):
        owner = team + m

        @pl.when(m != spot)
        def _():
            go(remote(res.at[m], home.at[spot], r_send.at[0], r_recv.at[0], owner, sp))

        @pl.when(m == spot)
        def _():
            here()

    end_copies = [
        remote(res.at[last_m, 2, 8], edges.at[0, spot], g_send.at[0], g_recv.at[0], team + last_m, right),
        remote(res.at[last_m, 2, 1], edges.at[1, spot], g_send.at[0], g_recv.at[0], team + last_m, left),
    ]

    def sweep(m):
        def term(field, k):
            block, place = PLACE[k % 8]
            return get_row(rx.at[block, m, k // 8, field], place)

        def keep(field, k, value):
            if 7 <= k < 17:
                res[m, field, k - 7] = value[:, :128]

        for k in range(7, 17):
            keep(0, k, w0[k])
        for k in range(1, 23):
            value = w0[k] + half_step * ring_rate(w0[k - 1], w0[k], w0[k + 1]) + term(0, k)
            w1[k] = value
            keep(1, k, value)
        for k in range(2, 22):
            value = w1[k] + half_step * ring_rate(w1[k - 1], w1[k], w1[k + 1]) + term(1, k)
            w0[k] = value
            keep(2, k, value)

        def here():
            home[spot] = res[m]

        go_home(m, lambda copy: copy.start(), here)

    each(GROUP, sweep)
    for copy in end_copies:
        copy.start()

    group_sends = [
        remote(wpack, wx.at[piece], w_send.at[0], w_recv.at[0], tm + GROUP, s) for s, piece in sides
    ]

    @pl.when(first_team)
    def _():
        rows = [split_tiles(w0[k]) for k in range(8, 16)]
        for block in range(2):
            put_block(wpack.at[block], [rows[r][0] for r in BLOCKS[block]], [rows[r][1] for r in BLOCKS[block]], lane)
        for copy in group_sends:
            copy.start()

    @pl.when(tm == GROUP - 1)
    def _():
        all_tiles(30, w_send.at[0]).wait_send()
        v_parts[4].start()

    @pl.when(first_team)
    def _():
        start_hop(2)


    def vin_out(n):
        rows = pl.ds(*ROWS[n])
        return pltpu.make_async_copy(vin.at[rows], vv_hbm.at[0, rows], out_sem.at[5 + n])

    def take_parts(which):
        for n in which:
            v_parts[n].wait_recv()
            vin_out(n).start()
        for n in which:
            first, count = ROWS[n]
            for i in range(first // 2, (first + count) // 2):
                c2p[i + 1] = restrict_row(vin[2 * i] + vin[2 * i + 1], staging.at[i % 6])

    all_tiles(6 * 16, u_send.at[0]).wait_send()
    all_tiles(2 * (3 * 16 + 4), e_send.at[0]).wait_send()
    all_tiles(2 * 4, h_send.at[0]).wait_send()
    for block in range(2):
        for count in (0, 3, 6, 10):
            pl.when(tiles_beside(block, spot) == count)(
                lambda: all_tiles(10 * (GROUP - 1) + 2 * GROUP * count, a_send.at[block]).wait_send()
            )

    @pl.when(is_first)
    def _():
        u0_out.wait()

    @pl.when(tm < GROUP - 1)
    def _():
        all_tiles(30, w_send.at[0]).wait_send()

    v1_out.wait()
    v2_out.wait()

    start_relay(1)

    @pl.when(not_first)
    def _():
        take_parts((0, 2))
        take_parts((1, 3, 4))

    all_tiles(30 * (GROUP - 1), r_recv.at[0]).wait_recv()

    for t in range(GROUP):
        columns = pl.ds(128 * t, 128)
        dd[1, :, :, columns] = home[t, 1] - c1[:, :, columns]
        dd[2, :, :, columns] = home[t, 2] - c2[:, :, columns]

    @pl.when(spot == last_m)
    def _():
        all_tiles(2 * GROUP, g_recv.at[0]).wait_recv()
        for t in range(GROUP):
            columns = pl.ds(128 * t, 128)
            for side in range(2):
                dd[2, 9 * side, :, columns] = edges[side, t] - c2[9 * side, :, columns]

    d_out = [
        pltpu.make_async_copy(dd.at[pl.ds(1, 2)], d_hbm.at[pl.ds(1, 2)], out_sem.at[3]),
        pltpu.make_async_copy(dd.at[pl.ds(0, 1)], d_hbm.at[pl.ds(0, 1)], out_sem.at[4]),
    ]
    d_out[0].start()

    @pl.when(is_first)
    def _():
        dd[0] = jnp.zeros(dd.shape[1:], F32)

    @pl.when(not_first)
    def _():
        all_tiles(8, p_recv.at[0]).wait_recv()
        for t in range(GROUP):
            columns = pl.ds(128 * t, 128)
            dd[0, :, :, columns] = home[t, 0] - c2p[:, :, columns]

    d_out[1].start()

    all_tiles(30 * (GROUP - 1), r_send.at[0]).wait_send()
    all_tiles(2, g_send.at[0]).wait_send()

    @pl.when(not_last)
    def _():
        all_tiles(8, p_send.at[0]).wait_send()
        for n in (0, 2, 4):
            v_parts[n].wait_send()

    @pl.when(not_last & (tm != GROUP - 1))
    def _():
        v_parts[3].wait_send()

    @pl.when(tm == GROUP - 1)
    def _():
        for copy in relay_in:
            copy.wait_send()

    @pl.when(is_first)
    def _():
        for copy in relay_out:
            copy.wait_send()

    for n in range(3):

        @pl.when(goes[n])
        def _():
            hops[n].wait_send()

    @pl.when(not_first)
    def _():
        for n in range(5):
            vin_out(n).wait()

    for copy in d_out:
        copy.wait()


def correct_kernel(vv_hbm, d_ref, o_hbm, vb, refined, in_sem, out_sem):
    sub, lane = iotas()
    lanes = vb.shape[-1]
    half = lanes // 256
    up_index = (sub // 4) * 4 + (sub + 1) % 4
    down_index = (sub // 4) * 4 + (sub + 3) % 4

    def load(m):
        return pltpu.make_async_copy(vv_hbm.at[m], vb.at[m], in_sem.at[m])

    def store(m, r):
        return pltpu.make_async_copy(vb.at[m, r], o_hbm.at[0, m, :, r, :], out_sem)

    for m in range(3):
        load(m).start()

    def spread_lanes(m, t):
        rows = [split_tiles(d_ref[m, k]) for k in range(10)]
        wide = jnp.concatenate(
            [jnp.concatenate([v[t], strip_of(v, t, lane)], axis=1) for v in rows], axis=0
        )
        total = None
        for _ in range(3):
            part = wide.astype(jnp.bfloat16)
            wide = wide - part.astype(F32)
            product = jnp.dot(part, weights, preferred_element_type=F32)
            total = product if total is None else total + product
        return total

    row_index = lax.broadcasted_iota(jnp.int32, (256, 256), 0)
    fine_index = lax.broadcasted_iota(jnp.int32, (256, 256), 1)
    near = fine_index // 2
    far = lax.rem(near + 255 + 2 * (fine_index % 2), 256)
    weights = jnp.where(row_index == near, 0.75, jnp.where(row_index == far, 0.25, 0.0)).astype(jnp.bfloat16)

    def spread_all(m):
        for i in range(half // 2):
            refined_lanes = spread_lanes(m, i)
            for k in range(10):
                for t in (2 * i, 2 * i + 1):
                    fine = refined_lanes[8 * k : 8 * k + 8, 128 * (t - 2 * i) : 128 * (t - 2 * i) + 128]
                    near_part, far_part = 0.75 * fine, 0.25 * fine
                    refined.at[k][pl.ds(16 * t, 8, stride=2), :] = near_part + take(far_part, down_index, 0)
                    refined.at[k][pl.ds(16 * t + 1, 8, stride=2), :] = near_part + take(far_part, up_index, 0)

    def refined_row(k):
        return jnp.concatenate(
            [refined[k, pl.ds(16 * t + 8 * h, 8), :] for h in range(2) for t in range(half)], axis=1
        )

    def node(m):
        spread_all(m)
        load(m).wait()

        def rows(k):
            own = 0.75 * refined_row(k + 1)
            vb[m, 2 * k] = vb[m, 2 * k] + (own + 0.25 * refined_row(k))
            vb[m, 2 * k + 1] = vb[m, 2 * k + 1] + (own + 0.25 * refined_row(k + 2))
            store(m, 2 * k).start()
            store(m, 2 * k + 1).start()

        each(8, rows, 4)

    each(3, node)

    pltpu.make_async_copy(vb, vb, out_sem).wait()


def on_device(node_values):
    _, _, depth, rows, lanes = node_values.shape
    half = lanes // 4
    fine = lambda n: pltpu.VMEM((n, 8, lanes), F32)
    coarse = lambda n: pltpu.VMEM((n, 8, half), F32)
    tiles = lambda *n: pltpu.VMEM(n + (8, 128), F32)
    dma = lambda *n: pltpu.SemaphoreType.DMA(n)
    anywhere = pl.BlockSpec(memory_space=pl.ANY)
    vv, dd = pl.pallas_call(
        main_kernel,
        name="sweeps",
        out_shape=(
            jax.ShapeDtypeStruct((3, rows, depth, lanes), F32),
            jax.ShapeDtypeStruct((3, 10, 8, half), F32),
        ),
        in_specs=[anywhere],
        out_specs=(anywhere, anywhere),
        scratch_shapes=[
            pltpu.VMEM((3, 22, 8, lanes), F32), fine(22), fine(20), fine(20), fine(20), fine(20), fine(20), fine(20), fine(18), fine(16), pltpu.VMEM((2, ROWS[1][1], 8, lanes), F32), pltpu.VMEM((2, ROWS[1][1], 8, lanes), F32),
            coarse(10), coarse(10), coarse(10), coarse(10), coarse(12), coarse(10),
            tiles(2, GROUP, 2, 5), tiles(GROUP, 2, 5), tiles(2, 5), tiles(2, GROUP, 3, 2, 5), tiles(3, 2, 5),
            pltpu.VMEM((24, 8, 256), F32), pltpu.VMEM((24, 8, 256), F32), tiles(GROUP, 3, 10), tiles(GROUP, 3, 10), tiles(2, GROUP), tiles(110),
            pltpu.VMEM((3, 10, 8, half), F32), pltpu.VMEM((6, lanes // 16, 128), F32),
            dma(2), dma(1), dma(1), dma(1), dma(1), dma(1), dma(1), dma(2), dma(2), dma(1), dma(1), dma(1), dma(1),
            dma(1), dma(1), dma(5), dma(5), dma(3), dma(2), dma(4), dma(2), dma(1), dma(1), dma(10),
        ],
        compiler_params=pltpu.CompilerParams(
            collective_id=0, has_side_effects=True, vmem_limit_bytes=48 * 1024 * 1024
        ),
    )(node_values)
    return pl.pallas_call(
        correct_kernel,
        name="correct",
        out_shape=jax.ShapeDtypeStruct(node_values.shape, F32),
        in_specs=[anywhere, pl.BlockSpec(memory_space=pltpu.VMEM)],
        out_specs=anywhere,
        scratch_shapes=[
            pltpu.VMEM((3, rows, 8, lanes), F32), pltpu.VMEM((10, lanes // 16, 128), F32),
            dma(3), pltpu.SemaphoreType.DMA,
        ],
        compiler_params=pltpu.CompilerParams(vmem_limit_bytes=48 * 1024 * 1024),
    )(vv, dd)


def solution(mesh):
    return jax.shard_map(
        on_device,
        mesh=mesh,
        in_specs=(P("tm", None, None, "space", None),),
        out_specs=P("tm", None, None, "space", None),
        check_vma=False,
    )
```

```python
import functools

import jax
import jax.numpy as jnp
from jax import lax
from jax.experimental import pallas as pl
from jax.experimental.pallas import tpu as pltpu
from jax.sharding import PartitionSpec as P

STEP = 0.25
WEIGHTS = ((5.0 / 24.0, 1.0 / 3.0, -1.0 / 24.0), (-1.0 / 24.0, 1.0 / 3.0, 5.0 / 24.0))
MESH = pl.DeviceIdType.MESH
GROUP = 4
ROWS = ((2, 2), (4, 4), (8, 4), (12, 4), (0, 2))
BLOCKS = ((2, 3, 4, 5), (0, 1, 6, 7))
PLACE = {r: (b, k) for b, rows in enumerate(BLOCKS) for k, r in enumerate(rows)}
F32 = jnp.float32


def neighbour_sum(above, center, below):
    lanes = center.shape[-1]
    beside = above + below + pltpu.roll(center, 1, 0) + pltpu.roll(center, 7, 0)
    return beside + pltpu.roll(center, 1, 1) + pltpu.roll(center, lanes - 1, 1)


def cube(value):
    return value * value * value


def combine(weights, terms):
    total = weights[0] * terms[0]
    for weight, term in zip(weights[1:], terms[1:]):
        total = total + weight * term
    return total


def each(count, body, unroll=1):
    def step(k, carry):
        body(k)
        return carry

    lax.fori_loop(0, count, step, 0, unroll=unroll)


def iotas():
    sub = lax.broadcasted_iota(jnp.int32, (8, 128), 0)
    lane = lax.broadcasted_iota(jnp.int32, (8, 128), 1)
    return sub, lane


def take(value, index, axis):
    return jnp.take_along_axis(value, index, axis=axis, mode="promise_in_bounds")


def split_tiles(value):
    return [value[:, 128 * t : 128 * (t + 1)] for t in range(value.shape[1] // 128)]


def lane_neighbours(tiles, lane):
    count = len(tiles)
    right_rolled = [pltpu.roll(t, 1, 1) for t in tiles]
    left_rolled = [pltpu.roll(t, 127, 1) for t in tiles]
    before = [pltpu.roll(right_rolled[-1], 4, 0)] + right_rolled[:-1]
    after = left_rolled[1:] + [pltpu.roll(left_rolled[0], 4, 0)]
    left = [jnp.where(lane == 0, before[i], right_rolled[i]) for i in range(count)]
    right = [jnp.where(lane == 127, after[i], left_rolled[i]) for i in range(count)]
    return left, right


def coarse_rate(above, center, below):
    sub, lane = iotas()
    up_index = (sub // 4) * 4 + (sub + 1) % 4
    down_index = (sub // 4) * 4 + (sub + 3) % 4
    a, c, b = split_tiles(above), split_tiles(center), split_tiles(below)
    left, right = lane_neighbours(c, lane)
    out = []
    for i in range(len(c)):
        beside = a[i] + b[i] + take(c[i], up_index, 0) + take(c[i], down_index, 0) + left[i] + right[i]
        out.append(0.25 * beside + c[i] * (0.5 - 2.0 * (c[i] * c[i])))
    return jnp.concatenate(out, axis=1)


def ring_rate(above, center, below):
    sub, _ = iotas()
    up_index = (sub // 4) * 4 + (sub + 1) % 4
    down_index = (sub // 4) * 4 + (sub + 3) % 4
    beside = above + below + pltpu.roll(center, 1, 1) + pltpu.roll(center, 255, 1)
    depth = [take(t, up_index, 0) + take(t, down_index, 0) for t in split_tiles(center)]
    beside = beside + jnp.concatenate(depth, axis=1)
    return 0.25 * beside + center * (0.5 - 2.0 * (center * center))


def strip_of(tiles, t, lane):
    after = tiles[t + 1] if t + 1 < len(tiles) else pltpu.roll(tiles[0], 4, 0)
    before = tiles[t - 1] if t > 0 else pltpu.roll(tiles[-1], 4, 0)
    return jnp.where(lane < 64, after, before)


def join_strips(strips, lane):
    block = ((lane + 16) // 32) % 4
    joined = strips[0]
    for k in range(1, 4):
        joined = jnp.where(block == k, pltpu.roll(strips[k], 32 * k, 1), joined)
    return joined


def put_block(ref, rows, strips, lane):
    for k, place in enumerate((0, 1, 3, 4)):
        ref[place] = rows[k]
    ref[2] = join_strips(strips, lane)


def get_row(ref, k):
    strip = pltpu.roll(ref[2], (128 - 32 * k) % 128, 1)
    return jnp.concatenate([ref[k if k < 2 else k + 1], strip], axis=1)


def packed_halves(row, staging):
    tiles = split_tiles(row)
    half = len(tiles) // 2
    for t in range(half):
        staging[pl.ds(16 * t, 8), :] = tiles[t]
        staging[pl.ds(16 * t + 8, 8), :] = tiles[t + half]
    even = [staging[pl.ds(16 * t, 8, stride=2), :] for t in range(half)]
    odd = [staging[pl.ds(16 * t + 1, 8, stride=2), :] for t in range(half)]
    return even, odd


def decimate_index(lane):
    return jnp.where(lane < 64, 2 * lane, 2 * lane - 127)


def lane_pairs(packed, lane):
    out = []
    for t in range(len(packed) // 2):
        p, q = packed[2 * t], packed[2 * t + 1]
        mixed = jnp.where(lane % 2 == 0, p + pltpu.roll(p, 127, 1), q + pltpu.roll(q, 1, 1))
        out.append(take(mixed, decimate_index(lane), 1))
    return out


def lane_even_odd(packed, lane):
    even, odd = [], []
    for t in range(len(packed) // 2):
        p, q = packed[2 * t], packed[2 * t + 1]
        even.append(take(jnp.where(lane % 2 == 0, p, pltpu.roll(q, 1, 1)), decimate_index(lane), 1))
        odd.append(take(jnp.where(lane % 2 == 0, pltpu.roll(p, 127, 1), q), decimate_index(lane), 1))
    return even, odd


def restrict_row(pair_sum, staging):
    _, lane = iotas()
    even, odd = packed_halves(pair_sum, staging)
    sums = lane_pairs([a + b for a, b in zip(even, odd)], lane)
    return jnp.concatenate([0.125 * v for v in sums], axis=1)


def coarse_terms(fields, staging):
    sub, lane = iotas()
    up_index = (sub // 4) * 4 + (sub + 1) % 4
    down_index = (sub // 4) * 4 + (sub + 3) % 4
    nodes, inner, evens, odds = [], [], [], []
    for n, (before, a, b, after) in enumerate(fields):
        total = a + b
        rest = (before + after) - total - 2.0 * (cube(a) + cube(b))
        even, odd = packed_halves(total, staging.at[2 * n])
        rest_even, rest_odd = packed_halves(rest, staging.at[2 * n + 1])
        count = len(even)
        inner.append(
            [
                rest_even[t] + rest_odd[t] + take(odd[t], down_index, 0) + take(even[t], up_index, 0)
                for t in range(count)
            ]
        )
        lane_even, lane_odd = lane_even_odd([even[t] + odd[t] for t in range(count)], lane)
        evens.append(lane_even)
        odds.append(lane_odd)
        nodes.append(jnp.concatenate([0.125 * (p + q) for p, q in zip(lane_even, lane_odd)], axis=1))
    sums = []
    for weights in WEIGHTS:
        weights = [0.125 * STEP * w for w in weights]
        body = lane_pairs([combine(weights, v) for v in zip(*inner)], lane)
        left, _ = lane_neighbours([combine(weights, v) for v in zip(*odds)], lane)
        _, right = lane_neighbours([combine(weights, v) for v in zip(*evens)], lane)
        sums.append(jnp.concatenate([b + l + r for b, l, r in zip(body, left, right)], axis=1))
    return nodes, sums


def main_kernel(
    u_hbm, vv_hbm, d_hbm,
    ub, bb, p0, kk, q1, v1, mm, p2, v2, vin, around, relay, c0, c1, c2, c2p, a0, a1, pack, cpack, wpack, rx, wx, w0, w1, res, home, edges, meter, rim, dd, staging,
    load_sem, u_send, u_recv, e_send, e_recv, h_send, h_recv, a_send, a_recv, w_send, w_recv, r_send, r_recv, g_send, g_recv, v_send, v_recv, o_send, o_recv, q_send, q_recv,
    p_send, p_recv, out_sem,
):
    tm, sp = lax.axis_index("tm"), lax.axis_index("space")
    n_tm, n_sp = lax.axis_size("tm"), lax.axis_size("space")
    left, right = lax.rem(sp + n_sp - 1, n_sp), lax.rem(sp + 1, n_sp)
    not_first, not_last = tm > 0, tm < n_tm - 1
    half_step = 0.5 * STEP
    team = GROUP * (tm // GROUP)
    spot = tm - team
    first_team = tm < GROUP
    sides = ((left, 2), (sp, 1), (right, 0))

    def load(m, r):
        return u_hbm.at[0, m, :, r, :], ub.at[m, r + 3]

    def remote(src, dst, send, recv, t, s):
        return pltpu.make_async_remote_copy(
            src_ref=src, dst_ref=dst, send_sem=send, recv_sem=recv, device_id=(t, s), device_id_type=MESH
        )

    def all_tiles(count, sem):
        return remote(meter.at[pl.ds(0, count)], meter.at[pl.ds(0, count)], sem, sem, tm, left)

    def edge_row(k):
        return jnp.where(k < 3, k, k + 10)

    def load_edges(k):
        for m in range(3):
            pltpu.make_async_copy(*load(m, edge_row(k)), load_sem.at[0]).start()

    def load_inner(k):
        for m in range(3):
            pltpu.make_async_copy(*load(m, k + 3), load_sem.at[1]).start()

    each(6, load_edges)
    each(10, load_inner)

    barrier = pltpu.get_barrier_semaphore()
    for d in range(GROUP):
        mate = team + lax.rem(spot + d, GROUP)
        for s, _ in sides:
            if d > 0 or s is not sp:
                pl.semaphore_signal(barrier, inc=1, device_id=(mate, s), device_id_type=MESH)

    @pl.when(jnp.logical_not(first_team))
    def _():
        for s, _ in sides:
            pl.semaphore_signal(barrier, inc=1, device_id=(tm - GROUP, s), device_id_type=MESH)

    @pl.when(tm == GROUP)
    def _():
        pl.semaphore_signal(barrier, inc=1, device_id=(tm - 1, sp), device_id_type=MESH)

    @pl.when(tm < GROUP - 1)
    def _():
        pl.semaphore_wait(barrier, 3 * GROUP + 2)

    @pl.when(tm == GROUP - 1)
    def _():
        pl.semaphore_wait(barrier, 3 * GROUP + 3)

    @pl.when(jnp.logical_not(first_team))
    def _():
        pl.semaphore_wait(barrier, 3 * GROUP - 1)

    def wait_rows(count, sem):
        rows = ub.at[:, pl.ds(3, count)]
        pltpu.make_async_copy(rows, rows, sem).wait()

    wait_rows(6, load_sem.at[0])
    u_copies = [
        remote(ub.at[:, pl.ds(18, 1)], ub.at[:, pl.ds(2, 1)], u_send.at[0], u_recv.at[0], tm, right),
        remote(ub.at[:, pl.ds(3, 1)], ub.at[:, pl.ds(19, 1)], u_send.at[0], u_recv.at[0], tm, left),
    ]
    for copy in u_copies:
        copy.start()

    weights = [STEP * w for w in WEIGHTS[0]]
    later_weights = [STEP * w for w in WEIGHTS[1]]
    later_weights[1] = later_weights[1] - half_step

    def local_terms(r):
        nodes = [ub[m, r + 3] for m in range(3)]
        cubes = [cube(v) for v in nodes]
        mixed = combine(weights, nodes)
        bb[r + 3] = mixed
        p0[r + 2] = nodes[0] - 4.0 * mixed + combine([-2.0 * w for w in weights], cubes)
        kk[r + 2] = combine(later_weights, nodes)
        q1[r + 2] = combine([-2.0 * w for w in later_weights], cubes)

    def first_sweep(r):
        value = p0[r + 2] + neighbour_sum(bb[r + 2], bb[r + 3], bb[r + 4])
        mixed = half_step * value + kk[r + 2]
        v1[r + 2] = value
        mm[r + 2] = mixed
        p2[r + 2] = value + q1[r + 2] - 4.0 * mixed - STEP * cube(value)

    def second_sweep(r):
        v2[r + 1] = p2[r + 2] + neighbour_sum(mm[r + 1], mm[r + 2], mm[r + 3])

    def restrict_rim(k):
        c1[9 * k] = rim[k + 2] + restrict_row(v1[17 * k + 1], staging.at[k])

    def coarse_row(i):
        r = 2 * i
        fields = [
            [ub[0, r + k] for k in range(2, 6)],
            [v1[r + k] for k in range(1, 5)],
            [v2[r + k] for k in range(4)],
        ]
        (_, c1[i + 1], c2[i + 1]), (a0[i + 2], a1[i + 1]) = coarse_terms(fields, staging)

    _, lane = iotas()
    is_first = jnp.logical_not(not_first)

    def pack_rows(rows, place):
        tiles = [split_tiles(row) for row in rows]
        for t in range(GROUP):
            put_block(place(t), [v[t] for v in tiles], [strip_of(v, t, lane) for v in tiles], lane)

    def start_copies(piece, go):
        for d in range(GROUP):
            keeper = lax.rem(spot + d, GROUP)
            for s, p in sides:
                if p == piece and (d > 0 or p != 1):
                    copy = remote(
                        cpack.at[keeper], wx.at[p], a_send.at[1], w_recv.at[0], team + keeper, s
                    )
                    go(copy)

    def terms_copy(block, fields, keeper, m, piece, s, entries=(0, 5)):
        where = (pl.ds(0, fields), pl.ds(*entries))
        return remote(
            pack.at[(block, keeper, *where)], rx.at[(block, m, piece, *where)],
            a_send.at[block], a_recv.at[block], team + keeper, s,
        )

    def sized(block, m, go):
        if block == 0:
            pl.when(m < 2)(lambda: go(2, False))
            pl.when(m == 2)(lambda: go(1, True))
        else:
            pl.when(m == 0)(lambda: go(2, False))
            pl.when((m == 1) | (m == 2))(lambda: go(2, True))
            pl.when(m == 3)(lambda: go(1, True))

    def terms_copies(block, go):
        def mate(d):
            keeper = lax.rem(spot + d, GROUP)

            @pl.when(d > 0)
            def _():
                go(terms_copy(block, 2, keeper, spot, 1, sp))

            def beside(fields, half):
                go(terms_copy(block, fields, keeper, spot, 2, left, (0, 3) if half else (0, 5)))
                go(terms_copy(block, fields, keeper, spot, 0, right, (2, 3) if half else (0, 5)))

            sized(block, spot, beside)

        each(GROUP, mate)

    def tiles_beside(block, m):
        if block == 0:
            return jnp.where(m < 2, 10, jnp.where(m == 2, 3, 0))
        return jnp.where(m == 0, 10, jnp.where(m < 3, 6, 3))

    def wait_terms(block):
        all_tiles(10 * (GROUP - 1) + 2 * (23, 25)[block], a_recv.at[block]).wait_recv()

    def send_terms(block):
        for k in BLOCKS[block]:
            a0[k + 2] = a0[k + 2] - half_step * coarse_rate(c0[k], c0[k + 1], c0[k + 2])
            a1[k + 1] = a1[k + 1] - half_step * coarse_rate(c1[k], c1[k + 1], c1[k + 2])
        pack_rows([a0[k + 2] for k in BLOCKS[block]], lambda t: pack.at[block, t, 0])
        pack_rows([a1[k + 1] for k in BLOCKS[block]], lambda t: pack.at[block, t, 1])
        terms_copies(block, lambda copy: copy.start())
        rx[block, spot, 1] = pack[block, spot]

    def restrict_first(i):
        c0[i + 1] = restrict_row(ub[0, 2 * i + 3] + ub[0, 2 * i + 4], staging.at[i % 4])

    each(6, lambda k: local_terms(edge_row(k)), 3)
    for k in (0, 7):
        restrict_first(k)
    for n, r in enumerate((14, 1)):
        first_sweep(r)
        rim[n] = restrict_row(v1[r + 2], staging.at[n])
    rim_copies, rows_of = [
        remote(rim.at[pl.ds(0, 1)], rim.at[pl.ds(2, 1)], e_send.at[0], e_recv.at[0], tm, right),
        remote(rim.at[pl.ds(1, 1)], rim.at[pl.ds(3, 1)], e_send.at[0], e_recv.at[0], tm, left),
    ], (16, 16, 8)
    for n, (field, offset, up, down) in enumerate(((bb, 3, 14, 1), (mm, 2, 14, 1), (c0, 1, 7, 0))):
        up_target, down_target = up + offset - rows_of[n], down + offset + rows_of[n]
        rim_copies += [
            remote(field.at[pl.ds(up + offset, 1)], field.at[pl.ds(up_target, 1)], e_send.at[0], e_recv.at[0], tm, right),
            remote(field.at[pl.ds(down + offset, 1)], field.at[pl.ds(down_target, 1)], e_send.at[0], e_recv.at[0], tm, left),
        ]
    for copy in rim_copies:
        copy.start()
    wait_rows(10, load_sem.at[1])
    for k in range(1, 7):
        restrict_first(k)

    @pl.when(is_first)
    def _():
        for block in range(2):
            pack_rows([c0[k + 1] for k in BLOCKS[block]], lambda t: cpack.at[t, block])
        for piece in range(3):
            start_copies(piece, lambda copy: copy.start())
        wx[1] = cpack[0]

    each(10, lambda k: local_terms(k + 3), 5)
    each(12, lambda k: first_sweep(k + 2), 6)
    each(12, lambda k: second_sweep(k + 2), 6)

    def v_part(index, start, count):
        return remote(
            v2.at[pl.ds(start + 1, count)], vin.at[pl.ds(start, count)], v_send.at[index], v_recv.at[index], tm + 1, sp
        )

    v_parts = [v_part(n, *rows) for n, rows in enumerate(ROWS)]
    behind = team + lax.rem(spot + GROUP - 1, GROUP)
    start, count = ROWS[1]
    hops = [
        remote(v2.at[pl.ds(start + 1, count)], around.at[0], o_send.at[0], o_recv.at[0], behind, sp),
        remote(around.at[0], around.at[1], o_send.at[1], o_recv.at[1], behind, sp),
        remote(around.at[1], vin.at[pl.ds(start, count)], o_send.at[2], v_recv.at[1], behind, sp),
    ]
    goes = [spot != GROUP - 1, spot != GROUP - 2, spot != GROUP - 3]

    def start_hop(n):
        @pl.when(goes[n])
        def _():
            if n > 0:
                hops[n - 1].wait_recv()
            hops[n].start()

    @pl.when(not_last)
    def _():
        v_parts[0].start()

    start_hop(0)

    relay_in, relay_out = [], []
    for k, n in enumerate((1, 3)):
        first, count = ROWS[n]
        held = relay.at[k]
        relay_in.append(remote(v2.at[pl.ds(first + 1, count)], held, q_send.at[k], q_recv.at[k], team, sp))
        relay_out.append(remote(held, vin.at[pl.ds(first, count)], q_send.at[2 + k], v_recv.at[n], tm + GROUP, sp))

    def start_relay(k):
        @pl.when(is_first)
        def _():
            relay_in[k].wait_recv()
            relay_out[k].start()

    @pl.when(tm == GROUP - 1)
    def _():
        relay_in[0].start()

    each(4, lambda k: coarse_row(k + 2), 2)
    for n, i in enumerate((1, 6)):
        c1[i + 1] = restrict_row(v1[2 * i + 2] + v1[2 * i + 3], staging.at[n])
    send_terms(0)

    all_tiles(6 * 16, u_recv.at[0]).wait_recv()
    for r in (-1, 16):
        local_terms(r)
    for r in (0, 15):
        first_sweep(r)
    for r in (1, 14):
        second_sweep(r)
    for i in (1, 6):
        coarse_row(i)
    all_tiles(2 * (2 * 16 + 2 * 4), e_recv.at[0]).wait_recv()
    for r in (-1, 16):
        first_sweep(r)
    for r in (-1, 0, 15, 16):
        second_sweep(r)
    for i in (0, 7):
        coarse_row(i)
    each(2, restrict_rim, 2)


    @pl.when(is_first)
    def _():
        all_tiles(10 * (3 * GROUP - 1), a_send.at[1]).wait_send()

    send_terms(1)

    @pl.when(not_last)
    def _():
        v_parts[2].start()


    c2_up = remote(c2.at[pl.ds(8, 1)], c2.at[pl.ds(0, 1)], h_send.at[0], h_recv.at[0], tm, right)
    c2_down = remote(c2.at[pl.ds(1, 1)], c2.at[pl.ds(9, 1)], h_send.at[0], h_recv.at[0], tm, left)
    c2_up.start()
    c2_down.start()
    v1_out = pltpu.make_async_copy(v1.at[pl.ds(2, 16)], vv_hbm.at[1], out_sem.at[0])
    v2_out = pltpu.make_async_copy(v2.at[pl.ds(1, 16)], vv_hbm.at[2], out_sem.at[1])
    u0_out = pltpu.make_async_copy(ub.at[0, pl.ds(3, 16)], vv_hbm.at[0], out_sem.at[2])
    p_next = [
        remote(c2.at[pl.ds(k, 1)], c2p.at[pl.ds(k, 1)], p_send.at[0], p_recv.at[0], tm + 1, sp) for n, k in enumerate((0, 9))
    ]
    v1_out.start()
    v2_out.start()

    @pl.when(is_first)
    def _():
        u0_out.start()

    start_hop(1)
    start_relay(0)
    wait_terms(0)
    wait_terms(1)

    def late_parts():
        for copy in v_parts[3:]:
            copy.start()

    @pl.when(not_last & (tm != GROUP - 1))
    def _():
        late_parts()

    @pl.when(tm == GROUP - 1)
    def _():
        relay_in[1].start()

    all_tiles(2 * 4, h_recv.at[0]).wait_recv()

    @pl.when(not_last)
    def _():
        for copy in p_next:
            copy.start()

    @pl.when(jnp.logical_not(first_team))
    def _():
        start_hop(2)

    @pl.when(is_first)
    def _():
        all_tiles(20, w_recv.at[0]).wait_recv()

    @pl.when(not_first)
    def _():
        all_tiles(30, w_recv.at[0]).wait_recv()

    for piece in range(3):
        for r in range(8):
            block, k = PLACE[r]
            w0[8 * piece + r] = get_row(wx.at[piece, block], k)

    last_m = GROUP - 1

    def go_home(m, go, here):
        owner = team + m

        @pl.when(m != spot)
        def _():
            go(remote(res.at[m], home.at[spot], r_send.at[0], r_recv.at[0], owner, sp))

        @pl.when(m == spot)
        def _():
            here()

    end_copies = [
        remote(res.at[last_m, 2, 8], edges.at[0, spot], g_send.at[0], g_recv.at[0], team + last_m, right),
        remote(res.at[last_m, 2, 1], edges.at[1, spot], g_send.at[0], g_recv.at[0], team + last_m, left),
    ]

    def sweep(m):
        def term(field, k):
            block, place = PLACE[k % 8]
            return get_row(rx.at[block, m, k // 8, field], place)

        def keep(field, k, value):
            if 7 <= k < 17:
                res[m, field, k - 7] = value[:, :128]

        for k in range(7, 17):
            keep(0, k, w0[k])
        for k in range(1, 23):
            value = w0[k] + half_step * ring_rate(w0[k - 1], w0[k], w0[k + 1]) + term(0, k)
            w1[k] = value
            keep(1, k, value)
        for k in range(2, 22):
            value = w1[k] + half_step * ring_rate(w1[k - 1], w1[k], w1[k + 1]) + term(1, k)
            w0[k] = value
            keep(2, k, value)

        def here():
            home[spot] = res[m]

        go_home(m, lambda copy: copy.start(), here)

    each(GROUP, sweep)
    for copy in end_copies:
        copy.start()

    group_sends = [
        remote(wpack, wx.at[piece], w_send.at[0], w_recv.at[0], tm + GROUP, s) for s, piece in sides
    ]

    @pl.when(first_team)
    def _():
        rows = [split_tiles(w0[k]) for k in range(8, 16)]
        for block in range(2):
            put_block(wpack.at[block], [rows[r][0] for r in BLOCKS[block]], [rows[r][1] for r in BLOCKS[block]], lane)
        for copy in group_sends:
            copy.start()

    @pl.when(tm == GROUP - 1)
    def _():
        all_tiles(30, w_send.at[0]).wait_send()
        v_parts[4].start()

    @pl.when(first_team)
    def _():
        start_hop(2)


    def vin_out(n):
        rows = pl.ds(*ROWS[n])
        return pltpu.make_async_copy(vin.at[rows], vv_hbm.at[0, rows], out_sem.at[5 + n])

    def take_parts(which):
        for n in which:
            v_parts[n].wait_recv()
            vin_out(n).start()
        for n in which:
            first, count = ROWS[n]
            for i in range(first // 2, (first + count) // 2):
                c2p[i + 1] = restrict_row(vin[2 * i] + vin[2 * i + 1], staging.at[i % 6])

    all_tiles(6 * 16, u_send.at[0]).wait_send()
    all_tiles(2 * (2 * 16 + 2 * 4), e_send.at[0]).wait_send()
    all_tiles(2 * 4, h_send.at[0]).wait_send()
    for block in range(2):
        for count in (0, 3, 6, 10):
            pl.when(tiles_beside(block, spot) == count)(
                lambda: all_tiles(10 * (GROUP - 1) + 2 * GROUP * count, a_send.at[block]).wait_send()
            )

    @pl.when(is_first)
    def _():
        u0_out.wait()

    @pl.when(tm < GROUP - 1)
    def _():
        all_tiles(30, w_send.at[0]).wait_send()

    v1_out.wait()
    v2_out.wait()

    start_relay(1)

    @pl.when(not_first)
    def _():
        take_parts((0, 2))
        take_parts((1, 3, 4))

    all_tiles(30 * (GROUP - 1), r_recv.at[0]).wait_recv()

    for t in range(GROUP):
        columns = pl.ds(128 * t, 128)
        dd[1, :, :, columns] = home[t, 1] - c1[:, :, columns]
        dd[2, :, :, columns] = home[t, 2] - c2[:, :, columns]

    @pl.when(spot == last_m)
    def _():
        all_tiles(2 * GROUP, g_recv.at[0]).wait_recv()
        for t in range(GROUP):
            columns = pl.ds(128 * t, 128)
            for side in range(2):
                dd[2, 9 * side, :, columns] = edges[side, t] - c2[9 * side, :, columns]

    d_out = [
        pltpu.make_async_copy(dd.at[pl.ds(1, 2)], d_hbm.at[pl.ds(1, 2)], out_sem.at[3]),
        pltpu.make_async_copy(dd.at[pl.ds(0, 1)], d_hbm.at[pl.ds(0, 1)], out_sem.at[4]),
    ]
    d_out[0].start()

    @pl.when(is_first)
    def _():
        dd[0] = jnp.zeros(dd.shape[1:], F32)

    @pl.when(not_first)
    def _():
        all_tiles(8, p_recv.at[0]).wait_recv()
        for t in range(GROUP):
            columns = pl.ds(128 * t, 128)
            dd[0, :, :, columns] = home[t, 0] - c2p[:, :, columns]

    d_out[1].start()

    all_tiles(30 * (GROUP - 1), r_send.at[0]).wait_send()
    all_tiles(2, g_send.at[0]).wait_send()

    @pl.when(not_last)
    def _():
        all_tiles(8, p_send.at[0]).wait_send()
        for n in (0, 2, 4):
            v_parts[n].wait_send()

    @pl.when(not_last & (tm != GROUP - 1))
    def _():
        v_parts[3].wait_send()

    @pl.when(tm == GROUP - 1)
    def _():
        for copy in relay_in:
            copy.wait_send()

    @pl.when(is_first)
    def _():
        for copy in relay_out:
            copy.wait_send()

    for n in range(3):

        @pl.when(goes[n])
        def _():
            hops[n].wait_send()

    @pl.when(not_first)
    def _():
        for n in range(5):
            vin_out(n).wait()

    for copy in d_out:
        copy.wait()


def correct_kernel(vv_hbm, d_ref, o_hbm, vb, refined, in_sem, out_sem):
    sub, lane = iotas()
    lanes = vb.shape[-1]
    half = lanes // 256
    up_index = (sub // 4) * 4 + (sub + 1) % 4
    down_index = (sub // 4) * 4 + (sub + 3) % 4

    def load(m):
        return pltpu.make_async_copy(vv_hbm.at[m], vb.at[m], in_sem.at[m])

    def store(m, r):
        return pltpu.make_async_copy(vb.at[m, r], o_hbm.at[0, m, :, r, :], out_sem)

    for m in range(3):
        load(m).start()

    def spread_lanes(m, t):
        rows = [split_tiles(d_ref[m, k]) for k in range(10)]
        wide = jnp.concatenate(
            [jnp.concatenate([v[t], strip_of(v, t, lane)], axis=1) for v in rows], axis=0
        )
        total = None
        for _ in range(3):
            part = wide.astype(jnp.bfloat16)
            wide = wide - part.astype(F32)
            product = jnp.dot(part, weights, preferred_element_type=F32)
            total = product if total is None else total + product
        return total

    row_index = lax.broadcasted_iota(jnp.int32, (256, 256), 0)
    fine_index = lax.broadcasted_iota(jnp.int32, (256, 256), 1)
    near = fine_index // 2
    far = lax.rem(near + 255 + 2 * (fine_index % 2), 256)
    weights = jnp.where(row_index == near, 0.75, jnp.where(row_index == far, 0.25, 0.0)).astype(jnp.bfloat16)

    def spread_all(m):
        for i in range(half // 2):
            refined_lanes = spread_lanes(m, i)
            for k in range(10):
                for t in (2 * i, 2 * i + 1):
                    fine = refined_lanes[8 * k : 8 * k + 8, 128 * (t - 2 * i) : 128 * (t - 2 * i) + 128]
                    near_part, far_part = 0.75 * fine, 0.25 * fine
                    refined.at[k][pl.ds(16 * t, 8, stride=2), :] = near_part + take(far_part, down_index, 0)
                    refined.at[k][pl.ds(16 * t + 1, 8, stride=2), :] = near_part + take(far_part, up_index, 0)

    def refined_row(k):
        return jnp.concatenate(
            [refined[k, pl.ds(16 * t + 8 * h, 8), :] for h in range(2) for t in range(half)], axis=1
        )

    def node(m):
        spread_all(m)
        load(m).wait()

        def rows(k):
            own = 0.75 * refined_row(k + 1)
            vb[m, 2 * k] = vb[m, 2 * k] + (own + 0.25 * refined_row(k))
            vb[m, 2 * k + 1] = vb[m, 2 * k + 1] + (own + 0.25 * refined_row(k + 2))
            store(m, 2 * k).start()
            store(m, 2 * k + 1).start()

        each(8, rows, 4)

    each(3, node)

    pltpu.make_async_copy(vb, vb, out_sem).wait()


def on_device(node_values):
    _, _, depth, rows, lanes = node_values.shape
    half = lanes // 4
    fine = lambda n: pltpu.VMEM((n, 8, lanes), F32)
    coarse = lambda n: pltpu.VMEM((n, 8, half), F32)
    tiles = lambda *n: pltpu.VMEM(n + (8, 128), F32)
    dma = lambda *n: pltpu.SemaphoreType.DMA(n)
    anywhere = pl.BlockSpec(memory_space=pl.ANY)
    vv, dd = pl.pallas_call(
        main_kernel,
        name="sweeps",
        out_shape=(
            jax.ShapeDtypeStruct((3, rows, depth, lanes), F32),
            jax.ShapeDtypeStruct((3, 10, 8, half), F32),
        ),
        in_specs=[anywhere],
        out_specs=(anywhere, anywhere),
        scratch_shapes=[
            pltpu.VMEM((3, 22, 8, lanes), F32), fine(22), fine(20), fine(20), fine(20), fine(20), fine(20), fine(20), fine(18), fine(16), pltpu.VMEM((2, ROWS[1][1], 8, lanes), F32), pltpu.VMEM((2, ROWS[1][1], 8, lanes), F32),
            coarse(10), coarse(10), coarse(10), coarse(10), coarse(12), coarse(10),
            tiles(2, GROUP, 2, 5), tiles(GROUP, 2, 5), tiles(2, 5), tiles(2, GROUP, 3, 2, 5), tiles(3, 2, 5),
            pltpu.VMEM((24, 8, 256), F32), pltpu.VMEM((24, 8, 256), F32), tiles(GROUP, 3, 10), tiles(GROUP, 3, 10), tiles(2, GROUP), tiles(110), coarse(4),
            pltpu.VMEM((3, 10, 8, half), F32), pltpu.VMEM((6, lanes // 16, 128), F32),
            dma(2), dma(1), dma(1), dma(1), dma(1), dma(1), dma(1), dma(2), dma(2), dma(1), dma(1), dma(1), dma(1),
            dma(1), dma(1), dma(5), dma(5), dma(3), dma(2), dma(4), dma(2), dma(1), dma(1), dma(10),
        ],
        compiler_params=pltpu.CompilerParams(
            collective_id=0, has_side_effects=True, vmem_limit_bytes=48 * 1024 * 1024
        ),
    )(node_values)
    return pl.pallas_call(
        correct_kernel,
        name="correct",
        out_shape=jax.ShapeDtypeStruct(node_values.shape, F32),
        in_specs=[anywhere, pl.BlockSpec(memory_space=pltpu.VMEM)],
        out_specs=anywhere,
        scratch_shapes=[
            pltpu.VMEM((3, rows, 8, lanes), F32), pltpu.VMEM((10, lanes // 16, 128), F32),
            dma(3), pltpu.SemaphoreType.DMA,
        ],
        compiler_params=pltpu.CompilerParams(vmem_limit_bytes=48 * 1024 * 1024),
    )(vv, dd)


def solution(mesh):
    return jax.shard_map(
        on_device,
        mesh=mesh,
        in_specs=(P("tm", None, None, "space", None),),
        out_specs=P("tm", None, None, "space", None),
        check_vma=False,
    )
```
